128 devices in a mesh: probe: 4 (over y_hi, core), slab: 32 (over x, y_lo, z).
Axes of the slice: x: 4, y: 4 (y_hi: 2, y_lo: 2; y = y_hi * 2 + y_lo), z: 4, core: 2. Of those that a mesh axis runs over, the one named last changes fastest.
Arguments:
- receptor: float32 [8, 256, 64, 128], P(None, 'slab'), may hold values from -14 to 14
- library: float32 [16, 8, 4913], replicated, may hold values from -1 to 1
- probe_ids: int32 [16], P('probe'), may hold values from 0 to 15, each once
- rotations: int32 [16, 1], P('probe'), may hold values from 0 to 23
- offsets: int32 [16, 1, 2], P('probe'), may hold values from 0 to 63
- probe_weight: float32 [16], replicated, may hold values from 0.25 to 4
Outputs:
- consensus: float32 [256, 64, 128], P('slab', 'probe')
The draws below stay inside these ranges and needn't reach their ends.
Inputs may be any that keep to these rules, and one draw needn't show every extreme that they name: `probe_ids`: each probe type once. `rotations`: indices into the table ROT.
All inputs are finite; a program needn't handle non-finite values.
Results may differ from the reference program's by a relative error of at most 0.0001.
Values sent between devices are 32-bit elements; how exact they have to be, the bound alone decides.
A program may use at most 320 MiB of HBM per device.

```python
import math
import jax
import jax.numpy as jnp
import numpy as np
from jax import lax

TERMS = 8
NTYPES = 16
RAD = 8
KS = 17
ROTS = 1
WY = 128
WZ = 64
NX = 256


def draw_receptor(key, part):
    key = jax.random.fold_in(key, 11)
    key_noise, key_across, key_rows, key_phase = jax.random.split(key, 4)
    shape = (TERMS, NX, WZ, WY)
    scale_across = jnp.exp(jax.random.uniform(key_across, (NX,), jnp.float32, math.log(0.55), math.log(1.8)))
    scale_rows = jnp.exp(jax.random.uniform(key_rows, (WY,), jnp.float32, math.log(0.55), math.log(1.8)))
    phase = jax.random.uniform(key_phase, (), jnp.float32, 0.0, 2.0 * math.pi)
    planes = jnp.arange(NX, dtype=jnp.float32)
    noise = jax.random.truncated_normal(key_noise, -4.0, 4.0, shape, jnp.float32)
    swing = jnp.sin(planes * (2.0 * math.pi / NX) + phase)
    return noise * scale_across[None, :, None, None] * scale_rows[None, None, None, :] + swing[None, :, None, None]


def draw_library(key, part):
    key = jax.random.fold_in(key, 23)
    key_noise, key_mean = jax.random.split(key, 2)
    volume = TERMS * KS * KS * KS
    spread = 1.5 / math.sqrt(volume)
    lift = 3.0 / volume * jnp.exp(jax.random.uniform(key_mean, (NTYPES, 1, 1), jnp.float32, math.log(0.5), math.log(2.0)))
    shape = (NTYPES, TERMS, KS * KS * KS)
    noise = jax.random.truncated_normal(key_noise, -4.0, 4.0, shape, jnp.float32)
    return noise * spread + lift


def set_ends(drawn, own_key, low, top_value):
    extent = drawn.shape
    spot = [jax.random.randint(jax.random.fold_in(own_key, axis), (), 0, extent[axis]) for axis in range(len(extent))]
    drawn = drawn.at[tuple(spot)].set(low)
    longest = extent.index(max(extent))
    spot[longest] = (spot[longest] + 1) % extent[longest]
    return drawn.at[tuple(spot)].set(top_value)


def setup_inputs(seed: int = 0) -> dict:
    key_list = jax.random.split(jax.random.key(seed), 7)
    receptor = draw_receptor(jax.random.fold_in(key_list[6], 71), 0)
    library = draw_library(jax.random.fold_in(key_list[6], 71), 0)
    probe_ids = jax.random.permutation(key_list[2], NTYPES).astype(jnp.int32)
    rotations = set_ends(jax.random.randint(key_list[3], (NTYPES, ROTS), 0, 24), jax.random.fold_in(key_list[3], 1), 0, 23).astype(jnp.int32)
    offsets = set_ends(jax.random.randint(key_list[4], (NTYPES, ROTS, 2), 0, WZ), jax.random.fold_in(key_list[4], 1), 0, WZ - 1).astype(jnp.int32)
    probe_weight = jnp.clip(jnp.exp(jax.random.uniform(key_list[5], (NTYPES,), jnp.float32, math.log(0.25), math.log(4.0))), 0.25, 4.0)
    return {"receptor": receptor, "library": library, "probe_ids": probe_ids, "rotations": rotations, "offsets": offsets, "probe_weight": probe_weight}


ENERGY_CAP = 6.0


def cube_rotations():
    permutes = [(0, 1, 2), (0, 2, 1), (1, 0, 2), (1, 2, 0), (2, 0, 1), (2, 1, 0)]
    parities = [1, -1, -1, 1, 1, -1]
    tables = []
    for permute, parity in zip(permutes, parities):
        for sign_x in (1, -1):
            for sign_y in (1, -1):
                for sign_z in (1, -1):
                    if parity * sign_x * sign_y * sign_z == 1:
                        matrix = np.zeros((3, 3), np.int32)
                        sign_list = (sign_x, sign_y, sign_z)
                        for row_index in range(3):
                            matrix[row_index, permute[row_index]] = sign_list[row_index]
                        tables.append(matrix)
    return np.stack(tables)


def offset_grid(radius):
    side_len = 2 * radius + 1
    flat_index = jnp.arange(side_len ** 3, dtype=jnp.int32)
    return (flat_index // (side_len * side_len) - radius, (flat_index // side_len) % side_len - radius, flat_index % side_len - radius)


def rotated_kernel(library, type_id, rot_id, radius):
    side_len = 2 * radius + 1
    turning = jnp.asarray(cube_rotations())[rot_id]
    step_x, step_y, step_z = offset_grid(radius)
    moved_to = [turning[row_index, 0] * step_x + turning[row_index, 1] * step_y + turning[row_index, 2] * step_z + radius for row_index in range(3)]
    source = (moved_to[0] * side_len + moved_to[1]) * side_len + moved_to[2]
    return jnp.take(library[type_id], source, axis=1)


def smooth_periodic(values_in):
    result = values_in
    for axis_index in range(3):
        result = (jnp.roll(result, 1, axis_index) + 2.0 * result + jnp.roll(result, -1, axis_index)) * 0.25
    return result


def reference(receptor, library, probe_ids, rotations, offsets, probe_weight):
    spectrum = jnp.fft.rfftn(receptor, axes=(1, 2, 3))
    step_x, step_y, step_z = offset_grid(RAD)
    cells = NX * WZ * WY

    def per_slot(mixture, inputs):
        type_id, rot_pair, shift_pair = inputs
        total = jnp.zeros((NX, WZ, WY), jnp.float32)
        for turn_index in range(ROTS):
            kernel = rotated_kernel(library, type_id, rot_pair[turn_index], RAD)
            placed = jnp.zeros((TERMS, NX, WZ, WY), jnp.float32).at[:, step_x % NX, step_z % WZ, step_y % WY].add(kernel)
            product = jnp.sum(jnp.conj(jnp.fft.rfftn(placed, axes=(1, 2, 3))) * spectrum, axis=0)
            energy = jnp.fft.irfftn(product, s=(NX, WZ, WY), axes=(0, 1, 2))
            energy = jnp.roll(energy, (shift_pair[turn_index, 1], shift_pair[turn_index, 0]), axis=(1, 2))
            total = total + jnp.exp(-ENERGY_CAP * jnp.tanh(energy / ENERGY_CAP))
        partition = jnp.sum(total)
        weight = probe_weight[type_id]
        return mixture + weight * (cells * total / partition), None

    mixture, unused = lax.scan(per_slot, jnp.zeros((NX, WZ, WY), jnp.float32), (probe_ids, rotations, offsets))
    return smooth_periodic(mixture) / NTYPES
```

```python
import functools
import math

import jax
import jax.numpy as jnp
import ml_dtypes
import numpy as np
from jax import lax
from jax.experimental import pallas as pl
from jax.experimental.pallas import tpu as pltpu
from jax.sharding import PartitionSpec as P

RAD = 8
KS = 17
AZ = 24
EXT = 24
KX = 13
PAIRS = 7
NZ = 64
NY = 128
ENERGY_CAP = 6.0
HIGHEST = lax.Precision.HIGHEST
MESH = pl.DeviceIdType.MESH
BF = jnp.bfloat16
F32 = jnp.float32


def cube_rotations():
    permutes = [(0, 1, 2), (0, 2, 1), (1, 0, 2), (1, 2, 0), (2, 0, 1), (2, 1, 0)]
    parities = [1, -1, -1, 1, 1, -1]
    perms, signs = [], []
    for permute, parity in zip(permutes, parities):
        for sign_x in (1, -1):
            for sign_y in (1, -1):
                for sign_z in (1, -1):
                    if parity * sign_x * sign_y * sign_z == 1:
                        perms.append(permute)
                        signs.append((sign_x, sign_y, sign_z))
    return np.array(perms, np.int32), np.array(signs, np.int32)


def split_np(table):
    table = table.astype(np.float32)
    hi = table.astype(ml_dtypes.bfloat16)
    lo = (table - hi.astype(np.float32)).astype(ml_dtypes.bfloat16)
    return hi, lo


def xy_table():
    a = np.arange(KS) - RAD
    kx = np.arange(2 * PAIRS)
    ky = np.arange(NY)
    px = (a[:, None] * kx[None, :]) % EXT / EXT
    py = (a[:, None] * ky[None, :]) % NY / NY
    ang = 2 * np.pi * (px[:, None, :, None] + py[None, :, None, :])
    live = (kx < KX).astype(np.float64)[None, None, :, None]
    both = np.stack([np.cos(ang) * live, np.sin(ang) * live], axis=2)
    both = both.reshape(KS, KS, 2, PAIRS, 2, NY).transpose(0, 1, 3, 2, 4, 5)
    return both.reshape(KS * KS, PAIRS * 2 * 2 * NY)


def probe_z_table():
    a = np.arange(AZ) - RAD
    live = (np.arange(AZ) < KS).astype(np.float64)
    kz = np.arange(NZ)
    ang = 2 * np.pi * ((kz[:, None] * a[None, :]) % NZ) / NZ
    c, s = np.cos(ang) * live, np.sin(ang) * live
    t = np.block([[c, -s], [s, c]])
    hi, lo = split_np(t)
    return np.concatenate([hi, lo, hi], axis=1)


def grid_z_table():
    k = np.arange(NZ)
    ang = 2 * np.pi * ((k[:, None] * k[None, :]) % NZ) / NZ
    t = np.concatenate([np.cos(ang), np.sin(ang)], axis=0)
    hi, lo = split_np(t)
    return np.concatenate([hi, lo, hi], axis=1)


def grid_y_table(direction):
    k = np.arange(NY)
    ang = 2 * np.pi * ((k[:, None] * k[None, :]) % NY) / NY
    c, s = np.cos(ang), direction * np.sin(ang)
    return split_np(np.block([[c, s], [-s, c]]))


def split(x):
    hi = x.astype(BF)
    lo = (x - hi.astype(F32)).astype(BF)
    return hi, lo


def probe_kernel(tz_ref, y_ref, q_ref):
    tz = tz_ref[...]
    for p in range(PAIRS):
        d = jnp.concatenate(
            [y_ref[0, :, p * 512 : p * 512 + 256], y_ref[0, :, p * 512 + 256 : p * 512 + 512]], axis=0
        )
        hi, lo = split(d)
        rhs = jnp.concatenate([hi, hi, lo], axis=0)
        q_ref[0, p] = jnp.dot(tz, rhs, preferred_element_type=F32)


def cos24(m):
    return math.cos(2 * math.pi * (m % 24) / 24)


def sin24(m):
    return math.sin(2 * math.pi * (m % 24) / 24)


def lin(terms):
    total = None
    for coef, value in terms:
        if abs(coef) < 1e-12:
            continue
        if abs(coef - 1) < 1e-12:
            total = value if total is None else total + value
        elif abs(coef + 1) < 1e-12:
            total = -value if total is None else total - value
        else:
            total = coef * value if total is None else total + coef * value
    return total


def real_dft24(r):
    a = [r[0]] + [r[n] + r[24 - n] for n in range(1, 12)] + [r[12]]
    b = [None] + [r[n] - r[24 - n] for n in range(1, 12)]
    re, im = [None] * 13, [None] * 13
    c = [a[n] + a[12 - n] for n in range(6)] + [a[6]]
    d = [a[n] - a[12 - n] for n in range(6)]
    ce = [c[n] + c[6 - n] for n in range(3)] + [c[3]]
    co = [c[n] - c[6 - n] for n in range(3)]
    for m in range(7):
        if m % 2 == 0:
            re[2 * m] = lin([(cos24(2 * m * n), ce[n]) for n in range(4)])
        else:
            re[2 * m] = lin([(cos24(2 * m * n), co[n]) for n in range(3)])
    for k in range(1, 12, 2):
        re[k] = lin([(cos24(k * n), d[n]) for n in range(6)])
    e = [None] + [b[n] + b[12 - n] for n in range(1, 6)] + [b[6]]
    f = [None] + [b[n] - b[12 - n] for n in range(1, 6)]
    for k in range(1, 12, 2):
        im[k] = lin([(-sin24(k * n), e[n]) for n in range(1, 7)])
    fo = [None] + [f[n] + f[6 - n] for n in range(1, 3)] + [f[3]]
    fe = [None] + [f[n] - f[6 - n] for n in range(1, 3)]
    for m in range(1, 6):
        if m % 2 == 1:
            im[2 * m] = lin([(-sin24(2 * m * n), fo[n]) for n in range(1, 4)])
        else:
            im[2 * m] = lin([(-sin24(2 * m * n), fe[n]) for n in range(1, 3)])
    return re, im


def y_stage(x, w_hi, w_lo):
    hi, lo = split(x)
    out = jnp.dot(hi, w_hi, preferred_element_type=F32)
    out = out + jnp.dot(lo, w_hi, preferred_element_type=F32)
    return out + jnp.dot(hi, w_lo, preferred_element_type=F32)


def z_stage(tz, x, direction):
    hi, lo = split(x)
    rhs = jnp.concatenate([hi, hi, lo], axis=0)
    p = jnp.dot(tz, rhs, preferred_element_type=F32)
    re = p[:NZ, :NY] - direction * p[NZ:, NY:]
    im = p[:NZ, NY:] + direction * p[NZ:, :NY]
    return re, im


def energy_kernel(
    scalars,
    own_ref,
    before_a,
    before_b,
    after_a,
    after_b,
    q_ref,
    tz_ref,
    wf_hi,
    wf_lo,
    wi_hi,
    wi_lo,
    total_ref,
    sum_ref,
    spec,
    work,
):
    step = pl.program_id(0)
    tz = tz_ref[...]

    def forward(before_ref, after_ref):
        @pl.loop(0, 8)
        def _(chunk):
            rows = pl.ds(pl.multiple_of(chunk * 8, 8), 8)
            r = (
                [before_ref[0, n, rows] for n in range(8)]
                + [own_ref[0, n, rows] for n in range(8)]
                + [after_ref[0, n, rows] for n in range(8)]
            )
            re, im = real_dft24(r)
            for k in range(KX):
                work[k, rows, :NY] = re[k]
                work[k, rows, NY:] = im[k] if im[k] is not None else jnp.zeros_like(re[k])

        @pl.loop(0, KX)
        def _(k):
            y = y_stage(work[k], wf_hi[...], wf_lo[...])
            re, im = z_stage(tz, y, -1.0)
            spec[step, k, :, :NY] = re
            spec[step, k, :, NY:] = im

    @pl.when(step < 4)
    def _():
        forward(before_a, after_a)

    @pl.when((step >= 4) & (step < 8))
    def _():
        forward(before_b, after_b)

    @pl.when(step >= 8)
    def _():
        slot = step - 8

        @pl.loop(0, 8)
        def _(chunk):
            start = pl.multiple_of(chunk * 8, 8)
            rows = pl.ds(start, 8)
            low = pl.ds(start + NZ, 8)
            for k in range(KX):
                p, lane = k // 2, (k % 2) * NY
                re = im = None
                for t in range(8):
                    gr, gi = spec[t, k, rows, :NY], spec[t, k, rows, NY:]
                    qr = q_ref[0, t, p, rows, lane : lane + NY]
                    qi = q_ref[0, t, p, low, lane : lane + NY]
                    tr = gr * qr - gi * qi
                    ti = gr * qi + gi * qr
                    re = tr if re is None else re + tr
                    im = ti if im is None else im + ti
                work[k, rows, :NY] = re
                work[k, rows, NY:] = im

        @pl.loop(0, KX)
        def _(k):
            re, im = z_stage(tz, work[k], 1.0)
            work[k] = y_stage(jnp.concatenate([re, im], axis=1), wi_hi[...], wi_lo[...])

        scale = 1.0 / (EXT * NZ * NY)

        @pl.loop(0, 8)
        def _(chunk):
            rows = pl.ds(pl.multiple_of(chunk * 8, 8), 8)
            fr = [work[k, rows, :NY] for k in range(KX)]
            fi = [work[k, rows, NY:] for k in range(KX)]
            for m in range(5):
                even, odd = [], []
                for k in range(KX):
                    w = scale * (1.0 if k in (0, 12) else 2.0) * (-1) ** k
                    even.append((w * cos24(k * m), fr[k]))
                    odd.append((w * sin24(k * m), fi[k]))
                even = sum_terms(even)
                odd = sum_terms(odd)
                if m == 0:
                    total_ref[0, 4, rows] = even
                else:
                    if m < 4:
                        total_ref[0, 4 + m, rows] = even - odd
                    total_ref[0, 4 - m, rows] = even + odd

        shift_y = scalars[1 + 2 * slot]
        shift_z = scalars[2 + 2 * slot]
        acc = jnp.zeros((8, NY), F32)
        for x in range(8):
            e = total_ref[0, x]
            e = pltpu.roll(e, shift_y, 1)
            e = pltpu.roll(e, shift_z, 0)
            b = jnp.exp(-ENERGY_CAP * jnp.tanh(e / ENERGY_CAP))
            total_ref[0, x] = b
            for c in range(8):
                acc = acc + b[c * 8 : c * 8 + 8]
        sum_ref[0] = acc


def sum_terms(terms):
    total = None
    for coef, value in terms:
        if abs(coef) < 1e-15:
            continue
        total = coef * value if total is None else total + coef * value
    return total


def tail_kernel(
    slabs,
    probes,
    cells,
    types,
    total_ref,
    sum_ref,
    weight_ref,
    out_ref,
    mine,
    gathered,
    halo,
    mixed,
    blocks,
    part_send,
    part_recv,
    halo_send,
    halo_recv,
    block_send,
    block_recv,
):
    slots = total_ref.shape[0]
    planes = total_ref.shape[1]
    rows = out_ref.shape[1]
    slab = lax.axis_index("slab")
    probe = lax.axis_index("probe")

    barrier = pltpu.get_barrier_semaphore()

    @pl.loop(1, slabs)
    def _(d):
        pl.semaphore_signal(
            barrier, inc=1, device_id={"slab": lax.rem(slab + d, slabs)}, device_id_type=MESH
        )

    for d in range(1, probes):
        pl.semaphore_signal(
            barrier, inc=1, device_id={"probe": lax.rem(probe + d, probes)}, device_id_type=MESH
        )

    parts = []
    for s in range(slots):
        v = jnp.sum(sum_ref[s], axis=0, keepdims=True)
        v = jnp.sum(v, axis=1, keepdims=True)
        parts.append(jnp.broadcast_to(v, (1, NY)))
    parts += [jnp.zeros((1, NY), F32)] * (8 - slots)
    own = jnp.concatenate(parts, axis=0)
    mine[...] = own

    pl.semaphore_wait(barrier, slabs - 1 + probes - 1)

    def part_copy(d):
        return pltpu.make_async_remote_copy(
            src_ref=mine,
            dst_ref=gathered.at[d],
            send_sem=part_send.at[d],
            recv_sem=part_recv.at[d],
            device_id={"slab": lax.rem(slab + d, slabs)},
            device_id_type=MESH,
        )

    @pl.loop(1, slabs)
    def _(d):
        part_copy(d).start()

    to_right = pltpu.make_async_remote_copy(
        src_ref=total_ref.at[:, planes - 1],
        dst_ref=halo.at[0],
        send_sem=halo_send.at[0],
        recv_sem=halo_recv.at[0],
        device_id={"slab": lax.rem(slab + 1, slabs)},
        device_id_type=MESH,
    )
    to_left = pltpu.make_async_remote_copy(
        src_ref=total_ref.at[:, 0],
        dst_ref=halo.at[1],
        send_sem=halo_send.at[1],
        recv_sem=halo_recv.at[1],
        device_id={"slab": lax.rem(slab + slabs - 1, slabs)},
        device_id_type=MESH,
    )
    to_right.start()
    to_left.start()

    @pl.loop(1, slabs)
    def _(d):
        part_copy(d).wait_recv()

    partition = own
    for d in range(1, slabs):
        partition = partition + gathered[d]
    coef = weight_ref[...] * (cells / partition)
    coefs = [jnp.broadcast_to(coef[s : s + 1], (8, NY)) for s in range(slots)]

    def weighted(read):
        total = None
        for s in range(slots):
            v = read(s).reshape(NZ // 8, 8, NY) * coefs[s][None]
            total = v if total is None else total + v
        return total.reshape(NZ, NY)

    to_right.wait_recv()
    to_left.wait_recv()
    mixed[0] = weighted(lambda s: halo[0, s])
    mixed[planes + 1] = weighted(lambda s: halo[1, s])
    for x in range(planes):
        mixed[x + 1] = weighted(lambda s: total_ref[s, x])
    for x in range(planes):
        v = (mixed[x] + 2.0 * mixed[x + 1] + mixed[x + 2]) * 0.25
        v = (pltpu.roll(v, 1, 0) + 2.0 * v + pltpu.roll(v, NZ - 1, 0)) * 0.25
        v = (pltpu.roll(v, 1, 1) + 2.0 * v + pltpu.roll(v, NY - 1, 1)) * 0.25
        mixed[x] = v

    def block_copy(d):
        target = lax.rem(probe + d, probes)
        return pltpu.make_async_remote_copy(
            src_ref=mixed.at[pl.ds(0, planes), pl.ds(pl.multiple_of(target * rows, 8), rows)],
            dst_ref=blocks.at[d - 1],
            send_sem=block_send.at[d - 1],
            recv_sem=block_recv.at[d - 1],
            device_id={"probe": target},
            device_id_type=MESH,
        )

    for d in range(1, probes):
        block_copy(d).start()
    result = mixed[pl.ds(0, planes), pl.ds(pl.multiple_of(probe * rows, 8), rows)]
    for d in range(1, probes):
        block_copy(d).wait_recv()
        result = result + blocks[d - 1]
    out_ref[...] = result * (1.0 / types)

    @pl.loop(1, slabs)
    def _(d):
        part_copy(d).wait_send()

    to_right.wait_send()
    to_left.wait_send()
    for d in range(1, probes):
        block_copy(d).wait_send()


def rotated_cubes(library, probe_ids, rotations, core):
    slots = probe_ids.shape[0]
    perms_np, signs_np = cube_rotations()
    chosen = library[probe_ids]
    terms = chosen.shape[1]
    half = terms // 2
    chosen = jnp.where(core == 0, chosen, jnp.concatenate([chosen[:, half:], chosen[:, :half]], axis=1))
    cube = chosen.reshape(slots, terms, KS, KS, KS)
    perm = jnp.asarray(perms_np)[rotations]
    sign = jnp.asarray(signs_np)[rotations]
    zaxis = jnp.argmax(perm == 2, axis=1)
    first = jnp.where(zaxis == 0, 1, 0)
    second = jnp.where(zaxis == 2, 1, 2)
    pick = lambda table, index: jnp.take_along_axis(table, index[:, None], axis=1)[:, 0]
    layouts = [
        cube.reshape(slots, terms, KS, KS * KS),
        cube.transpose(0, 1, 3, 2, 4).reshape(slots, terms, KS, KS * KS),
        cube.transpose(0, 1, 4, 2, 3).reshape(slots, terms, KS, KS * KS),
    ]
    z4 = zaxis[:, None, None, None]
    rows = jnp.where(z4 == 0, layouts[0], jnp.where(z4 == 1, layouts[1], layouts[2]))
    sz = pick(sign, zaxis)[:, None, None, None]
    rows = jnp.where(sz > 0, rows, jnp.flip(rows, axis=2))
    flat = jnp.arange(KS * KS, dtype=jnp.int32)
    ax, ay = flat // KS - RAD, flat % KS - RAD

    def along(index):
        p, s = pick(perm, index)[:, None], pick(sign, index)[:, None]
        return s * jnp.where(p == 0, ax[None], ay[None]) + RAD

    source = along(first) * KS + along(second)
    onehot = (source[:, None, :] == flat[None, :, None]).astype(F32)
    turned = jnp.einsum(
        "srl,slm->srm", rows.reshape(slots, terms * KS, KS * KS), onehot, precision=HIGHEST
    ).reshape(slots, terms, KS, KS * KS)
    return jnp.pad(turned, ((0, 0), (0, 0), (0, AZ - KS), (0, 0)))


def local(receptor, library, probe_ids, rotations, offsets, probe_weight):
    terms, planes, nz, ny = receptor.shape
    slabs = lax.axis_size("slab")
    probes = lax.axis_size("probe")
    slots = probe_ids.shape[0]
    types = probe_weight.shape[0]
    core = lax.axis_index("probe") % 2
    half = terms // 2
    cells = float(planes * slabs * nz * ny)

    up = [(i, (i + 1) % slabs) for i in range(slabs)]
    down = [(j, i) for i, j in up]
    swap = [(i, i ^ 1) for i in range(probes)]
    share = lax.dynamic_slice_in_dim(receptor, core * half, half, axis=0)
    before_a = lax.ppermute(share, "slab", up)
    after_a = lax.ppermute(share, "slab", down)
    before_b = lax.ppermute(before_a, "probe", swap)
    after_b = lax.ppermute(after_a, "probe", swap)

    cubes = rotated_cubes(library, probe_ids, rotations[:, 0], core)
    table = jnp.asarray(xy_table().astype(np.float32))
    yk = jnp.dot(cubes.reshape(slots * terms * AZ, KS * KS), table, precision=lax.Precision.HIGH)
    yk = yk.reshape(slots * terms, AZ, PAIRS * 512)

    q = pl.pallas_call(
        probe_kernel,
        grid=(slots * terms,),
        in_specs=[
            pl.BlockSpec((128, 6 * AZ), lambda i: (0, 0)),
            pl.BlockSpec((1, AZ, PAIRS * 512), lambda i: (i, 0, 0)),
        ],
        out_specs=pl.BlockSpec((1, PAIRS, 128, 256), lambda i: (i, 0, 0, 0)),
        out_shape=jax.ShapeDtypeStruct((slots * terms, PAIRS, 128, 256), F32),
        compiler_params=pltpu.CompilerParams(vmem_limit_bytes=24 << 20),
        cost_estimate=pl.CostEstimate(
            flops=2 * slots * terms * PAIRS * 128 * 144 * 256, bytes_accessed=40 << 20, transcendentals=0
        ),
        name="probe_spectra",
    )(jnp.asarray(probe_z_table()), yk)
    q = q.reshape(slots, terms, PAIRS, 128, 256)

    scalars = jnp.concatenate([core[None].astype(jnp.int32), offsets.reshape(-1)])
    wf_hi, wf_lo = grid_y_table(-1.0)
    wi_hi, wi_lo = grid_y_table(1.0)
    plane_block = (1, planes, nz, ny)
    fixed = lambda shape: pl.BlockSpec(shape, lambda i, s: (0,) * len(shape))
    total, sums = pl.pallas_call(
        energy_kernel,
        grid_spec=pltpu.PrefetchScalarGridSpec(
            num_scalar_prefetch=1,
            grid=(terms + slots,),
            in_specs=[
                pl.BlockSpec(
                    plane_block, lambda i, s: ((jnp.minimum(i, terms - 1) + half * s[0]) % terms, 0, 0, 0)
                ),
                pl.BlockSpec(plane_block, lambda i, s: (jnp.minimum(i, half - 1), 0, 0, 0)),
                pl.BlockSpec(plane_block, lambda i, s: (jnp.clip(i - half, 0, half - 1), 0, 0, 0)),
                pl.BlockSpec(plane_block, lambda i, s: (jnp.minimum(i, half - 1), 0, 0, 0)),
                pl.BlockSpec(plane_block, lambda i, s: (jnp.clip(i - half, 0, half - 1), 0, 0, 0)),
                pl.BlockSpec(
                    (1, terms, PAIRS, 128, 256), lambda i, s: (jnp.maximum(i - terms, 0), 0, 0, 0, 0)
                ),
                fixed((128, 192)),
                fixed((256, 256)),
                fixed((256, 256)),
                fixed((256, 256)),
                fixed((256, 256)),
            ],
            out_specs=[
                pl.BlockSpec(plane_block, lambda i, s: (jnp.maximum(i - terms, 0), 0, 0, 0)),
                pl.BlockSpec((1, 8, ny), lambda i, s: (jnp.maximum(i - terms, 0), 0, 0)),
            ],
            scratch_shapes=[
                pltpu.VMEM((terms, KX, nz, 2 * ny), F32),
                pltpu.VMEM((KX, nz, 2 * ny), F32),
            ],
        ),
        out_shape=[
            jax.ShapeDtypeStruct((slots, planes, nz, ny), F32),
            jax.ShapeDtypeStruct((slots, 8, ny), F32),
        ],
        compiler_params=pltpu.CompilerParams(vmem_limit_bytes=48 << 20),
        cost_estimate=pl.CostEstimate(flops=12 << 30, bytes_accessed=40 << 20, transcendentals=1 << 20),
        name="energy_maps",
    )(
        scalars,
        receptor,
        before_a,
        before_b,
        after_a,
        after_b,
        q,
        jnp.asarray(grid_z_table()),
        jnp.asarray(wf_hi),
        jnp.asarray(wf_lo),
        jnp.asarray(wi_hi),
        jnp.asarray(wi_lo),
    )

    onehot = (probe_ids[:, None] == jnp.arange(types, dtype=jnp.int32)[None, :]).astype(F32)
    chosen = jnp.sum(onehot * probe_weight[None], axis=1)
    weight = jnp.broadcast_to(jnp.pad(chosen, (0, 8 - slots))[:, None], (8, ny))
    rows = nz // probes
    vmem = pl.BlockSpec(memory_space=pltpu.VMEM)
    return pl.pallas_call(
        functools.partial(tail_kernel, slabs, probes, cells, types),
        in_specs=[vmem] * 3,
        out_specs=vmem,
        out_shape=jax.ShapeDtypeStruct((planes, rows, ny), F32),
        scratch_shapes=[
            pltpu.VMEM((8, ny), F32),
            pltpu.VMEM((slabs, 8, ny), F32),
            pltpu.VMEM((2, slots, nz, ny), F32),
            pltpu.VMEM((planes + 2, nz, ny), F32),
            pltpu.VMEM((probes - 1, planes, rows, ny), F32),
            pltpu.SemaphoreType.DMA((slabs,)),
            pltpu.SemaphoreType.DMA((slabs,)),
            pltpu.SemaphoreType.DMA((2,)),
            pltpu.SemaphoreType.DMA((2,)),
            pltpu.SemaphoreType.DMA((probes - 1,)),
            pltpu.SemaphoreType.DMA((probes - 1,)),
        ],
        compiler_params=pltpu.CompilerParams(
            collective_id=0, has_side_effects=True, vmem_limit_bytes=24 << 20
        ),
        name="consensus_tail",
    )(total, sums, weight)


def solution(mesh):
    in_specs = (
        P(None, "slab", None, None),
        P(),
        P("probe"),
        P("probe", None),
        P("probe", None, None),
        P(),
    )
    out_specs = P("slab", "probe", None)
    return jax.shard_map(local, mesh=mesh, in_specs=in_specs, out_specs=out_specs, check_vma=False)
```

```python
import functools
import math

import jax
import jax.numpy as jnp
import ml_dtypes
import numpy as np
from jax import lax
from jax.experimental import pallas as pl
from jax.experimental.pallas import tpu as pltpu
from jax.sharding import PartitionSpec as P

RAD = 8
KS = 17
AZ = 24
EXT = 24
KX = 13
PAIRS = 7
NZ = 64
NY = 128
ENERGY_CAP = 6.0
HIGHEST = lax.Precision.HIGHEST
MESH = pl.DeviceIdType.MESH
BF = jnp.bfloat16
F32 = jnp.float32


def cube_rotations():
    permutes = [(0, 1, 2), (0, 2, 1), (1, 0, 2), (1, 2, 0), (2, 0, 1), (2, 1, 0)]
    parities = [1, -1, -1, 1, 1, -1]
    perms, signs = [], []
    for permute, parity in zip(permutes, parities):
        for sign_x in (1, -1):
            for sign_y in (1, -1):
                for sign_z in (1, -1):
                    if parity * sign_x * sign_y * sign_z == 1:
                        perms.append(permute)
                        signs.append((sign_x, sign_y, sign_z))
    return np.array(perms, np.int32), np.array(signs, np.int32)


def split_np(table):
    table = table.astype(np.float32)
    hi = table.astype(ml_dtypes.bfloat16)
    lo = (table - hi.astype(np.float32)).astype(ml_dtypes.bfloat16)
    return hi, lo


HALF = (KS * KS + 1) // 2
CUBE = 384
PACK = 512


def half_offsets():
    flat = np.arange(HALF) + HALF - 1
    return flat // KS - RAD, flat % KS - RAD


def xy_tables():
    ax, ay = half_offsets()
    kx = np.arange(2 * PAIRS)
    ky = np.arange(NY)
    px = (ax[:, None] * kx[None, :]) % EXT / EXT
    py = (ay[:, None] * ky[None, :]) % NY / NY
    ang = 2 * np.pi * (px[:, :, None] + py[:, None, :])
    live = (kx < KX).astype(np.float64)[None, :, None]
    out = []
    for t in (np.cos(ang) * live, np.sin(ang) * live):
        hi, lo = split_np(t.reshape(HALF, -1))
        pad = np.zeros((PACK - 3 * HALF, hi.shape[1]), hi.dtype)
        out.append(np.concatenate([hi, hi, lo, pad], axis=0))
    return out


def lane_offsets():
    ax, ay = half_offsets()
    rows = np.full((8, PACK), 10000, np.int32)
    for c in range(3):
        rows[0, c * HALF : (c + 1) * HALF] = ax
        rows[1, c * HALF : (c + 1) * HALF] = ay
    rows[2] = 0
    rows[2, [0, HALF, 2 * HALF]] = 10000
    return rows


def swap_table():
    t = np.zeros((CUBE, CUBE), np.float32)
    for m in range(KS):
        for n in range(KS):
            t[n * KS + m, m * KS + n] = 1
    return t.astype(ml_dtypes.bfloat16)


def rotation_table():
    perms, signs = cube_rotations()
    table = np.zeros((24, 4), np.int32)
    for q in range(24):
        zaxis = [i for i in range(3) if perms[q, i] == 2][0]
        others = [i for i in range(3) if i != zaxis]
        table[q, 0] = zaxis
        table[q, 1] = 1 if signs[q, zaxis] < 0 else 0
        for i, unit in zip(others, (KS, 1)):
            table[q, 2 + perms[q, i]] = unit * signs[q, i]
    return table


def probe_z_table():
    a = np.arange(AZ) - RAD
    live = (np.arange(AZ) < KS).astype(np.float64)
    kz = np.arange(NZ)
    ang = 2 * np.pi * ((kz[:, None] * a[None, :]) % NZ) / NZ
    c, s = np.cos(ang) * live, np.sin(ang) * live
    t = np.block([[c, -s], [s, c]])
    hi, lo = split_np(t)
    return np.concatenate([hi, lo, hi], axis=1)


def grid_z_table():
    k = np.arange(NZ)
    ang = 2 * np.pi * ((k[:, None] * k[None, :]) % NZ) / NZ
    t = np.concatenate([np.cos(ang), np.sin(ang)], axis=0)
    hi, lo = split_np(t)
    return np.concatenate([hi, lo, hi], axis=1)


def grid_y_table(direction):
    k = np.arange(NY)
    ang = 2 * np.pi * ((k[:, None] * k[None, :]) % NY) / NY
    c, s = np.cos(ang), direction * np.sin(ang)
    hi, lo = split_np(np.block([[c, s], [-s, c]]))
    return np.concatenate([hi, hi, lo], axis=0)


def split(x):
    hi = x.astype(BF)
    lo = (x - hi.astype(F32)).astype(BF)
    return hi, lo


def probe_kernel(
    ids, rots, core, turns, lib_ref, swap_ref, lane_ref, te_ref, to_ref, tz_ref, q_ref, xa, xb, kd, even, odd
):
    slots = ids.shape[0]
    terms = lib_ref.shape[1]

    @pl.when(pl.program_id(0) == 0)
    def _():
        xa[...] = jnp.zeros_like(xa)
        kd[...] = jnp.zeros_like(kd)
        lane = lax.broadcasted_iota(jnp.int32, (terms, CUBE), 1)
        packed_lane = lax.broadcasted_iota(jnp.int32, (terms * AZ, 128), 1)
        source = lax.broadcasted_iota(jnp.int32, (CUBE, PACK), 0)

        @pl.loop(0, slots)
        def _(slot):
            rot = rots[slot]
            zaxis, flipped = turns[rot, 0], turns[rot, 1]
            step_x, step_y = turns[rot, 2], turns[rot, 3]
            for m in range(KS):
                w = lib_ref[ids[slot], :, m * KS * KS : (m + 1) * KS * KS]
                xa[m, :, : KS * KS] = pltpu.roll(w, core[0] * (terms // 2), 0)

            def permuted(x, table):
                hi, lo = split(x)
                out = jnp.dot(jnp.concatenate([hi, lo], axis=0), table, preferred_element_type=F32)
                return out[: x.shape[0]] + out[x.shape[0] :]

            @pl.when(zaxis == 2)
            def _():
                turned = permuted(xa[...].reshape(KS * terms, CUBE), swap_ref[...])
                xa[...] = turned.reshape(KS, terms, CUBE)

            @pl.when(zaxis == 0)
            def _():
                xb[...] = xa[...]

            @pl.when(zaxis > 0)
            def _():
                for m in range(KS):
                    acc = jnp.zeros((terms, CUBE), F32)
                    for n in range(KS):
                        moved = pltpu.roll(xa[n], ((n - m) * KS) % CUBE, 1)
                        acc = jnp.where((lane >= n * KS) & (lane < (n + 1) * KS), moved, acc)
                    xb[m] = acc

            here = lane_ref[0:1] * step_x + lane_ref[1:2] * step_y + (HALF - 1)
            there = 2 * (HALF - 1) - here + lane_ref[2:3]
            plus = (source == here).astype(F32)
            minus = (source == there).astype(F32)
            x = xb[...].reshape(KS * terms, CUBE)
            for table, ref in ((plus + minus, even), (plus - minus, odd)):
                turned = permuted(x, table.astype(BF))
                for m in range(KS):
                    az = jnp.where(flipped == 1, KS - 1 - m, m)
                    for j in range(PACK // 128):
                        kd[j, pl.ds(az, terms, stride=AZ), :] = turned[
                            m * terms : (m + 1) * terms, j * 128 : (j + 1) * 128
                        ]
                rows = pl.ds(pl.multiple_of(slot * terms * AZ, terms * AZ), terms * AZ)
                for j in range(PACK // 128):
                    hi, lo = split(kd[j])
                    packed = packed_lane + j * 128
                    low = (packed >= HALF) & (packed < 2 * HALF)
                    ref[rows, j * 128 : (j + 1) * 128] = jnp.where(
                        low, lo.astype(F32), hi.astype(F32)
                    ).astype(BF)

    tz = tz_ref[...]
    re = jnp.dot(even[...], te_ref[...], preferred_element_type=F32)
    im = jnp.dot(odd[...], to_ref[...], preferred_element_type=F32)
    for i in range(slots * terms):
        d = jnp.concatenate([re[i * AZ : (i + 1) * AZ], im[i * AZ : (i + 1) * AZ]], axis=0)
        hi, lo = split(d)
        q_ref[i, 0] = jnp.dot(tz, jnp.concatenate([hi, hi, lo], axis=0), preferred_element_type=F32)


def probe_call(library, probe_ids, rotations, core):
    slots, terms = probe_ids.shape[0], library.shape[1]
    te, to = xy_tables()
    fixed = lambda shape: pl.BlockSpec(shape, lambda i, *s: (0,) * len(shape))
    table = pl.BlockSpec((PACK, 256), lambda i, *s: (0, i))
    q = pl.pallas_call(
        probe_kernel,
        grid_spec=pltpu.PrefetchScalarGridSpec(
            num_scalar_prefetch=4,
            grid=(PAIRS,),
            in_specs=[
                fixed(library.shape),
                fixed((CUBE, CUBE)),
                fixed((8, PACK)),
                table,
                table,
                fixed((128, 6 * AZ)),
            ],
            out_specs=pl.BlockSpec((slots * terms, 1, 128, 256), lambda i, *s: (0, i, 0, 0)),
            scratch_shapes=[
                pltpu.VMEM((KS, terms, CUBE), F32),
                pltpu.VMEM((KS, terms, CUBE), F32),
                pltpu.VMEM((PACK // 128, terms * AZ, 128), F32),
                pltpu.VMEM((slots * terms * AZ, PACK), BF),
                pltpu.VMEM((slots * terms * AZ, PACK), BF),
            ],
        ),
        out_shape=jax.ShapeDtypeStruct((slots * terms, PAIRS, 128, 256), F32),
        compiler_params=pltpu.CompilerParams(vmem_limit_bytes=40 << 20),
        cost_estimate=pl.CostEstimate(flops=8 << 30, bytes_accessed=40 << 20, transcendentals=0),
        name="probe_spectra",
    )(
        probe_ids,
        rotations,
        core,
        jnp.asarray(rotation_table()),
        library,
        jnp.asarray(swap_table()),
        jnp.asarray(lane_offsets()),
        jnp.asarray(te),
        jnp.asarray(to),
        jnp.asarray(probe_z_table()),
    )
    return q.reshape(slots, terms, PAIRS, 128, 256)


def cos24(m):
    return math.cos(2 * math.pi * (m % 24) / 24)


def sin24(m):
    return math.sin(2 * math.pi * (m % 24) / 24)


def lin(terms):
    total = None
    for coef, value in terms:
        if abs(coef) < 1e-12:
            continue
        if abs(coef - 1) < 1e-12:
            total = value if total is None else total + value
        elif abs(coef + 1) < 1e-12:
            total = -value if total is None else total - value
        else:
            total = coef * value if total is None else total + coef * value
    return total


def real_dft24(r):
    a = [r[0]] + [r[n] + r[24 - n] for n in range(1, 12)] + [r[12]]
    b = [None] + [r[n] - r[24 - n] for n in range(1, 12)]
    re, im = [None] * 13, [None] * 13
    c = [a[n] + a[12 - n] for n in range(6)] + [a[6]]
    d = [a[n] - a[12 - n] for n in range(6)]
    ce = [c[n] + c[6 - n] for n in range(3)] + [c[3]]
    co = [c[n] - c[6 - n] for n in range(3)]
    for m in range(7):
        if m % 2 == 0:
            re[2 * m] = lin([(cos24(2 * m * n), ce[n]) for n in range(4)])
        else:
            re[2 * m] = lin([(cos24(2 * m * n), co[n]) for n in range(3)])
    for k in range(1, 12, 2):
        re[k] = lin([(cos24(k * n), d[n]) for n in range(6)])
    e = [None] + [b[n] + b[12 - n] for n in range(1, 6)] + [b[6]]
    f = [None] + [b[n] - b[12 - n] for n in range(1, 6)]
    for k in range(1, 12, 2):
        im[k] = lin([(-sin24(k * n), e[n]) for n in range(1, 7)])
    fo = [None] + [f[n] + f[6 - n] for n in range(1, 3)] + [f[3]]
    fe = [None] + [f[n] - f[6 - n] for n in range(1, 3)]
    for m in range(1, 6):
        if m % 2 == 1:
            im[2 * m] = lin([(-sin24(2 * m * n), fo[n]) for n in range(1, 4)])
        else:
            im[2 * m] = lin([(-sin24(2 * m * n), fe[n]) for n in range(1, 3)])
    return re, im


def y_stage(x, w):
    hi, lo = split(x)
    return jnp.dot(jnp.concatenate([hi, lo, hi], axis=1), w, preferred_element_type=F32)


def z_stage(tz, x, direction):
    hi, lo = split(x)
    rhs = jnp.concatenate([hi, hi, lo], axis=0)
    p = jnp.dot(tz, rhs, preferred_element_type=F32)
    re = p[:NZ, :NY] - direction * p[NZ:, NY:]
    im = p[:NZ, NY:] + direction * p[NZ:, :NY]
    return re, im


def energy_kernel(
    scalars,
    own_ref,
    before_a,
    before_b,
    after_a,
    after_b,
    q_ref,
    tz_ref,
    wf_ref,
    wi_ref,
    total_ref,
    sum_ref,
    spec,
    work,
):
    step = pl.program_id(0)
    tz = tz_ref[...]

    def forward(before_ref, after_ref):
        @pl.loop(0, 8)
        def _(chunk):
            rows = pl.ds(pl.multiple_of(chunk * 8, 8), 8)
            r = (
                [before_ref[0, n, rows] for n in range(8)]
                + [own_ref[0, n, rows] for n in range(8)]
                + [after_ref[0, n, rows] for n in range(8)]
            )
            re, im = real_dft24(r)
            for k in range(KX):
                work[k, rows, :NY] = re[k]
                work[k, rows, NY:] = im[k] if im[k] is not None else jnp.zeros_like(re[k])

        y = y_stage(work[...].reshape(KX * NZ, 2 * NY), wf_ref[...])
        work[...] = y.reshape(KX, NZ, 2 * NY)
        for k in range(KX):
            re, im = z_stage(tz, work[k], -1.0)
            spec[step, k, :, :NY] = re
            spec[step, k, :, NY:] = im

    @pl.when(step < 4)
    def _():
        forward(before_a, after_a)

    @pl.when((step >= 4) & (step < 8))
    def _():
        forward(before_b, after_b)

    @pl.when(step >= 8)
    def _():
        slot = step - 8

        @pl.loop(0, 8)
        def _(chunk):
            start = pl.multiple_of(chunk * 8, 8)
            rows = pl.ds(start, 8)
            low = pl.ds(start + NZ, 8)
            for k in range(KX):
                p, lane = k // 2, (k % 2) * NY
                re = im = None
                for t in range(8):
                    gr, gi = spec[t, k, rows, :NY], spec[t, k, rows, NY:]
                    qr = q_ref[0, t, p, rows, lane : lane + NY]
                    qi = q_ref[0, t, p, low, lane : lane + NY]
                    tr = gr * qr - gi * qi
                    ti = gr * qi + gi * qr
                    re = tr if re is None else re + tr
                    im = ti if im is None else im + ti
                work[k, rows, :NY] = re
                work[k, rows, NY:] = im

        for k in range(KX):
            re, im = z_stage(tz, work[k], 1.0)
            work[k, :, :NY] = re
            work[k, :, NY:] = im
        y = y_stage(work[...].reshape(KX * NZ, 2 * NY), wi_ref[...])
        work[...] = y.reshape(KX, NZ, 2 * NY)

        scale = 1.0 / (EXT * NZ * NY)

        @pl.loop(0, 8)
        def _(chunk):
            rows = pl.ds(pl.multiple_of(chunk * 8, 8), 8)
            fr = [work[k, rows, :NY] for k in range(KX)]
            fi = [work[k, rows, NY:] for k in range(KX)]
            for m in range(5):
                even, odd = [], []
                for k in range(KX):
                    w = scale * (1.0 if k in (0, 12) else 2.0) * (-1) ** k
                    even.append((w * cos24(k * m), fr[k]))
                    odd.append((w * sin24(k * m), fi[k]))
                even = sum_terms(even)
                odd = sum_terms(odd)
                if m == 0:
                    total_ref[0, 4, rows] = even
                else:
                    if m < 4:
                        total_ref[0, 4 + m, rows] = even - odd
                    total_ref[0, 4 - m, rows] = even + odd

        shift_y = scalars[1 + 2 * slot]
        shift_z = scalars[2 + 2 * slot]
        acc = jnp.zeros((8, NY), F32)
        for x in range(8):
            e = total_ref[0, x]
            e = pltpu.roll(e, shift_y, 1)
            e = pltpu.roll(e, shift_z, 0)
            b = jnp.exp(-ENERGY_CAP * jnp.tanh(e / ENERGY_CAP))
            total_ref[0, x] = b
            for c in range(8):
                acc = acc + b[c * 8 : c * 8 + 8]
        sum_ref[0] = acc


def sum_terms(terms):
    total = None
    for coef, value in terms:
        if abs(coef) < 1e-15:
            continue
        total = coef * value if total is None else total + coef * value
    return total


def tail_kernel(
    slabs,
    probes,
    cells,
    types,
    total_ref,
    sum_ref,
    weight_ref,
    out_ref,
    mine,
    gathered,
    halo,
    mixed,
    blocks,
    part_send,
    part_recv,
    halo_send,
    halo_recv,
    block_send,
    block_recv,
):
    slots = total_ref.shape[0]
    planes = total_ref.shape[1]
    rows = out_ref.shape[1]
    slab = lax.axis_index("slab")
    probe = lax.axis_index("probe")

    barrier = pltpu.get_barrier_semaphore()

    @pl.loop(1, slabs)
    def _(d):
        pl.semaphore_signal(
            barrier, inc=1, device_id={"slab": lax.rem(slab + d, slabs)}, device_id_type=MESH
        )

    for d in range(1, probes):
        pl.semaphore_signal(
            barrier, inc=1, device_id={"probe": lax.rem(probe + d, probes)}, device_id_type=MESH
        )

    parts = []
    for s in range(slots):
        v = jnp.sum(sum_ref[s], axis=0, keepdims=True)
        v = jnp.sum(v, axis=1, keepdims=True)
        parts.append(jnp.broadcast_to(v, (1, NY)))
    parts += [jnp.zeros((1, NY), F32)] * (8 - slots)
    own = jnp.concatenate(parts, axis=0)
    mine[...] = own

    pl.semaphore_wait(barrier, slabs - 1 + probes - 1)

    def part_copy(d):
        return pltpu.make_async_remote_copy(
            src_ref=mine,
            dst_ref=gathered.at[d],
            send_sem=part_send.at[d],
            recv_sem=part_recv.at[d],
            device_id={"slab": lax.rem(slab + d, slabs)},
            device_id_type=MESH,
        )

    @pl.loop(1, slabs)
    def _(d):
        part_copy(d).start()

    to_right = pltpu.make_async_remote_copy(
        src_ref=total_ref.at[:, planes - 1],
        dst_ref=halo.at[0],
        send_sem=halo_send.at[0],
        recv_sem=halo_recv.at[0],
        device_id={"slab": lax.rem(slab + 1, slabs)},
        device_id_type=MESH,
    )
    to_left = pltpu.make_async_remote_copy(
        src_ref=total_ref.at[:, 0],
        dst_ref=halo.at[1],
        send_sem=halo_send.at[1],
        recv_sem=halo_recv.at[1],
        device_id={"slab": lax.rem(slab + slabs - 1, slabs)},
        device_id_type=MESH,
    )
    to_right.start()
    to_left.start()

    @pl.loop(1, slabs)
    def _(d):
        part_copy(d).wait_recv()

    partition = own
    for d in range(1, slabs):
        partition = partition + gathered[d]
    coef = weight_ref[...] * (cells / partition)
    coefs = [jnp.broadcast_to(coef[s : s + 1], (8, NY)) for s in range(slots)]

    def weighted(read):
        total = None
        for s in range(slots):
            v = read(s).reshape(NZ // 8, 8, NY) * coefs[s][None]
            total = v if total is None else total + v
        return total.reshape(NZ, NY)

    to_right.wait_recv()
    to_left.wait_recv()
    mixed[0] = weighted(lambda s: halo[0, s])
    mixed[planes + 1] = weighted(lambda s: halo[1, s])
    for x in range(planes):
        mixed[x + 1] = weighted(lambda s: total_ref[s, x])
    for x in range(planes):
        v = (mixed[x] + 2.0 * mixed[x + 1] + mixed[x + 2]) * 0.25
        v = (pltpu.roll(v, 1, 0) + 2.0 * v + pltpu.roll(v, NZ - 1, 0)) * 0.25
        v = (pltpu.roll(v, 1, 1) + 2.0 * v + pltpu.roll(v, NY - 1, 1)) * 0.25
        mixed[x] = v

    def block_copy(d):
        target = lax.rem(probe + d, probes)
        return pltpu.make_async_remote_copy(
            src_ref=mixed.at[pl.ds(0, planes), pl.ds(pl.multiple_of(target * rows, 8), rows)],
            dst_ref=blocks.at[d - 1],
            send_sem=block_send.at[d - 1],
            recv_sem=block_recv.at[d - 1],
            device_id={"probe": target},
            device_id_type=MESH,
        )

    for d in range(1, probes):
        block_copy(d).start()
    result = mixed[pl.ds(0, planes), pl.ds(pl.multiple_of(probe * rows, 8), rows)]
    for d in range(1, probes):
        block_copy(d).wait_recv()
        result = result + blocks[d - 1]
    out_ref[...] = result * (1.0 / types)

    @pl.loop(1, slabs)
    def _(d):
        part_copy(d).wait_send()

    to_right.wait_send()
    to_left.wait_send()
    for d in range(1, probes):
        block_copy(d).wait_send()


def energy_call(scalars, receptor, before_a, before_b, after_a, after_b, q):
    terms, planes, nz, ny = receptor.shape
    slots, half = q.shape[0], terms // 2
    plane_block = (1, planes, nz, ny)
    fixed = lambda shape: pl.BlockSpec(shape, lambda i, s: (0,) * len(shape))
    return pl.pallas_call(
        energy_kernel,
        grid_spec=pltpu.PrefetchScalarGridSpec(
            num_scalar_prefetch=1,
            grid=(terms + slots,),
            in_specs=[
                pl.BlockSpec(
                    plane_block, lambda i, s: ((jnp.minimum(i, terms - 1) + half * s[0]) % terms, 0, 0, 0)
                ),
                pl.BlockSpec(plane_block, lambda i, s: (jnp.minimum(i, half - 1), 0, 0, 0)),
                pl.BlockSpec(plane_block, lambda i, s: (jnp.clip(i - half, 0, half - 1), 0, 0, 0)),
                pl.BlockSpec(plane_block, lambda i, s: (jnp.minimum(i, half - 1), 0, 0, 0)),
                pl.BlockSpec(plane_block, lambda i, s: (jnp.clip(i - half, 0, half - 1), 0, 0, 0)),
                pl.BlockSpec(
                    (1, terms, PAIRS, 128, 256), lambda i, s: (jnp.maximum(i - terms, 0), 0, 0, 0, 0)
                ),
                fixed((128, 192)),
                fixed((768, 256)),
                fixed((768, 256)),
            ],
            out_specs=[
                pl.BlockSpec(plane_block, lambda i, s: (jnp.maximum(i - terms, 0), 0, 0, 0)),
                pl.BlockSpec((1, 8, ny), lambda i, s: (jnp.maximum(i - terms, 0), 0, 0)),
            ],
            scratch_shapes=[
                pltpu.VMEM((terms, KX, nz, 2 * ny), F32),
                pltpu.VMEM((KX, nz, 2 * ny), F32),
            ],
        ),
        out_shape=[
            jax.ShapeDtypeStruct((slots, planes, nz, ny), F32),
            jax.ShapeDtypeStruct((slots, 8, ny), F32),
        ],
        compiler_params=pltpu.CompilerParams(vmem_limit_bytes=48 << 20),
        cost_estimate=pl.CostEstimate(flops=12 << 30, bytes_accessed=40 << 20, transcendentals=1 << 20),
        name="energy_maps",
    )(
        scalars,
        receptor,
        before_a,
        before_b,
        after_a,
        after_b,
        q,
        jnp.asarray(grid_z_table()),
        jnp.asarray(grid_y_table(-1.0)),
        jnp.asarray(grid_y_table(1.0)),
    )


def local(receptor, library, probe_ids, rotations, offsets, probe_weight):
    terms, planes, nz, ny = receptor.shape
    slabs = lax.axis_size("slab")
    probes = lax.axis_size("probe")
    slots = probe_ids.shape[0]
    types = probe_weight.shape[0]
    core = lax.axis_index("probe") % 2
    half = terms // 2
    cells = float(planes * slabs * nz * ny)

    up = [(i, (i + 1) % slabs) for i in range(slabs)]
    down = [(j, i) for i, j in up]
    swap = [(i, i ^ 1) for i in range(probes)]
    share = lax.dynamic_slice_in_dim(receptor, core * half, half, axis=0)
    before_a = lax.ppermute(share, "slab", up)
    after_a = lax.ppermute(share, "slab", down)
    before_b = lax.ppermute(before_a, "probe", swap)
    after_b = lax.ppermute(after_a, "probe", swap)

    q = probe_call(library, probe_ids, rotations[:, 0], core[None].astype(jnp.int32))

    scalars = jnp.concatenate([core[None].astype(jnp.int32), offsets.reshape(-1)])
    total, sums = energy_call(scalars, receptor, before_a, before_b, after_a, after_b, q)

    onehot = (probe_ids[:, None] == jnp.arange(types, dtype=jnp.int32)[None, :]).astype(F32)
    chosen = jnp.sum(onehot * probe_weight[None], axis=1)
    weight = jnp.broadcast_to(jnp.pad(chosen, (0, 8 - slots))[:, None], (8, ny))
    rows = nz // probes
    vmem = pl.BlockSpec(memory_space=pltpu.VMEM)
    return pl.pallas_call(
        functools.partial(tail_kernel, slabs, probes, cells, types),
        in_specs=[vmem] * 3,
        out_specs=vmem,
        out_shape=jax.ShapeDtypeStruct((planes, rows, ny), F32),
        scratch_shapes=[
            pltpu.VMEM((8, ny), F32),
            pltpu.VMEM((slabs, 8, ny), F32),
            pltpu.VMEM((2, slots, nz, ny), F32),
            pltpu.VMEM((planes + 2, nz, ny), F32),
            pltpu.VMEM((probes - 1, planes, rows, ny), F32),
            pltpu.SemaphoreType.DMA((slabs,)),
            pltpu.SemaphoreType.DMA((slabs,)),
            pltpu.SemaphoreType.DMA((2,)),
            pltpu.SemaphoreType.DMA((2,)),
            pltpu.SemaphoreType.DMA((probes - 1,)),
            pltpu.SemaphoreType.DMA((probes - 1,)),
        ],
        compiler_params=pltpu.CompilerParams(
            collective_id=0, has_side_effects=True, vmem_limit_bytes=24 << 20
        ),
        name="consensus_tail",
    )(total, sums, weight)


def solution(mesh):
    in_specs = (
        P(None, "slab", None, None),
        P(),
        P("probe"),
        P("probe", None),
        P("probe", None, None),
        P(),
    )
    out_specs = P("slab", "probe", None)
    return jax.shard_map(local, mesh=mesh, in_specs=in_specs, out_specs=out_specs, check_vma=False)
```

```python
import functools
import math

import jax
import jax.numpy as jnp
import ml_dtypes
import numpy as np
from jax import lax
from jax.experimental import pallas as pl
from jax.experimental.pallas import tpu as pltpu
from jax.sharding import PartitionSpec as P

RAD = 8
KS = 17
AZ = 24
EXT = 24
KX = 13
PAIRS = 7
NZ = 64
NY = 128
ENERGY_CAP = 6.0
HIGHEST = lax.Precision.HIGHEST
MESH = pl.DeviceIdType.MESH
BF = jnp.bfloat16
F32 = jnp.float32


def cube_rotations():
    permutes = [(0, 1, 2), (0, 2, 1), (1, 0, 2), (1, 2, 0), (2, 0, 1), (2, 1, 0)]
    parities = [1, -1, -1, 1, 1, -1]
    perms, signs = [], []
    for permute, parity in zip(permutes, parities):
        for sign_x in (1, -1):
            for sign_y in (1, -1):
                for sign_z in (1, -1):
                    if parity * sign_x * sign_y * sign_z == 1:
                        perms.append(permute)
                        signs.append((sign_x, sign_y, sign_z))
    return np.array(perms, np.int32), np.array(signs, np.int32)


def split_np(table):
    table = table.astype(np.float32)
    hi = table.astype(ml_dtypes.bfloat16)
    lo = (table - hi.astype(np.float32)).astype(ml_dtypes.bfloat16)
    return hi, lo


HALF = (KS * KS + 1) // 2
CUBE = 384
PACK = 512


def half_offsets():
    flat = np.arange(HALF) + HALF - 1
    return flat // KS - RAD, flat % KS - RAD


def xy_tables():
    ax, ay = half_offsets()
    kx = np.arange(2 * PAIRS)
    ky = np.arange(NY)
    px = (ax[:, None] * kx[None, :]) % EXT / EXT
    py = (ay[:, None] * ky[None, :]) % NY / NY
    ang = 2 * np.pi * (px[:, :, None] + py[:, None, :])
    live = (kx < KX).astype(np.float64)[None, :, None]
    out = []
    for t in (np.cos(ang) * live, np.sin(ang) * live):
        hi, lo = split_np(t.reshape(HALF, -1))
        pad = np.zeros((PACK - 3 * HALF, hi.shape[1]), hi.dtype)
        out.append(np.concatenate([hi, hi, lo, pad], axis=0))
    return out


def lane_offsets():
    ax, ay = half_offsets()
    rows = np.full((8, PACK), 10000, np.int32)
    for c in range(3):
        rows[0, c * HALF : (c + 1) * HALF] = ax
        rows[1, c * HALF : (c + 1) * HALF] = ay
    rows[2] = 0
    rows[2, [0, HALF, 2 * HALF]] = 10000
    return rows


def swap_table():
    t = np.zeros((CUBE, CUBE), np.float32)
    for m in range(KS):
        for n in range(KS):
            t[n * KS + m, m * KS + n] = 1
    return t.astype(ml_dtypes.bfloat16)


def rotation_table():
    perms, signs = cube_rotations()
    table = np.zeros((24, 4), np.int32)
    for q in range(24):
        zaxis = [i for i in range(3) if perms[q, i] == 2][0]
        others = [i for i in range(3) if i != zaxis]
        table[q, 0] = zaxis
        table[q, 1] = 1 if signs[q, zaxis] < 0 else 0
        for i, unit in zip(others, (KS, 1)):
            table[q, 2 + perms[q, i]] = unit * signs[q, i]
    return table


def probe_z_steps():
    kz = np.arange(2 * NZ) % NZ
    lane = np.arange(6 * AZ) % (2 * AZ)
    az = lane % AZ
    quarter = np.where((np.arange(2 * NZ) < NZ)[:, None], np.where(lane < AZ, 0, 16), np.where(lane < AZ, -16, 0))
    turn = (kz[:, None] * (az - RAD)[None, :] + quarter) % NZ
    live = np.broadcast_to((az < KS).astype(np.int64)[None], turn.shape)
    return np.stack([turn, np.broadcast_to(kz[:, None], turn.shape), live]).astype(np.int32)


def grid_z_table():
    k = np.arange(NZ)
    ang = 2 * np.pi * ((k[:, None] * k[None, :]) % NZ) / NZ
    t = np.concatenate([np.cos(ang), np.sin(ang)], axis=0)
    hi, lo = split_np(t)
    return np.concatenate([hi, lo, hi], axis=1)


def grid_y_table(direction):
    k = np.arange(NY)
    ang = 2 * np.pi * ((k[:, None] * k[None, :]) % NY) / NY
    c, s = np.cos(ang), direction * np.sin(ang)
    hi, lo = split_np(np.block([[c, s], [-s, c]]))
    return np.concatenate([hi, hi, lo], axis=0)


def split(x):
    hi = x.astype(BF)
    lo = (x - hi.astype(F32)).astype(BF)
    return hi, lo


def turned_probes(ids, rots, offs, turns, core, lib_ref, swap_ref, lane_ref, zstep_ref, xa, xb, kd, even, odd, tzs, ph):
    slots, terms = tzs.shape[0], lib_ref.shape[1]
    xa[...] = jnp.zeros_like(xa)
    kd[...] = jnp.zeros_like(kd)
    lane = lax.broadcasted_iota(jnp.int32, (terms, CUBE), 1)
    packed_lane = lax.broadcasted_iota(jnp.int32, (terms * AZ, 128), 1)
    source = lax.broadcasted_iota(jnp.int32, (CUBE, PACK), 0)
    zlane = lax.broadcasted_iota(jnp.int32, (2 * NZ, 6 * AZ), 1)
    ky = lax.broadcasted_iota(jnp.int32, (8, 2 * NY), 1) % NY

    def permuted(x, table):
        hi, lo = split(x)
        out = jnp.dot(jnp.concatenate([hi, lo], axis=0), table, preferred_element_type=F32)
        return out[: x.shape[0]] + out[x.shape[0] :]

    @pl.loop(0, slots)
    def _(slot):
        rot = rots[slot]
        zaxis, flipped = turns[rot, 0], turns[rot, 1]
        step_x, step_y = turns[rot, 2], turns[rot, 3]
        off_y, off_z = offs[2 * slot], offs[2 * slot + 1]

        turn = (zstep_ref[0] - zstep_ref[1] * off_z + NZ * NZ) & (NZ - 1)
        t = jnp.cos(turn.astype(F32) * (2 * math.pi / NZ)) * zstep_ref[2].astype(F32)
        hi, lo = split(t)
        tzs[slot] = jnp.where((zlane >= 2 * AZ) & (zlane < 4 * AZ), lo.astype(F32), hi.astype(F32)).astype(BF)
        turn = ky * off_y
        ph[slot, 0] = jnp.cos((turn & (NY - 1)).astype(F32) * (2 * math.pi / NY))
        ph[slot, 1] = jnp.cos(((turn - NY // 4) & (NY - 1)).astype(F32) * (2 * math.pi / NY))

        for m in range(KS):
            w = lib_ref[ids[slot], :, m * KS * KS : (m + 1) * KS * KS]
            xa[m, :, : KS * KS] = jnp.where(core == 0, w, pltpu.roll(w, terms // 2, 0))
        x = xa[...]
        swapped = permuted(x.reshape(KS * terms, CUBE), swap_ref[...]).reshape(KS, terms, CUBE)
        xa[...] = jnp.where(zaxis == 2, swapped, x)
        for m in range(KS):
            acc = jnp.zeros((terms, CUBE), F32)
            for n in range(KS):
                moved = pltpu.roll(xa[n], ((n - m) * KS) % CUBE, 1)
                acc = jnp.where((lane >= n * KS) & (lane < (n + 1) * KS), moved, acc)
            xb[m] = jnp.where(zaxis == 0, xa[m], acc)

        here = lane_ref[0:1] * step_x + lane_ref[1:2] * step_y + (HALF - 1)
        there = 2 * (HALF - 1) - here + lane_ref[2:3]
        plus = (source == here).astype(F32)
        minus = (source == there).astype(F32)
        x = xb[...].reshape(KS * terms, CUBE)
        for table, ref in ((plus + minus, even), (plus - minus, odd)):
            turned = permuted(x, table.astype(BF))
            for m in range(KS):
                f = KS - 1 - m
                row = jnp.where(flipped == 1, turned[f * terms : (f + 1) * terms], turned[m * terms : (m + 1) * terms])
                for j in range(PACK // 128):
                    kd[j, pl.ds(m, terms, stride=AZ), :] = row[:, j * 128 : (j + 1) * 128]
            rows = pl.ds(pl.multiple_of(slot * terms * AZ, terms * AZ), terms * AZ)
            for j in range(PACK // 128):
                hi, lo = split(kd[j])
                packed = packed_lane + j * 128
                low = (packed >= HALF) & (packed < 2 * HALF)
                ref[rows, j * 128 : (j + 1) * 128] = jnp.where(low, lo.astype(F32), hi.astype(F32)).astype(BF)


def probe_pair(p, te, to, even, odd, tzs, ph, q):
    slots, terms = q.shape[0], q.shape[1]
    columns = pl.ds(pl.multiple_of(p * 2 * NY, 2 * NY), 2 * NY)
    re_all = jnp.dot(even[...], te[:, columns], preferred_element_type=F32)
    im_all = jnp.dot(odd[...], to[:, columns], preferred_element_type=F32)
    for s in range(slots):
        c, n = ph[s, 0, 0:1], ph[s, 1, 0:1]
        rows = slice(s * terms * AZ, (s + 1) * terms * AZ)
        re = re_all[rows] * c + im_all[rows] * n
        im = im_all[rows] * c - re_all[rows] * n
        tz = tzs[s]
        for t in range(terms):
            d = jnp.concatenate([re[t * AZ : (t + 1) * AZ], im[t * AZ : (t + 1) * AZ]], axis=0)
            hi, lo = split(d)
            q[s, t, p] = jnp.dot(tz, jnp.concatenate([hi, hi, lo], axis=0), preferred_element_type=F32)


def cos24(m):
    return math.cos(2 * math.pi * (m % 24) / 24)


def sin24(m):
    return math.sin(2 * math.pi * (m % 24) / 24)


def lin(terms):
    total = None
    for coef, value in terms:
        if abs(coef) < 1e-12:
            continue
        if abs(coef - 1) < 1e-12:
            total = value if total is None else total + value
        elif abs(coef + 1) < 1e-12:
            total = -value if total is None else total - value
        else:
            total = coef * value if total is None else total + coef * value
    return total


def real_dft24(r):
    a = [r[0]] + [r[n] + r[24 - n] for n in range(1, 12)] + [r[12]]
    b = [None] + [r[n] - r[24 - n] for n in range(1, 12)]
    re, im = [None] * 13, [None] * 13
    c = [a[n] + a[12 - n] for n in range(6)] + [a[6]]
    d = [a[n] - a[12 - n] for n in range(6)]
    ce = [c[n] + c[6 - n] for n in range(3)] + [c[3]]
    co = [c[n] - c[6 - n] for n in range(3)]
    for m in range(7):
        if m % 2 == 0:
            re[2 * m] = lin([(cos24(2 * m * n), ce[n]) for n in range(4)])
        else:
            re[2 * m] = lin([(cos24(2 * m * n), co[n]) for n in range(3)])
    for k in range(1, 12, 2):
        re[k] = lin([(cos24(k * n), d[n]) for n in range(6)])
    e = [None] + [b[n] + b[12 - n] for n in range(1, 6)] + [b[6]]
    f = [None] + [b[n] - b[12 - n] for n in range(1, 6)]
    for k in range(1, 12, 2):
        im[k] = lin([(-sin24(k * n), e[n]) for n in range(1, 7)])
    fo = [None] + [f[n] + f[6 - n] for n in range(1, 3)] + [f[3]]
    fe = [None] + [f[n] - f[6 - n] for n in range(1, 3)]
    for m in range(1, 6):
        if m % 2 == 1:
            im[2 * m] = lin([(-sin24(2 * m * n), fo[n]) for n in range(1, 4)])
        else:
            im[2 * m] = lin([(-sin24(2 * m * n), fe[n]) for n in range(1, 3)])
    return re, im


def y_stage(x, w):
    hi, lo = split(x)
    return jnp.dot(jnp.concatenate([hi, lo, hi], axis=1), w, preferred_element_type=F32)


def z_stage(tz, x, direction):
    hi, lo = split(x)
    rhs = jnp.concatenate([hi, hi, lo], axis=0)
    p = jnp.dot(tz, rhs, preferred_element_type=F32)
    re = p[:NZ, :NY] - direction * p[NZ:, NY:]
    im = p[:NZ, NY:] + direction * p[NZ:, :NY]
    return re, im


def forward(i, own, before, after, wf_ref, tz, work, spec):
    @pl.loop(0, 8)
    def _(chunk):
        rows = pl.ds(pl.multiple_of(chunk * 8, 8), 8)
        r = (
            [before[i, n, rows] for n in range(8)]
            + [own[i, n, rows] for n in range(8)]
            + [after[i, n, rows] for n in range(8)]
        )
        re, im = real_dft24(r)
        for k in range(KX):
            work[k, rows, :NY] = re[k]
            work[k, rows, NY:] = im[k] if im[k] is not None else jnp.zeros_like(re[k])

    y = y_stage(work[...].reshape(KX * NZ, 2 * NY), wf_ref[...])
    work[...] = y.reshape(KX, NZ, 2 * NY)
    for k in range(KX):
        re, im = z_stage(tz, work[k], -1.0)
        spec[i, k, :, :NY] = re
        spec[i, k, :, NY:] = im


def boltzmann(slot, q, wi_ref, tz, work, spec, total_ref, sum_ref):
    @pl.loop(0, 8)
    def _(chunk):
        start = pl.multiple_of(chunk * 8, 8)
        rows = pl.ds(start, 8)
        low = pl.ds(start + NZ, 8)
        for k in range(KX):
            p, lane = k // 2, (k % 2) * NY
            re = im = None
            for t in range(8):
                gr, gi = spec[t, k, rows, :NY], spec[t, k, rows, NY:]
                qr = q[slot, t, p, rows, lane : lane + NY]
                qi = q[slot, t, p, low, lane : lane + NY]
                tr = gr * qr - gi * qi
                ti = gr * qi + gi * qr
                re = tr if re is None else re + tr
                im = ti if im is None else im + ti
            work[k, rows, :NY] = re
            work[k, rows, NY:] = im

    for k in range(KX):
        re, im = z_stage(tz, work[k], 1.0)
        work[k, :, :NY] = re
        work[k, :, NY:] = im
    y = y_stage(work[...].reshape(KX * NZ, 2 * NY), wi_ref[...])
    work[...] = y.reshape(KX, NZ, 2 * NY)
    sum_ref[slot] = jnp.zeros((8, NY), F32)
    scale = 1.0 / (EXT * NZ * NY)

    @pl.loop(0, 8)
    def _(chunk):
        rows = pl.ds(pl.multiple_of(chunk * 8, 8), 8)
        fr = [work[k, rows, :NY] for k in range(KX)]
        fi = [work[k, rows, NY:] for k in range(KX)]
        acc = sum_ref[slot]
        for m in range(5):
            even, odd = [], []
            for k in range(KX):
                w = scale * (1.0 if k in (0, 12) else 2.0) * (-1) ** k
                even.append((w * cos24(k * m), fr[k]))
                odd.append((w * sin24(k * m), fi[k]))
            even, odd = sum_terms(even), sum_terms(odd)
            for x, e in ((4, even),) if m == 0 else ((4 + m, even - odd), (4 - m, even + odd)):
                if x < 8:
                    b = jnp.exp(-ENERGY_CAP * jnp.tanh(e / ENERGY_CAP))
                    total_ref[slot, x, rows] = b
                    acc = acc + b
        sum_ref[slot] = acc


def energy_kernel(
    slabs,
    ids,
    rots,
    offs,
    turns,
    receptor,
    library,
    te_hbm,
    to_hbm,
    swap_ref,
    lane_ref,
    zstep_ref,
    tz_ref,
    wf_ref,
    wi_ref,
    total_ref,
    sum_ref,
    lib,
    te,
    to,
    own,
    before,
    after,
    xa,
    xb,
    kd,
    even,
    odd,
    tzs,
    ph,
    q,
    spec,
    work,
    send,
    recv,
    hand_send,
    hand_recv,
    near,
):
    terms = receptor.shape[0]
    half = terms // 2
    slots = total_ref.shape[0]
    slab = lax.axis_index("slab")
    probe = lax.axis_index("probe")
    core = lax.rem(probe, 2)
    right = {"slab": lax.rem(slab + 1, slabs)}
    left = {"slab": lax.rem(slab + slabs - 1, slabs)}
    other = {"probe": probe + 1 - 2 * core}

    barrier = pltpu.get_barrier_semaphore()
    for device in (left, right, other):
        pl.semaphore_signal(barrier, inc=1, device_id=device, device_id_type=MESH)
    nearby = [
        pltpu.make_async_copy(library, lib, near.at[0]),
        pltpu.make_async_copy(te_hbm, te, near.at[1]),
        pltpu.make_async_copy(to_hbm, to, near.at[2]),
        pltpu.make_async_copy(receptor.at[pl.ds(core * half, half)], own.at[pl.ds(0, half)], near.at[3]),
        pltpu.make_async_copy(receptor.at[pl.ds((1 - core) * half, half)], own.at[pl.ds(half, half)], near.at[4]),
    ]
    pl.semaphore_wait(barrier, 3)

    def halo_copy(j, side):
        return pltpu.make_async_remote_copy(
            src_ref=receptor.at[core * half + j],
            dst_ref=(before, after)[side].at[j],
            send_sem=send.at[side, j],
            recv_sem=recv.at[side, j],
            device_id=(right, left)[side],
            device_id_type=MESH,
        )

    def hand_copy(j, side):
        ref = (before, after)[side]
        return pltpu.make_async_remote_copy(
            src_ref=ref.at[j],
            dst_ref=ref.at[half + j],
            send_sem=hand_send.at[side, j],
            recv_sem=hand_recv.at[side, j],
            device_id=other,
            device_id_type=MESH,
        )

    def hand_over(j):
        for side in range(2):
            halo_copy(j, side).wait_recv()
            hand_copy(j, side).start()

    for j in range(half):
        for side in range(2):
            halo_copy(j, side).start()
    for copy in nearby:
        copy.start()
    nearby[0].wait()
    turned_probes(ids, rots, offs, turns, core, lib, swap_ref, lane_ref, zstep_ref, xa, xb, kd, even, odd, tzs, ph)
    for copy in nearby[1:]:
        copy.wait()

    def pairs(low, high):
        @pl.loop(low, high)
        def _(p):
            probe_pair(p, te, to, even, odd, tzs, ph, q)

    pairs(0, 3)
    hand_over(0)
    pairs(3, PAIRS)
    hand_over(1)
    tz = tz_ref[...]

    @pl.loop(0, half)
    def _(j):
        @pl.when(j >= 2)
        def _():
            hand_over(j)

        @pl.loop(0, 2)
        def _(h):
            @pl.when(h == 1)
            def _():
                for side in range(2):
                    hand_copy(j, side).wait_recv()

            forward(j + half * h, own, before, after, wf_ref, tz, work, spec)

    @pl.loop(0, slots)
    def _(slot):
        boltzmann(slot, q, wi_ref, tz, work, spec, total_ref, sum_ref)

    @pl.loop(0, half)
    def _(j):
        for side in range(2):
            halo_copy(j, side).wait_send()
            hand_copy(j, side).wait_send()


def sum_terms(terms):
    total = None
    for coef, value in terms:
        if abs(coef) < 1e-15:
            continue
        total = coef * value if total is None else total + coef * value
    return total


def tail_kernel(
    slabs,
    probes,
    cells,
    types,
    total_ref,
    sum_ref,
    weight_ref,
    out_ref,
    mine,
    gathered,
    halo,
    mixed,
    blocks,
    part_send,
    part_recv,
    halo_send,
    halo_recv,
    block_send,
    block_recv,
):
    slots = total_ref.shape[0]
    planes = total_ref.shape[1]
    rows = out_ref.shape[1]
    slab = lax.axis_index("slab")
    probe = lax.axis_index("probe")

    barrier = pltpu.get_barrier_semaphore()

    @pl.loop(1, slabs)
    def _(d):
        pl.semaphore_signal(
            barrier, inc=1, device_id={"slab": lax.rem(slab + d, slabs)}, device_id_type=MESH
        )

    for d in range(1, probes):
        pl.semaphore_signal(
            barrier, inc=1, device_id={"probe": lax.rem(probe + d, probes)}, device_id_type=MESH
        )

    parts = []
    for s in range(slots):
        v = jnp.sum(sum_ref[s], axis=0, keepdims=True)
        v = jnp.sum(v, axis=1, keepdims=True)
        parts.append(jnp.broadcast_to(v, (1, NY)))
    parts += [jnp.zeros((1, NY), F32)] * (8 - slots)
    own = jnp.concatenate(parts, axis=0)
    mine[...] = own

    pl.semaphore_wait(barrier, slabs - 1 + probes - 1)

    def part_copy(d):
        return pltpu.make_async_remote_copy(
            src_ref=mine,
            dst_ref=gathered.at[d],
            send_sem=part_send.at[d],
            recv_sem=part_recv.at[d],
            device_id={"slab": lax.rem(slab + d, slabs)},
            device_id_type=MESH,
        )

    @pl.loop(1, slabs)
    def _(d):
        part_copy(d).start()

    to_right = pltpu.make_async_remote_copy(
        src_ref=total_ref.at[:, planes - 1],
        dst_ref=halo.at[0],
        send_sem=halo_send.at[0],
        recv_sem=halo_recv.at[0],
        device_id={"slab": lax.rem(slab + 1, slabs)},
        device_id_type=MESH,
    )
    to_left = pltpu.make_async_remote_copy(
        src_ref=total_ref.at[:, 0],
        dst_ref=halo.at[1],
        send_sem=halo_send.at[1],
        recv_sem=halo_recv.at[1],
        device_id={"slab": lax.rem(slab + slabs - 1, slabs)},
        device_id_type=MESH,
    )
    to_right.start()
    to_left.start()

    @pl.loop(1, slabs)
    def _(d):
        part_copy(d).wait_recv()

    partition = own
    for d in range(1, slabs):
        partition = partition + gathered[d]
    coef = weight_ref[...] * (cells / partition)
    coefs = [jnp.broadcast_to(coef[s : s + 1], (8, NY)) for s in range(slots)]

    def weighted(read):
        total = None
        for s in range(slots):
            v = read(s).reshape(NZ // 8, 8, NY) * coefs[s][None]
            total = v if total is None else total + v
        return total.reshape(NZ, NY)

    to_right.wait_recv()
    to_left.wait_recv()
    mixed[0] = weighted(lambda s: halo[0, s])
    mixed[planes + 1] = weighted(lambda s: halo[1, s])
    for x in range(planes):
        mixed[x + 1] = weighted(lambda s: total_ref[s, x])
    for x in range(planes):
        v = (mixed[x] + 2.0 * mixed[x + 1] + mixed[x + 2]) * 0.25
        v = (pltpu.roll(v, 1, 0) + 2.0 * v + pltpu.roll(v, NZ - 1, 0)) * 0.25
        v = (pltpu.roll(v, 1, 1) + 2.0 * v + pltpu.roll(v, NY - 1, 1)) * 0.25
        mixed[x] = v

    def block_copy(d):
        target = lax.rem(probe + d, probes)
        return pltpu.make_async_remote_copy(
            src_ref=mixed.at[pl.ds(0, planes), pl.ds(pl.multiple_of(target * rows, 8), rows)],
            dst_ref=blocks.at[d - 1],
            send_sem=block_send.at[d - 1],
            recv_sem=block_recv.at[d - 1],
            device_id={"probe": target},
            device_id_type=MESH,
        )

    for d in range(1, probes):
        block_copy(d).start()
    result = mixed[pl.ds(0, planes), pl.ds(pl.multiple_of(probe * rows, 8), rows)]
    for d in range(1, probes):
        block_copy(d).wait_recv()
        result = result + blocks[d - 1]
    out_ref[...] = result * (1.0 / types)

    @pl.loop(1, slabs)
    def _(d):
        part_copy(d).wait_send()

    to_right.wait_send()
    to_left.wait_send()
    for d in range(1, probes):
        block_copy(d).wait_send()


def energy_call(slabs, receptor, library, probe_ids, rotations, offsets):
    terms, planes, nz, ny = receptor.shape
    slots, half = probe_ids.shape[0], terms // 2
    te, to = xy_tables()
    smem = pl.BlockSpec(memory_space=pltpu.SMEM)
    vmem = pl.BlockSpec(memory_space=pltpu.VMEM)
    hbm = pl.BlockSpec(memory_space=pl.ANY)
    dma = pltpu.SemaphoreType.DMA
    return pl.pallas_call(
        functools.partial(energy_kernel, slabs),
        in_specs=[smem] * 4 + [hbm] * 4 + [vmem] * 6,
        out_specs=[vmem, vmem],
        out_shape=[
            jax.ShapeDtypeStruct((slots, planes, nz, ny), F32),
            jax.ShapeDtypeStruct((slots, 8, ny), F32),
        ],
        scratch_shapes=[
            pltpu.VMEM(library.shape, F32),
            pltpu.VMEM(te.shape, BF),
            pltpu.VMEM(to.shape, BF),
            pltpu.VMEM(receptor.shape, F32),
            pltpu.VMEM(receptor.shape, F32),
            pltpu.VMEM(receptor.shape, F32),
            pltpu.VMEM((KS, terms, CUBE), F32),
            pltpu.VMEM((KS, terms, CUBE), F32),
            pltpu.VMEM((PACK // 128, terms * AZ, 128), F32),
            pltpu.VMEM((slots * terms * AZ, PACK), BF),
            pltpu.VMEM((slots * terms * AZ, PACK), BF),
            pltpu.VMEM((slots, 2 * NZ, 6 * AZ), BF),
            pltpu.VMEM((slots, 2, 8, 2 * NY), F32),
            pltpu.VMEM((slots, terms, PAIRS, 2 * NZ, 2 * NY), F32),
            pltpu.VMEM((terms, KX, nz, 2 * ny), F32),
            pltpu.VMEM((KX, nz, 2 * ny), F32),
            dma((2, half)),
            dma((2, half)),
            dma((2, half)),
            dma((2, half)),
            dma((5,)),
        ],
        compiler_params=pltpu.CompilerParams(
            collective_id=1, has_side_effects=True, vmem_limit_bytes=63 << 20
        ),
        name="energy_maps",
    )(
        probe_ids,
        rotations,
        offsets,
        jnp.asarray(rotation_table()),
        receptor,
        library,
        jnp.asarray(te),
        jnp.asarray(to),
        jnp.asarray(swap_table()),
        jnp.asarray(lane_offsets()),
        jnp.asarray(probe_z_steps()),
        jnp.asarray(grid_z_table()),
        jnp.asarray(grid_y_table(-1.0)),
        jnp.asarray(grid_y_table(1.0)),
    )


def local(receptor, library, probe_ids, rotations, offsets, probe_weight):
    terms, planes, nz, ny = receptor.shape
    slabs = lax.axis_size("slab")
    probes = lax.axis_size("probe")
    slots = probe_ids.shape[0]
    types = probe_weight.shape[0]
    cells = float(planes * slabs * nz * ny)

    total, sums = energy_call(
        slabs, receptor, library, probe_ids, rotations.reshape(-1), offsets.reshape(-1)
    )

    onehot = (probe_ids[:, None] == jnp.arange(types, dtype=jnp.int32)[None, :]).astype(F32)
    chosen = jnp.sum(onehot * probe_weight[None], axis=1)
    weight = jnp.broadcast_to(jnp.pad(chosen, (0, 8 - slots))[:, None], (8, ny))
    rows = nz // probes
    vmem = pl.BlockSpec(memory_space=pltpu.VMEM)
    return pl.pallas_call(
        functools.partial(tail_kernel, slabs, probes, cells, types),
        in_specs=[vmem] * 3,
        out_specs=vmem,
        out_shape=jax.ShapeDtypeStruct((planes, rows, ny), F32),
        scratch_shapes=[
            pltpu.VMEM((8, ny), F32),
            pltpu.VMEM((slabs, 8, ny), F32),
            pltpu.VMEM((2, slots, nz, ny), F32),
            pltpu.VMEM((planes + 2, nz, ny), F32),
            pltpu.VMEM((probes - 1, planes, rows, ny), F32),
            pltpu.SemaphoreType.DMA((slabs,)),
            pltpu.SemaphoreType.DMA((slabs,)),
            pltpu.SemaphoreType.DMA((2,)),
            pltpu.SemaphoreType.DMA((2,)),
            pltpu.SemaphoreType.DMA((probes - 1,)),
            pltpu.SemaphoreType.DMA((probes - 1,)),
        ],
        compiler_params=pltpu.CompilerParams(
            collective_id=0, has_side_effects=True, vmem_limit_bytes=24 << 20
        ),
        name="consensus_tail",
    )(total, sums, weight)


def solution(mesh):
    in_specs = (
        P(None, "slab", None, None),
        P(),
        P("probe"),
        P("probe", None),
        P("probe", None, None),
        P(),
    )
    out_specs = P("slab", "probe", None)
    return jax.shard_map(local, mesh=mesh, in_specs=in_specs, out_specs=out_specs, check_vma=False)
```

```python
import functools
import math

import jax
import jax.numpy as jnp
import ml_dtypes
import numpy as np
from jax import lax
from jax.experimental import pallas as pl
from jax.experimental.pallas import tpu as pltpu
from jax.sharding import PartitionSpec as P

RAD = 8
KS = 17
AZ = 24
EXT = 24
KX = 13
PAIRS = 7
NZ = 64
NY = 128
ENERGY_CAP = 6.0
HIGHEST = lax.Precision.HIGHEST
MESH = pl.DeviceIdType.MESH
BF = jnp.bfloat16
F32 = jnp.float32


def cube_rotations():
    permutes = [(0, 1, 2), (0, 2, 1), (1, 0, 2), (1, 2, 0), (2, 0, 1), (2, 1, 0)]
    parities = [1, -1, -1, 1, 1, -1]
    perms, signs = [], []
    for permute, parity in zip(permutes, parities):
        for sign_x in (1, -1):
            for sign_y in (1, -1):
                for sign_z in (1, -1):
                    if parity * sign_x * sign_y * sign_z == 1:
                        perms.append(permute)
                        signs.append((sign_x, sign_y, sign_z))
    return np.array(perms, np.int32), np.array(signs, np.int32)


def split_np(table):
    table = table.astype(np.float32)
    hi = table.astype(ml_dtypes.bfloat16)
    lo = (table - hi.astype(np.float32)).astype(ml_dtypes.bfloat16)
    return hi, lo


HALF = (KS * KS + 1) // 2
CUBE = 384
PACK = 512


def half_offsets():
    flat = np.arange(HALF) + HALF - 1
    return flat // KS - RAD, flat % KS - RAD


def xy_tables():
    ax, ay = half_offsets()
    kx = np.arange(2 * PAIRS)
    ky = np.arange(NY)
    px = (ax[:, None] * kx[None, :]) % EXT / EXT
    py = (ay[:, None] * ky[None, :]) % NY / NY
    ang = 2 * np.pi * (px[:, :, None] + py[:, None, :])
    live = (kx < KX).astype(np.float64)[None, :, None]
    out = []
    for t in (np.cos(ang) * live, np.sin(ang) * live):
        hi, lo = split_np(t.reshape(HALF, -1))
        pad = np.zeros((PACK - 3 * HALF, hi.shape[1]), hi.dtype)
        out.append(np.concatenate([hi, hi, lo, pad], axis=0))
    return out


def lane_offsets():
    ax, ay = half_offsets()
    rows = np.full((8, PACK), 10000, np.int32)
    for c in range(3):
        rows[0, c * HALF : (c + 1) * HALF] = ax
        rows[1, c * HALF : (c + 1) * HALF] = ay
    rows[2] = 0
    rows[2, [0, HALF, 2 * HALF]] = 10000
    return rows


def swap_table():
    t = np.zeros((CUBE, CUBE), np.float32)
    for m in range(KS):
        for n in range(KS):
            t[n * KS + m, m * KS + n] = 1
    return t.astype(ml_dtypes.bfloat16)


def rotation_table():
    perms, signs = cube_rotations()
    table = np.zeros((24, 4), np.int32)
    for q in range(24):
        zaxis = [i for i in range(3) if perms[q, i] == 2][0]
        others = [i for i in range(3) if i != zaxis]
        table[q, 0] = zaxis
        table[q, 1] = 1 if signs[q, zaxis] < 0 else 0
        for i, unit in zip(others, (KS, 1)):
            table[q, 2 + perms[q, i]] = unit * signs[q, i]
    return table


def probe_z_steps():
    kz = np.arange(2 * NZ) % NZ
    lane = np.arange(6 * AZ) % (2 * AZ)
    az = lane % AZ
    quarter = np.where((np.arange(2 * NZ) < NZ)[:, None], np.where(lane < AZ, 0, 16), np.where(lane < AZ, -16, 0))
    turn = (kz[:, None] * (az - RAD)[None, :] + quarter) % NZ
    live = np.broadcast_to((az < KS).astype(np.int64)[None], turn.shape)
    return np.stack([turn, np.broadcast_to(kz[:, None], turn.shape), live]).astype(np.int32)


def grid_z_table():
    k = np.arange(NZ)
    ang = 2 * np.pi * ((k[:, None] * k[None, :]) % NZ) / NZ
    t = np.concatenate([np.cos(ang), np.sin(ang)], axis=0)
    hi, lo = split_np(t)
    return np.concatenate([hi, lo, hi], axis=1)


def grid_y_table(direction):
    k = np.arange(NY)
    ang = 2 * np.pi * ((k[:, None] * k[None, :]) % NY) / NY
    c, s = np.cos(ang), direction * np.sin(ang)
    hi, lo = split_np(np.block([[c, s], [-s, c]]))
    return np.concatenate([hi, hi, lo], axis=0)


def split(x):
    hi = x.astype(BF)
    lo = (x - hi.astype(F32)).astype(BF)
    return hi, lo


def turned_probes(ids, rots, offs, turns, core, lib_ref, swap_ref, lane_ref, zstep_ref, xa, xb, kd, even, odd, tzs, ph):
    slots, terms = tzs.shape[0], lib_ref.shape[1]
    xa[...] = jnp.zeros_like(xa)
    kd[...] = jnp.zeros_like(kd)
    lane = lax.broadcasted_iota(jnp.int32, (terms, CUBE), 1)
    packed_lane = lax.broadcasted_iota(jnp.int32, (terms * AZ, 128), 1)
    source = lax.broadcasted_iota(jnp.int32, (CUBE, PACK), 0)
    zlane = lax.broadcasted_iota(jnp.int32, (2 * NZ, 6 * AZ), 1)
    ky = lax.broadcasted_iota(jnp.int32, (8, 2 * NY), 1) % NY

    def permuted(x, table):
        hi, lo = split(x)
        out = jnp.dot(jnp.concatenate([hi, lo], axis=0), table, preferred_element_type=F32)
        return out[: x.shape[0]] + out[x.shape[0] :]

    @pl.loop(0, slots)
    def _(slot):
        rot = rots[slot, 0]
        zaxis, flipped = turns[rot, 0], turns[rot, 1]
        step_x, step_y = turns[rot, 2], turns[rot, 3]
        off_y, off_z = offs[slot, 0, 0], offs[slot, 0, 1]

        turn = (zstep_ref[0] - zstep_ref[1] * off_z + NZ * NZ) & (NZ - 1)
        t = jnp.cos(turn.astype(F32) * (2 * math.pi / NZ)) * zstep_ref[2].astype(F32)
        hi, lo = split(t)
        tzs[slot] = jnp.where((zlane >= 2 * AZ) & (zlane < 4 * AZ), lo.astype(F32), hi.astype(F32)).astype(BF)
        turn = ky * off_y
        ph[slot, 0] = jnp.cos((turn & (NY - 1)).astype(F32) * (2 * math.pi / NY))
        ph[slot, 1] = jnp.cos(((turn - NY // 4) & (NY - 1)).astype(F32) * (2 * math.pi / NY))

        for m in range(KS):
            w = lib_ref[ids[slot], :, m * KS * KS : (m + 1) * KS * KS]
            xa[m, :, : KS * KS] = jnp.where(core == 0, w, pltpu.roll(w, terms // 2, 0))
        x = xa[...]
        swapped = permuted(x.reshape(KS * terms, CUBE), swap_ref[...]).reshape(KS, terms, CUBE)
        xa[...] = jnp.where(zaxis == 2, swapped, x)
        for m in range(KS):
            acc = jnp.zeros((terms, CUBE), F32)
            for n in range(KS):
                moved = pltpu.roll(xa[n], ((n - m) * KS) % CUBE, 1)
                acc = jnp.where((lane >= n * KS) & (lane < (n + 1) * KS), moved, acc)
            xb[m] = jnp.where(zaxis == 0, xa[m], acc)

        here = lane_ref[0:1] * step_x + lane_ref[1:2] * step_y + (HALF - 1)
        there = 2 * (HALF - 1) - here + lane_ref[2:3]
        plus = (source == here).astype(F32)
        minus = (source == there).astype(F32)
        x = xb[...].reshape(KS * terms, CUBE)
        for table, ref in ((plus + minus, even), (plus - minus, odd)):
            turned = permuted(x, table.astype(BF))
            for m in range(KS):
                f = KS - 1 - m
                row = jnp.where(flipped == 1, turned[f * terms : (f + 1) * terms], turned[m * terms : (m + 1) * terms])
                for j in range(PACK // 128):
                    kd[j, pl.ds(m, terms, stride=AZ), :] = row[:, j * 128 : (j + 1) * 128]
            rows = pl.ds(pl.multiple_of(slot * terms * AZ, terms * AZ), terms * AZ)
            for j in range(PACK // 128):
                hi, lo = split(kd[j])
                packed = packed_lane + j * 128
                low = (packed >= HALF) & (packed < 2 * HALF)
                ref[rows, j * 128 : (j + 1) * 128] = jnp.where(low, lo.astype(F32), hi.astype(F32)).astype(BF)


def probe_pair(p, te, to, even, odd, tzs, ph, q):
    slots, terms = q.shape[0], q.shape[1]
    columns = pl.ds(pl.multiple_of(p * 2 * NY, 2 * NY), 2 * NY)
    re_all = jnp.dot(even[...], te[:, columns], preferred_element_type=F32)
    im_all = jnp.dot(odd[...], to[:, columns], preferred_element_type=F32)
    for s in range(slots):
        c, n = ph[s, 0, 0:1], ph[s, 1, 0:1]
        rows = slice(s * terms * AZ, (s + 1) * terms * AZ)
        re = re_all[rows] * c + im_all[rows] * n
        im = im_all[rows] * c - re_all[rows] * n
        tz = tzs[s]
        for t in range(terms):
            d = jnp.concatenate([re[t * AZ : (t + 1) * AZ], im[t * AZ : (t + 1) * AZ]], axis=0)
            hi, lo = split(d)
            q[s, t, p] = jnp.dot(tz, jnp.concatenate([hi, hi, lo], axis=0), preferred_element_type=F32)


def cos24(m):
    return math.cos(2 * math.pi * (m % 24) / 24)


def sin24(m):
    return math.sin(2 * math.pi * (m % 24) / 24)


def lin(terms):
    total = None
    for coef, value in terms:
        if abs(coef) < 1e-12:
            continue
        if abs(coef - 1) < 1e-12:
            total = value if total is None else total + value
        elif abs(coef + 1) < 1e-12:
            total = -value if total is None else total - value
        else:
            total = coef * value if total is None else total + coef * value
    return total


def real_dft24(r):
    a = [r[0]] + [r[n] + r[24 - n] for n in range(1, 12)] + [r[12]]
    b = [None] + [r[n] - r[24 - n] for n in range(1, 12)]
    re, im = [None] * 13, [None] * 13
    c = [a[n] + a[12 - n] for n in range(6)] + [a[6]]
    d = [a[n] - a[12 - n] for n in range(6)]
    ce = [c[n] + c[6 - n] for n in range(3)] + [c[3]]
    co = [c[n] - c[6 - n] for n in range(3)]
    for m in range(7):
        if m % 2 == 0:
            re[2 * m] = lin([(cos24(2 * m * n), ce[n]) for n in range(4)])
        else:
            re[2 * m] = lin([(cos24(2 * m * n), co[n]) for n in range(3)])
    for k in range(1, 12, 2):
        re[k] = lin([(cos24(k * n), d[n]) for n in range(6)])
    e = [None] + [b[n] + b[12 - n] for n in range(1, 6)] + [b[6]]
    f = [None] + [b[n] - b[12 - n] for n in range(1, 6)]
    for k in range(1, 12, 2):
        im[k] = lin([(-sin24(k * n), e[n]) for n in range(1, 7)])
    fo = [None] + [f[n] + f[6 - n] for n in range(1, 3)] + [f[3]]
    fe = [None] + [f[n] - f[6 - n] for n in range(1, 3)]
    for m in range(1, 6):
        if m % 2 == 1:
            im[2 * m] = lin([(-sin24(2 * m * n), fo[n]) for n in range(1, 4)])
        else:
            im[2 * m] = lin([(-sin24(2 * m * n), fe[n]) for n in range(1, 3)])
    return re, im


def y_stage(x, w):
    hi, lo = split(x)
    return jnp.dot(jnp.concatenate([hi, lo, hi], axis=1), w, preferred_element_type=F32)


def z_stage(tz, x, direction):
    hi, lo = split(x)
    rhs = jnp.concatenate([hi, hi, lo], axis=0)
    p = jnp.dot(tz, rhs, preferred_element_type=F32)
    re = p[:NZ, :NY] - direction * p[NZ:, NY:]
    im = p[:NZ, NY:] + direction * p[NZ:, :NY]
    return re, im


def forward(i, own, before, after, wf_ref, tz, work, spec):
    @pl.loop(0, 8)
    def _(chunk):
        rows = pl.ds(pl.multiple_of(chunk * 8, 8), 8)
        r = (
            [before[i, n, rows] for n in range(8)]
            + [own[i, n, rows] for n in range(8)]
            + [after[i, n, rows] for n in range(8)]
        )
        re, im = real_dft24(r)
        for k in range(KX):
            work[k, rows, :NY] = re[k]
            work[k, rows, NY:] = im[k] if im[k] is not None else jnp.zeros_like(re[k])

    y = y_stage(work[...].reshape(KX * NZ, 2 * NY), wf_ref[...])
    work[...] = y.reshape(KX, NZ, 2 * NY)
    for k in range(KX):
        re, im = z_stage(tz, work[k], -1.0)
        spec[i, k, :, :NY] = re
        spec[i, k, :, NY:] = im


def contract(slot, group, q, spec, source, target):
    @pl.loop(0, 8)
    def _(chunk):
        start = pl.multiple_of(chunk * 8, 8)
        rows = pl.ds(start, 8)
        low = pl.ds(start + NZ, 8)
        for k in range(KX):
            p, lane = k // 2, (k % 2) * NY
            re = None if source is None else source[k, rows, :NY]
            im = None if source is None else source[k, rows, NY:]
            for t in group:
                gr, gi = spec[t, k, rows, :NY], spec[t, k, rows, NY:]
                qr = q[slot, t, p, rows, lane : lane + NY]
                qi = q[slot, t, p, low, lane : lane + NY]
                tr = gr * qr - gi * qi
                ti = gr * qi + gi * qr
                re = tr if re is None else re + tr
                im = ti if im is None else im + ti
            target[k, rows, :NY] = re
            target[k, rows, NY:] = im


def boltzmann(slot, wi_ref, tz, work, total_ref, sum_ref):
    for k in range(KX):
        re, im = z_stage(tz, work[k], 1.0)
        work[k, :, :NY] = re
        work[k, :, NY:] = im
    y = y_stage(work[...].reshape(KX * NZ, 2 * NY), wi_ref[...])
    work[...] = y.reshape(KX, NZ, 2 * NY)
    sum_ref[slot] = jnp.zeros((8, NY), F32)
    scale = 1.0 / (EXT * NZ * NY)

    @pl.loop(0, 8)
    def _(chunk):
        rows = pl.ds(pl.multiple_of(chunk * 8, 8), 8)
        fr = [work[k, rows, :NY] for k in range(KX)]
        fi = [work[k, rows, NY:] for k in range(KX)]
        acc = sum_ref[slot]
        for m in range(5):
            even, odd = [], []
            for k in range(KX):
                w = scale * (1.0 if k in (0, 12) else 2.0) * (-1) ** k
                even.append((w * cos24(k * m), fr[k]))
                odd.append((w * sin24(k * m), fi[k]))
            even, odd = sum_terms(even), sum_terms(odd)
            for x, e in ((4, even),) if m == 0 else ((4 + m, even - odd), (4 - m, even + odd)):
                if x < 8:
                    b = jnp.exp(-ENERGY_CAP * jnp.tanh(e / ENERGY_CAP))
                    total_ref[slot, x, rows] = b
                    acc = acc + b
        sum_ref[slot] = acc


def energy_kernel(
    slabs,
    probes,
    cells,
    ids,
    rots,
    offs,
    weights,
    turns,
    receptor,
    library,
    te_hbm,
    to_hbm,
    swap_ref,
    lane_ref,
    zstep_ref,
    tz_ref,
    wf_ref,
    wi_ref,
    out_ref,
    lib,
    te,
    to,
    own,
    before,
    after,
    xa,
    xb,
    kd,
    even,
    odd,
    tzs,
    ph,
    q,
    spec,
    work,
    joint,
    total,
    sums,
    mine,
    gathered,
    faces,
    mixed,
    blocks,
    send,
    recv,
    hand_send,
    hand_recv,
    near,
    part_send,
    part_recv,
    face_send,
    face_recv,
    block_send,
    block_recv,
):
    terms, planes = receptor.shape[0], receptor.shape[1]
    half = terms // 2
    slots = total.shape[0]
    rows = out_ref.shape[1]
    slab = lax.axis_index("slab")
    probe = lax.axis_index("probe")
    core = lax.rem(probe, 2)
    right = {"slab": lax.rem(slab + 1, slabs)}
    left = {"slab": lax.rem(slab + slabs - 1, slabs)}
    sibling = probe + 1 - 2 * core
    partner = lax.rem(probe + 2, probes)
    other = {"probe": sibling}

    barrier = pltpu.get_barrier_semaphore()

    @pl.loop(1, slabs)
    def _(d):
        pl.semaphore_signal(barrier, inc=1, device_id={"slab": lax.rem(slab + d, slabs)}, device_id_type=MESH)

    for device in (sibling, partner):
        pl.semaphore_signal(barrier, inc=1, device_id={"probe": device}, device_id_type=MESH)
    nearby = [
        pltpu.make_async_copy(library, lib, near.at[0]),
        pltpu.make_async_copy(te_hbm, te, near.at[1]),
        pltpu.make_async_copy(to_hbm, to, near.at[2]),
        pltpu.make_async_copy(receptor.at[pl.ds(core * half, half)], own.at[pl.ds(0, half)], near.at[3]),
        pltpu.make_async_copy(receptor.at[pl.ds((1 - core) * half, half)], own.at[pl.ds(half, half)], near.at[4]),
    ]
    pl.semaphore_wait(barrier, slabs - 1 + 2)

    def halo_copy(j, side):
        return pltpu.make_async_remote_copy(
            src_ref=receptor.at[core * half + j],
            dst_ref=(before, after)[side].at[j],
            send_sem=send.at[side, j],
            recv_sem=recv.at[side, j],
            device_id=(right, left)[side],
            device_id_type=MESH,
        )

    def hand_copy(j, side):
        ref = (before, after)[side]
        return pltpu.make_async_remote_copy(
            src_ref=ref.at[j],
            dst_ref=ref.at[half + j],
            send_sem=hand_send.at[side, j],
            recv_sem=hand_recv.at[side, j],
            device_id=other,
            device_id_type=MESH,
        )

    def hand_over(j):
        for side in range(2):
            halo_copy(j, side).wait_recv()
            hand_copy(j, side).start()

    for j in range(half):
        for side in range(2):
            halo_copy(j, side).start()
    for copy in nearby:
        copy.start()
    nearby[0].wait()
    turned_probes(ids, rots, offs, turns, core, lib, swap_ref, lane_ref, zstep_ref, xa, xb, kd, even, odd, tzs, ph)
    for copy in nearby[1:]:
        copy.wait()

    def pairs(low, high):
        @pl.loop(low, high)
        def _(p):
            probe_pair(p, te, to, even, odd, tzs, ph, q)

    tz = tz_ref[...]

    def transforms(j):
        @pl.loop(0, 2)
        def _(h):
            @pl.when(h == 1)
            def _():
                for side in range(2):
                    hand_copy(j, side).wait_recv()

            forward(j + half * h, own, before, after, wf_ref, tz, work, spec)

    pairs(0, 3)
    hand_over(0)
    pairs(3, PAIRS)
    hand_over(1)

    @pl.loop(0, 2)
    def _(j):
        transforms(j)

    @pl.loop(0, slots)
    def _(slot):
        contract(slot, (0, 1, half, half + 1), q, spec, None, joint.at[slot])

    hand_over(2)
    transforms(2)

    @pl.loop(0, slots)
    def _(slot):
        contract(slot, (2, half + 2), q, spec, joint.at[slot], joint.at[slot])

    hand_over(3)
    transforms(3)

    def face_copy(slot, side):
        return pltpu.make_async_remote_copy(
            src_ref=total.at[slot, (planes - 1, 0)[side]],
            dst_ref=faces.at[side, slot],
            send_sem=face_send.at[side, slot],
            recv_sem=face_recv.at[side, slot],
            device_id=(right, left)[side],
            device_id_type=MESH,
        )

    @pl.loop(0, slots)
    def _(slot):
        contract(slot, (3, half + 3), q, spec, joint.at[slot], work)
        boltzmann(slot, wi_ref, tz, work, total, sums)
        for side in range(2):
            face_copy(slot, side).start()

    parts = []
    for s in range(slots):
        v = jnp.sum(sums[s], axis=0, keepdims=True)
        parts.append(jnp.broadcast_to(jnp.sum(v, axis=1, keepdims=True), (1, NY)))
    parts += [jnp.zeros((1, NY), F32)] * (8 - slots)
    local_part = jnp.concatenate(parts, axis=0)
    mine[...] = local_part

    def part_copy(d):
        return pltpu.make_async_remote_copy(
            src_ref=mine,
            dst_ref=gathered.at[d],
            send_sem=part_send.at[d],
            recv_sem=part_recv.at[d],
            device_id={"slab": lax.rem(slab + d, slabs)},
            device_id_type=MESH,
        )

    @pl.loop(1, slabs)
    def _(d):
        part_copy(d).start()

    @pl.loop(0, slots)
    def _(slot):
        for side in range(2):
            face_copy(slot, side).wait_recv()

    @pl.loop(1, slabs)
    def _(d):
        part_copy(d).wait_recv()

    partition = local_part
    for d in range(1, slabs):
        partition = partition + gathered[d]
    share = cells / partition
    coefs = [jnp.broadcast_to(share[s : s + 1] * weights[ids[s]], (8, NY)) for s in range(slots)]

    def weighted(read):
        result = None
        for s in range(slots):
            v = read(s).reshape(NZ // 8, 8, NY) * coefs[s][None]
            result = v if result is None else result + v
        return result.reshape(NZ, NY)

    mixed[0] = weighted(lambda s: faces[0, s])
    mixed[planes + 1] = weighted(lambda s: faces[1, s])
    for x in range(planes):
        mixed[x + 1] = weighted(lambda s: total[s, x])
    for x in range(planes):
        v = (mixed[x] + 2.0 * mixed[x + 1] + mixed[x + 2]) * 0.25
        v = (pltpu.roll(v, 1, 0) + 2.0 * v + pltpu.roll(v, NZ - 1, 0)) * 0.25
        v = (pltpu.roll(v, 1, 1) + 2.0 * v + pltpu.roll(v, NY - 1, 1)) * 0.25
        mixed[x] = v

    def block(p):
        return mixed.at[pl.ds(0, planes), pl.ds(pl.multiple_of(p * rows, 8), rows)]

    away = partner + sibling - probe
    crossing = [
        pltpu.make_async_remote_copy(
            src_ref=block(p),
            dst_ref=blocks.at[i],
            send_sem=block_send.at[i],
            recv_sem=block_recv.at[i],
            device_id={"probe": device},
            device_id_type=MESH,
        )
        for i, (p, device) in enumerate(((away, sibling), (sibling, sibling)))
    ]
    last = pltpu.make_async_remote_copy(
        src_ref=blocks.at[2],
        dst_ref=blocks.at[3],
        send_sem=block_send.at[2],
        recv_sem=block_recv.at[2],
        device_id={"probe": partner},
        device_id_type=MESH,
    )
    for copy in crossing:
        copy.start()
    crossing[0].wait_recv()
    blocks[2] = block(partner)[...] + blocks[0]
    last.start()
    crossing[1].wait_recv()
    result = block(probe)[...] + blocks[1]
    last.wait_recv()
    out_ref[...] = (result + blocks[3]) * (1.0 / weights.shape[0])

    @pl.loop(0, half)
    def _(j):
        for side in range(2):
            halo_copy(j, side).wait_send()
            hand_copy(j, side).wait_send()

    @pl.loop(0, slots)
    def _(slot):
        for side in range(2):
            face_copy(slot, side).wait_send()

    @pl.loop(1, slabs)
    def _(d):
        part_copy(d).wait_send()

    for copy in (*crossing, last):
        copy.wait_send()


def sum_terms(terms):
    total = None
    for coef, value in terms:
        if abs(coef) < 1e-15:
            continue
        total = coef * value if total is None else total + coef * value
    return total


def local(receptor, library, probe_ids, rotations, offsets, probe_weight):
    terms, planes, nz, ny = receptor.shape
    slabs = lax.axis_size("slab")
    probes = lax.axis_size("probe")
    slots, half = probe_ids.shape[0], terms // 2
    rows = nz // probes
    cells = float(planes * slabs * nz * ny)
    te, to = xy_tables()
    smem = pl.BlockSpec(memory_space=pltpu.SMEM)
    vmem = pl.BlockSpec(memory_space=pltpu.VMEM)
    hbm = pl.BlockSpec(memory_space=pl.ANY)
    dma = pltpu.SemaphoreType.DMA
    return pl.pallas_call(
        functools.partial(energy_kernel, slabs, probes, cells),
        in_specs=[smem] * 5 + [hbm] * 4 + [vmem] * 6,
        out_specs=vmem,
        out_shape=jax.ShapeDtypeStruct((planes, rows, ny), F32),
        scratch_shapes=[
            pltpu.VMEM(library.shape, F32),
            pltpu.VMEM(te.shape, BF),
            pltpu.VMEM(to.shape, BF),
            pltpu.VMEM(receptor.shape, F32),
            pltpu.VMEM(receptor.shape, F32),
            pltpu.VMEM(receptor.shape, F32),
            pltpu.VMEM((KS, terms, CUBE), F32),
            pltpu.VMEM((KS, terms, CUBE), F32),
            pltpu.VMEM((PACK // 128, terms * AZ, 128), F32),
            pltpu.VMEM((slots * terms * AZ, PACK), BF),
            pltpu.VMEM((slots * terms * AZ, PACK), BF),
            pltpu.VMEM((slots, 2 * NZ, 6 * AZ), BF),
            pltpu.VMEM((slots, 2, 8, 2 * NY), F32),
            pltpu.VMEM((slots, terms, PAIRS, 2 * NZ, 2 * NY), F32),
            pltpu.VMEM((terms, KX, nz, 2 * ny), F32),
            pltpu.VMEM((KX, nz, 2 * ny), F32),
            pltpu.VMEM((slots, KX, nz, 2 * ny), F32),
            pltpu.VMEM((slots, planes, nz, ny), F32),
            pltpu.VMEM((slots, 8, ny), F32),
            pltpu.VMEM((8, ny), F32),
            pltpu.VMEM((slabs, 8, ny), F32),
            pltpu.VMEM((2, slots, nz, ny), F32),
            pltpu.VMEM((planes + 2, nz, ny), F32),
            pltpu.VMEM((4, planes, rows, ny), F32),
            dma((2, half)),
            dma((2, half)),
            dma((2, half)),
            dma((2, half)),
            dma((5,)),
            dma((slabs,)),
            dma((slabs,)),
            dma((2, slots)),
            dma((2, slots)),
            dma((3,)),
            dma((3,)),
        ],
        compiler_params=pltpu.CompilerParams(
            collective_id=0, has_side_effects=True, vmem_limit_bytes=63 << 20
        ),
        name="consensus_density",
    )(
        probe_ids,
        rotations,
        offsets,
        probe_weight,
        jnp.asarray(rotation_table()),
        receptor,
        library,
        jnp.asarray(te),
        jnp.asarray(to),
        jnp.asarray(swap_table()),
        jnp.asarray(lane_offsets()),
        jnp.asarray(probe_z_steps()),
        jnp.asarray(grid_z_table()),
        jnp.asarray(grid_y_table(-1.0)),
        jnp.asarray(grid_y_table(1.0)),
    )


def solution(mesh):
    in_specs = (
        P(None, "slab", None, None),
        P(),
        P("probe"),
        P("probe", None),
        P("probe", None, None),
        P(),
    )
    out_specs = P("slab", "probe", None)
    return jax.shard_map(local, mesh=mesh, in_specs=in_specs, out_specs=out_specs, check_vma=False)
```

```python
import functools
import math

import jax
import jax.numpy as jnp
import ml_dtypes
import numpy as np
from jax import lax
from jax.experimental import pallas as pl
from jax.experimental.pallas import tpu as pltpu
from jax.sharding import PartitionSpec as P

RAD = 8
KS = 17
AZ = 24
EXT = 24
KX = 13
PAIRS = 7
NZ = 64
NY = 128
ENERGY_CAP = 6.0
HIGHEST = lax.Precision.HIGHEST
MESH = pl.DeviceIdType.MESH
BF = jnp.bfloat16
F32 = jnp.float32


def cube_rotations():
    permutes = [(0, 1, 2), (0, 2, 1), (1, 0, 2), (1, 2, 0), (2, 0, 1), (2, 1, 0)]
    parities = [1, -1, -1, 1, 1, -1]
    perms, signs = [], []
    for permute, parity in zip(permutes, parities):
        for sign_x in (1, -1):
            for sign_y in (1, -1):
                for sign_z in (1, -1):
                    if parity * sign_x * sign_y * sign_z == 1:
                        perms.append(permute)
                        signs.append((sign_x, sign_y, sign_z))
    return np.array(perms, np.int32), np.array(signs, np.int32)


def split_np(table):
    table = table.astype(np.float32)
    hi = table.astype(ml_dtypes.bfloat16)
    lo = (table - hi.astype(np.float32)).astype(ml_dtypes.bfloat16)
    return hi, lo


HALF = (KS * KS + 1) // 2
CUBE = 384
PACK = 512


def half_offsets():
    flat = np.arange(HALF) + HALF - 1
    return flat // KS - RAD, flat % KS - RAD


def xy_tables():
    ax, ay = half_offsets()
    kx = np.arange(2 * PAIRS)
    ky = np.arange(NY)
    px = (ax[:, None] * kx[None, :]) % EXT / EXT
    py = (ay[:, None] * ky[None, :]) % NY / NY
    ang = 2 * np.pi * (px[:, :, None] + py[:, None, :])
    live = (kx < KX).astype(np.float64)[None, :, None]
    out = []
    for t in (np.cos(ang) * live, np.sin(ang) * live):
        hi, lo = split_np(t.reshape(HALF, -1))
        pad = np.zeros((PACK - 3 * HALF, hi.shape[1]), hi.dtype)
        out.append(np.concatenate([hi, hi, lo, pad], axis=0))
    return out


def lane_offsets():
    ax, ay = half_offsets()
    rows = np.full((8, CUBE), 10000, np.int32)
    rows[2:] = 0
    for c in range(2):
        lanes = slice(c * HALF, (c + 1) * HALF)
        rows[0, lanes] = ax
        rows[1, lanes] = ay
        rows[2, c * HALF] = 10000
        rows[3, lanes] = 1 - 2 * c
    return rows


def swap_table():
    t = np.zeros((CUBE, CUBE), np.float32)
    for m in range(KS):
        for n in range(KS):
            t[n * KS + m, m * KS + n] = 1
    return t.astype(ml_dtypes.bfloat16)


def rotation_table():
    perms, signs = cube_rotations()
    table = np.zeros((24, 4), np.int32)
    for q in range(24):
        zaxis = [i for i in range(3) if perms[q, i] == 2][0]
        others = [i for i in range(3) if i != zaxis]
        table[q, 0] = zaxis
        table[q, 1] = 1 if signs[q, zaxis] < 0 else 0
        for i, unit in zip(others, (KS, 1)):
            table[q, 2 + perms[q, i]] = unit * signs[q, i]
    return table


def probe_z_steps():
    kz = np.arange(2 * NZ) % NZ
    lane = np.arange(6 * AZ) % (2 * AZ)
    az = lane % AZ
    quarter = np.where((np.arange(2 * NZ) < NZ)[:, None], np.where(lane < AZ, 0, 16), np.where(lane < AZ, -16, 0))
    turn = (kz[:, None] * (az - RAD)[None, :] + quarter) % NZ
    live = np.broadcast_to((az < KS).astype(np.int64)[None], turn.shape)
    return np.stack([turn, np.broadcast_to(kz[:, None], turn.shape), live]).astype(np.int32)


def grid_z_table():
    k = np.arange(NZ)
    ang = 2 * np.pi * ((k[:, None] * k[None, :]) % NZ) / NZ
    t = np.concatenate([np.cos(ang), np.sin(ang)], axis=0)
    hi, lo = split_np(t)
    return np.concatenate([hi, lo, hi], axis=1)


def grid_y_table(direction):
    k = np.arange(NY)
    ang = 2 * np.pi * ((k[:, None] * k[None, :]) % NY) / NY
    c, s = np.cos(ang), direction * np.sin(ang)
    hi, lo = split_np(np.block([[c, s], [-s, c]]))
    return np.concatenate([hi, hi, lo], axis=0)


def split(x):
    hi = x.astype(BF)
    lo = (x - hi.astype(F32)).astype(BF)
    return hi, lo


def turned_probes(first, last, ids, rots, offs, turns, core, lib_ref, swap_ref, lane_ref, zstep_ref, xa, xb, kd, even, odd, tzs, ph):
    terms = lib_ref.shape[1]
    lane = lax.broadcasted_iota(jnp.int32, (terms, CUBE), 1)
    source = lax.broadcasted_iota(jnp.int32, (CUBE, CUBE), 0)
    zlane = lax.broadcasted_iota(jnp.int32, (2 * NZ, 6 * AZ), 1)
    ky = lax.broadcasted_iota(jnp.int32, (8, 2 * NY), 1) % NY

    def permuted(x, table):
        hi, lo = split(x)
        out = jnp.dot(jnp.concatenate([hi, lo], axis=0), table, preferred_element_type=F32)
        return out[: x.shape[0]] + out[x.shape[0] :]

    @pl.loop(first, last)
    def _(slot):
        rot = rots[slot]
        zaxis, flipped = turns[rot, 0], turns[rot, 1]
        step_x, step_y = turns[rot, 2], turns[rot, 3]
        off_y, off_z = offs[2 * slot], offs[2 * slot + 1]

        turn = (zstep_ref[0] - zstep_ref[1] * off_z + NZ * NZ) & (NZ - 1)
        t = jnp.cos(turn.astype(F32) * (2 * math.pi / NZ)) * zstep_ref[2].astype(F32)
        hi, lo = split(t)
        tzs[slot] = jnp.where((zlane >= 2 * AZ) & (zlane < 4 * AZ), lo.astype(F32), hi.astype(F32)).astype(BF)
        turn = ky * off_y
        ph[slot, 0] = jnp.cos((turn & (NY - 1)).astype(F32) * (2 * math.pi / NY))
        ph[slot, 1] = jnp.cos(((turn - NY // 4) & (NY - 1)).astype(F32) * (2 * math.pi / NY))

        for m in range(KS):
            w = lib_ref[ids[slot], :, m * KS * KS : (m + 1) * KS * KS]
            xa[m, :, : KS * KS] = jnp.where(core == 0, w, pltpu.roll(w, terms // 2, 0))
        x = xa[...]
        swapped = permuted(x.reshape(KS * terms, CUBE), swap_ref[...]).reshape(KS, terms, CUBE)
        xa[...] = jnp.where(zaxis == 2, swapped, x)
        for m in range(KS):
            acc = jnp.concatenate(
                [xa[n, :, m * KS : (m + 1) * KS] for n in range(KS)] + [jnp.zeros((terms, CUBE - KS * KS), F32)],
                axis=1,
            )
            xb[m] = jnp.where(zaxis == 0, xa[m], acc)

        here = lane_ref[0:1] * step_x + lane_ref[1:2] * step_y + (HALF - 1)
        there = 2 * (HALF - 1) - here + lane_ref[2:3]
        plus = (source == here).astype(F32)
        minus = jnp.where(source == there, lane_ref[3:4], 0).astype(F32)
        turned = permuted(xb[...].reshape(KS * terms, CUBE), (plus + minus).astype(BF))
        for m in range(KS):
            f = KS - 1 - m
            row = jnp.where(flipped == 1, turned[f * terms : (f + 1) * terms], turned[m * terms : (m + 1) * terms])
            for j in range(CUBE // 128):
                kd[j, pl.ds(m, terms, stride=AZ), :] = row[:, j * 128 : (j + 1) * 128]
        rows = pl.ds(pl.multiple_of(slot * terms * AZ, terms * AZ), terms * AZ)
        both = jnp.concatenate([kd[j] for j in range(CUBE // 128)], axis=1)
        hi, lo = split(both)
        hi, lo = hi.astype(F32), lo.astype(F32)
        spare = jnp.zeros((terms * AZ, PACK - 3 * HALF), F32)
        for ref, lanes in ((even, slice(0, HALF)), (odd, slice(HALF, 2 * HALF))):
            ref[rows, :] = jnp.concatenate([hi[:, lanes], lo[:, lanes], hi[:, lanes], spare], axis=1).astype(BF)


def probe_pair(p, te, to, even, odd, tzs, ph, q):
    slots, terms = q.shape[0], q.shape[1]
    columns = pl.ds(pl.multiple_of(p * 2 * NY, 2 * NY), 2 * NY)
    re_all = jnp.dot(even[...], te[:, columns], preferred_element_type=F32)
    im_all = jnp.dot(odd[...], to[:, columns], preferred_element_type=F32)
    for s in range(slots):
        c, n = ph[s, 0, 0:1], ph[s, 1, 0:1]
        rows = slice(s * terms * AZ, (s + 1) * terms * AZ)
        re = re_all[rows] * c + im_all[rows] * n
        im = im_all[rows] * c - re_all[rows] * n
        tz = tzs[s]
        for t in range(terms):
            d = jnp.concatenate([re[t * AZ : (t + 1) * AZ], im[t * AZ : (t + 1) * AZ]], axis=0)
            hi, lo = split(d)
            q[s, t, p] = jnp.dot(tz, jnp.concatenate([hi, hi, lo], axis=0), preferred_element_type=F32)


def cos24(m):
    return math.cos(2 * math.pi * (m % 24) / 24)


def sin24(m):
    return math.sin(2 * math.pi * (m % 24) / 24)


def lin(terms):
    total = None
    for coef, value in terms:
        if abs(coef) < 1e-12:
            continue
        if abs(coef - 1) < 1e-12:
            total = value if total is None else total + value
        elif abs(coef + 1) < 1e-12:
            total = -value if total is None else total - value
        else:
            total = coef * value if total is None else total + coef * value
    return total


def real_dft24(r):
    a = [r[0]] + [r[n] + r[24 - n] for n in range(1, 12)] + [r[12]]
    b = [None] + [r[n] - r[24 - n] for n in range(1, 12)]
    re, im = [None] * 13, [None] * 13
    c = [a[n] + a[12 - n] for n in range(6)] + [a[6]]
    d = [a[n] - a[12 - n] for n in range(6)]
    ce = [c[n] + c[6 - n] for n in range(3)] + [c[3]]
    co = [c[n] - c[6 - n] for n in range(3)]
    for m in range(7):
        if m % 2 == 0:
            re[2 * m] = lin([(cos24(2 * m * n), ce[n]) for n in range(4)])
        else:
            re[2 * m] = lin([(cos24(2 * m * n), co[n]) for n in range(3)])
    for k in range(1, 12, 2):
        re[k] = lin([(cos24(k * n), d[n]) for n in range(6)])
    e = [None] + [b[n] + b[12 - n] for n in range(1, 6)] + [b[6]]
    f = [None] + [b[n] - b[12 - n] for n in range(1, 6)]
    for k in range(1, 12, 2):
        im[k] = lin([(-sin24(k * n), e[n]) for n in range(1, 7)])
    fo = [None] + [f[n] + f[6 - n] for n in range(1, 3)] + [f[3]]
    fe = [None] + [f[n] - f[6 - n] for n in range(1, 3)]
    for m in range(1, 6):
        if m % 2 == 1:
            im[2 * m] = lin([(-sin24(2 * m * n), fo[n]) for n in range(1, 4)])
        else:
            im[2 * m] = lin([(-sin24(2 * m * n), fe[n]) for n in range(1, 3)])
    return re, im


def y_stage(x, w):
    hi, lo = split(x)
    return jnp.dot(jnp.concatenate([hi, lo, hi], axis=1), w, preferred_element_type=F32)


def z_stage(tz, x, direction):
    hi, lo = split(x)
    rhs = jnp.concatenate([hi, hi, lo], axis=0)
    p = jnp.dot(tz, rhs, preferred_element_type=F32)
    re = p[:NZ, :NY] - direction * p[NZ:, NY:]
    im = p[:NZ, NY:] + direction * p[NZ:, :NY]
    return re, im


def forward(i, own, before, after, wf_ref, tz, work, spec):
    @pl.loop(0, 8, unroll=True)
    def _(chunk):
        rows = pl.ds(pl.multiple_of(chunk * 8, 8), 8)
        r = (
            [before[i, n, rows] for n in range(8)]
            + [own[i, n, rows] for n in range(8)]
            + [after[i, n, rows] for n in range(8)]
        )
        re, im = real_dft24(r)
        for k in range(KX):
            work[k, rows, :NY] = re[k]
            work[k, rows, NY:] = im[k] if im[k] is not None else jnp.zeros_like(re[k])

    y = y_stage(work[...].reshape(KX * NZ, 2 * NY), wf_ref[...])
    work[...] = y.reshape(KX, NZ, 2 * NY)
    for k in range(KX):
        re, im = z_stage(tz, work[k], -1.0)
        spec[i, k, :, :NY] = re
        spec[i, k, :, NY:] = im


def contract(slot, group, q, spec, source, target):
    @pl.loop(0, 8, unroll=2)
    def _(chunk):
        start = pl.multiple_of(chunk * 8, 8)
        rows = pl.ds(start, 8)
        low = pl.ds(start + NZ, 8)
        for k in range(KX):
            p, lane = k // 2, (k % 2) * NY
            re = None if source is None else source[k, rows, :NY]
            im = None if source is None else source[k, rows, NY:]
            for t in group:
                gr, gi = spec[t, k, rows, :NY], spec[t, k, rows, NY:]
                qr = q[slot, t, p, rows, lane : lane + NY]
                qi = q[slot, t, p, low, lane : lane + NY]
                tr = gr * qr - gi * qi
                ti = gr * qi + gi * qr
                re = tr if re is None else re + tr
                im = ti if im is None else im + ti
            target[k, rows, :NY] = re
            target[k, rows, NY:] = im


def boltzmann(slot, wi_ref, tz, work, total_ref, sum_ref):
    for k in range(KX):
        re, im = z_stage(tz, work[k], 1.0)
        work[k, :, :NY] = re
        work[k, :, NY:] = im
    y = y_stage(work[...].reshape(KX * NZ, 2 * NY), wi_ref[...])
    work[...] = y.reshape(KX, NZ, 2 * NY)
    sum_ref[slot] = jnp.zeros((8, NY), F32)
    scale = 1.0 / (EXT * NZ * NY)

    @pl.loop(0, 8, unroll=4)
    def _(chunk):
        rows = pl.ds(pl.multiple_of(chunk * 8, 8), 8)
        fr = [work[k, rows, :NY] for k in range(KX)]
        fi = [work[k, rows, NY:] for k in range(KX)]
        acc = sum_ref[slot]
        for m in range(5):
            even, odd = [], []
            for k in range(KX):
                w = scale * (1.0 if k in (0, 12) else 2.0) * (-1) ** k
                even.append((w * cos24(k * m), fr[k]))
                odd.append((w * sin24(k * m), fi[k]))
            even, odd = sum_terms(even), sum_terms(odd)
            for x, e in ((4, even),) if m == 0 else ((4 + m, even - odd), (4 - m, even + odd)):
                if x < 8:
                    b = jnp.exp(-ENERGY_CAP * jnp.tanh(e / ENERGY_CAP))
                    total_ref[slot, x, rows] = b
                    acc = acc + b
        sum_ref[slot] = acc


def energy_kernel(
    slabs,
    probes,
    cells,
    ids,
    rots,
    offs,
    weights,
    turns,
    receptor,
    library,
    te_hbm,
    to_hbm,
    swap_ref,
    lane_ref,
    zstep_ref,
    tz_ref,
    wf_ref,
    wi_ref,
    out_ref,
    lib,
    te,
    to,
    own,
    before,
    after,
    xa,
    xb,
    kd,
    even,
    odd,
    tzs,
    ph,
    q,
    spec,
    work,
    joint,
    total,
    sums,
    mine,
    gathered,
    faces,
    mixed,
    blocks,
    send,
    recv,
    hand_send,
    hand_recv,
    near,
    part_send,
    part_recv,
    face_send,
    face_recv,
    block_send,
    block_recv,
):
    terms, planes = receptor.shape[0], receptor.shape[1]
    half = terms // 2
    slots = total.shape[0]
    rows = out_ref.shape[1]
    slab = lax.axis_index("slab")
    probe = lax.axis_index("probe")
    core = lax.rem(probe, 2)
    right = {"slab": lax.rem(slab + 1, slabs)}
    left = {"slab": lax.rem(slab + slabs - 1, slabs)}
    sibling = probe + 1 - 2 * core
    partner = lax.rem(probe + 2, probes)
    other = {"probe": sibling}

    barrier = pltpu.get_barrier_semaphore()

    @pl.loop(1, slabs)
    def _(d):
        pl.semaphore_signal(barrier, inc=1, device_id={"slab": lax.rem(slab + d, slabs)}, device_id_type=MESH)

    for device in (sibling, partner):
        pl.semaphore_signal(barrier, inc=1, device_id={"probe": device}, device_id_type=MESH)
    nearby = [
        pltpu.make_async_copy(library, lib, near.at[0]),
        pltpu.make_async_copy(te_hbm, te, near.at[1]),
        pltpu.make_async_copy(to_hbm, to, near.at[2]),
        pltpu.make_async_copy(receptor.at[pl.ds(core * half, half)], own.at[pl.ds(0, half)], near.at[3]),
        pltpu.make_async_copy(receptor.at[pl.ds((1 - core) * half, half)], own.at[pl.ds(half, half)], near.at[4]),
    ]

    def halo_copy(j, side):
        return pltpu.make_async_remote_copy(
            src_ref=receptor.at[core * half + j],
            dst_ref=(before, after)[side].at[j],
            send_sem=send.at[side, j],
            recv_sem=recv.at[side, j],
            device_id=(right, left)[side],
            device_id_type=MESH,
        )

    def hand_copy(j, side):
        ref = (before, after)[side]
        return pltpu.make_async_remote_copy(
            src_ref=ref.at[j],
            dst_ref=ref.at[half + j],
            send_sem=hand_send.at[side, j],
            recv_sem=hand_recv.at[side, j],
            device_id=other,
            device_id_type=MESH,
        )

    def hand_over(j):
        for side in range(2):
            halo_copy(j, side).wait_recv()
            hand_copy(j, side).start()

    for copy in nearby:
        copy.start()
    xa[...] = jnp.zeros_like(xa)
    kd[...] = jnp.zeros_like(kd)
    pl.semaphore_wait(barrier, slabs - 1 + 2)

    def send_off(j):
        for side in range(2):
            halo_copy(j, side).start()

    send_off(0)
    nearby[0].wait()
    early = slots - 1

    @pl.loop(0, 2)
    def _(part):
        turned_probes(
            part * early, early + part * (slots - early),
            ids, rots, offs, turns, core, lib, swap_ref, lane_ref, zstep_ref, xa, xb, kd, even, odd, tzs, ph,
        )

        @pl.when(part == 0)
        def _():
            send_off(1)

    for copy in nearby[1:]:
        copy.wait()
    hand_over(0)

    def pairs(low, high):
        @pl.loop(low, high)
        def _(p):
            probe_pair(p, te, to, even, odd, tzs, ph, q)

    tz = tz_ref[...]

    def products(group, first):
        @pl.loop(0, slots)
        def _(slot):
            contract(slot, group, q, spec, None if first else joint.at[slot], joint.at[slot])

    pairs(0, 3)
    send_off(2)
    pairs(3, 5)
    hand_over(1)
    pairs(5, PAIRS)
    send_off(3)

    @pl.loop(0, terms)
    def _(i):
        j, h = i // 2, i % 2

        @pl.when(h == 1)
        def _():
            for side in range(2):
                hand_copy(j, side).wait_recv()

        forward(j + half * h, own, before, after, wf_ref, tz, work, spec)

        @pl.when(i == 1)
        def _():
            hand_over(2)

        @pl.when(i == 3)
        def _():
            products((0, 1, half, half + 1), True)
            hand_over(3)

        @pl.when(i == 5)
        def _():
            products((2, half + 2), False)

    def face_copy(slot, side):
        return pltpu.make_async_remote_copy(
            src_ref=total.at[slot, (planes - 1, 0)[side]],
            dst_ref=faces.at[side, slot],
            send_sem=face_send.at[side, slot],
            recv_sem=face_recv.at[side, slot],
            device_id=(right, left)[side],
            device_id_type=MESH,
        )

    @pl.loop(0, slots)
    def _(slot):
        contract(slot, (3, half + 3), q, spec, joint.at[slot], work)
        boltzmann(slot, wi_ref, tz, work, total, sums)
        for side in range(2):
            face_copy(slot, side).start()

    parts = []
    for s in range(slots):
        v = jnp.sum(sums[s], axis=0, keepdims=True)
        parts.append(jnp.broadcast_to(jnp.sum(v, axis=1, keepdims=True), (1, NY)))
    parts += [jnp.zeros((1, NY), F32)] * (8 - slots)
    local_part = jnp.concatenate(parts, axis=0)
    mine[...] = local_part

    def part_copy(d):
        return pltpu.make_async_remote_copy(
            src_ref=mine,
            dst_ref=gathered.at[d],
            send_sem=part_send.at[d],
            recv_sem=part_recv.at[d],
            device_id={"slab": lax.rem(slab + d, slabs)},
            device_id_type=MESH,
        )

    @pl.loop(1, slabs)
    def _(d):
        part_copy(d).start()

    @pl.loop(0, slots)
    def _(slot):
        for side in range(2):
            face_copy(slot, side).wait_recv()

    @pl.loop(1, slabs)
    def _(d):
        part_copy(d).wait_recv()

    partition = local_part
    for d in range(1, slabs):
        partition = partition + gathered[d]
    share = cells / partition
    coefs = [jnp.broadcast_to(share[s : s + 1] * weights[ids[s]], (8, NY)) for s in range(slots)]

    def weighted(read):
        result = None
        for s in range(slots):
            v = read(s).reshape(NZ // 8, 8, NY) * coefs[s][None]
            result = v if result is None else result + v
        return result.reshape(NZ, NY)

    mixed[0] = weighted(lambda s: faces[0, s])
    mixed[planes + 1] = weighted(lambda s: faces[1, s])
    for x in range(planes):
        mixed[x + 1] = weighted(lambda s: total[s, x])
    for x in range(planes):
        v = (mixed[x] + 2.0 * mixed[x + 1] + mixed[x + 2]) * 0.25
        v = (pltpu.roll(v, 1, 0) + 2.0 * v + pltpu.roll(v, NZ - 1, 0)) * 0.25
        v = (pltpu.roll(v, 1, 1) + 2.0 * v + pltpu.roll(v, NY - 1, 1)) * 0.25
        mixed[x] = v

    def block(p):
        return mixed.at[pl.ds(0, planes), pl.ds(pl.multiple_of(p * rows, 8), rows)]

    away = partner + sibling - probe
    crossing = [
        pltpu.make_async_remote_copy(
            src_ref=block(p),
            dst_ref=blocks.at[i],
            send_sem=block_send.at[i],
            recv_sem=block_recv.at[i],
            device_id={"probe": device},
            device_id_type=MESH,
        )
        for i, (p, device) in enumerate(((away, sibling), (sibling, sibling)))
    ]
    last = pltpu.make_async_remote_copy(
        src_ref=blocks.at[2],
        dst_ref=blocks.at[3],
        send_sem=block_send.at[2],
        recv_sem=block_recv.at[2],
        device_id={"probe": partner},
        device_id_type=MESH,
    )
    for copy in crossing:
        copy.start()
    crossing[0].wait_recv()
    blocks[2] = block(partner)[...] + blocks[0]
    last.start()
    crossing[1].wait_recv()
    result = block(probe)[...] + blocks[1]
    last.wait_recv()
    out_ref[...] = (result + blocks[3]) * (1.0 / weights.shape[0])

    @pl.loop(0, half)
    def _(j):
        for side in range(2):
            halo_copy(j, side).wait_send()
            hand_copy(j, side).wait_send()

    @pl.loop(0, slots)
    def _(slot):
        for side in range(2):
            face_copy(slot, side).wait_send()

    @pl.loop(1, slabs)
    def _(d):
        part_copy(d).wait_send()

    for copy in (*crossing, last):
        copy.wait_send()


def sum_terms(terms):
    total = None
    for coef, value in terms:
        if abs(coef) < 1e-15:
            continue
        total = coef * value if total is None else total + coef * value
    return total


def local(receptor, library, probe_ids, rotations, offsets, probe_weight):
    terms, planes, nz, ny = receptor.shape
    slabs = lax.axis_size("slab")
    probes = lax.axis_size("probe")
    slots, half = probe_ids.shape[0], terms // 2
    rows = nz // probes
    cells = float(planes * slabs * nz * ny)
    te, to = xy_tables()
    smem = pl.BlockSpec(memory_space=pltpu.SMEM)
    vmem = pl.BlockSpec(memory_space=pltpu.VMEM)
    hbm = pl.BlockSpec(memory_space=pl.ANY)
    dma = pltpu.SemaphoreType.DMA
    return pl.pallas_call(
        functools.partial(energy_kernel, slabs, probes, cells),
        in_specs=[smem] * 5 + [hbm] * 4 + [vmem] * 6,
        out_specs=vmem,
        out_shape=jax.ShapeDtypeStruct((planes, rows, ny), F32),
        scratch_shapes=[
            pltpu.VMEM(library.shape, F32),
            pltpu.VMEM(te.shape, BF),
            pltpu.VMEM(to.shape, BF),
            pltpu.VMEM(receptor.shape, F32),
            pltpu.VMEM(receptor.shape, F32),
            pltpu.VMEM(receptor.shape, F32),
            pltpu.VMEM((KS, terms, CUBE), F32),
            pltpu.VMEM((KS, terms, CUBE), F32),
            pltpu.VMEM((CUBE // 128, terms * AZ, 128), F32),
            pltpu.VMEM((slots * terms * AZ, PACK), BF),
            pltpu.VMEM((slots * terms * AZ, PACK), BF),
            pltpu.VMEM((slots, 2 * NZ, 6 * AZ), BF),
            pltpu.VMEM((slots, 2, 8, 2 * NY), F32),
            pltpu.VMEM((slots, terms, PAIRS, 2 * NZ, 2 * NY), F32),
            pltpu.VMEM((terms, KX, nz, 2 * ny), F32),
            pltpu.VMEM((KX, nz, 2 * ny), F32),
            pltpu.VMEM((slots, KX, nz, 2 * ny), F32),
            pltpu.VMEM((slots, planes, nz, ny), F32),
            pltpu.VMEM((slots, 8, ny), F32),
            pltpu.VMEM((8, ny), F32),
            pltpu.VMEM((slabs, 8, ny), F32),
            pltpu.VMEM((2, slots, nz, ny), F32),
            pltpu.VMEM((planes + 2, nz, ny), F32),
            pltpu.VMEM((4, planes, rows, ny), F32),
            dma((2, half)),
            dma((2, half)),
            dma((2, half)),
            dma((2, half)),
            dma((5,)),
            dma((slabs,)),
            dma((slabs,)),
            dma((2, slots)),
            dma((2, slots)),
            dma((3,)),
            dma((3,)),
        ],
        compiler_params=pltpu.CompilerParams(
            collective_id=0, has_side_effects=True, vmem_limit_bytes=63 << 20
        ),
        name="consensus_density",
    )(
        probe_ids,
        rotations.reshape(-1),
        offsets.reshape(-1),
        probe_weight,
        jnp.asarray(rotation_table()),
        receptor,
        library,
        jnp.asarray(te),
        jnp.asarray(to),
        jnp.asarray(swap_table()),
        jnp.asarray(lane_offsets()),
        jnp.asarray(probe_z_steps()),
        jnp.asarray(grid_z_table()),
        jnp.asarray(grid_y_table(-1.0)),
        jnp.asarray(grid_y_table(1.0)),
    )


def solution(mesh):
    in_specs = (
        P(None, "slab", None, None),
        P(),
        P("probe"),
        P("probe", None),
        P("probe", None, None),
        P(),
    )
    out_specs = P("slab", "probe", None)
    return jax.shard_map(local, mesh=mesh, in_specs=in_specs, out_specs=out_specs, check_vma=False)
```

```python
import functools
import math

import jax
import jax.numpy as jnp
import ml_dtypes
import numpy as np
from jax import lax
from jax.experimental import pallas as pl
from jax.experimental.pallas import tpu as pltpu
from jax.sharding import PartitionSpec as P

RAD = 8
KS = 17
AZ = 24
EXT = 24
KX = 13
PAIRS = 7
NZ = 64
NY = 128
ENERGY_CAP = 6.0
HIGHEST = lax.Precision.HIGHEST
MESH = pl.DeviceIdType.MESH
BF = jnp.bfloat16
F32 = jnp.float32


def cube_rotations():
    permutes = [(0, 1, 2), (0, 2, 1), (1, 0, 2), (1, 2, 0), (2, 0, 1), (2, 1, 0)]
    parities = [1, -1, -1, 1, 1, -1]
    perms, signs = [], []
    for permute, parity in zip(permutes, parities):
        for sign_x in (1, -1):
            for sign_y in (1, -1):
                for sign_z in (1, -1):
                    if parity * sign_x * sign_y * sign_z == 1:
                        perms.append(permute)
                        signs.append((sign_x, sign_y, sign_z))
    return np.array(perms, np.int32), np.array(signs, np.int32)


def split_np(table):
    table = table.astype(np.float32)
    hi = table.astype(ml_dtypes.bfloat16)
    lo = (table - hi.astype(np.float32)).astype(ml_dtypes.bfloat16)
    return hi, lo


HALF = (KS * KS + 1) // 2
CUBE = 384
PACK = 512


def half_offsets():
    flat = np.arange(HALF) + HALF - 1
    return flat // KS - RAD, flat % KS - RAD


def xy_tables():
    ax, ay = half_offsets()
    kx = np.arange(2 * PAIRS)
    ky = np.arange(NY)
    px = (ax[:, None] * kx[None, :]) % EXT / EXT
    py = (ay[:, None] * ky[None, :]) % NY / NY
    ang = 2 * np.pi * (px[:, :, None] + py[:, None, :])
    live = (kx < KX).astype(np.float64)[None, :, None]
    out = []
    for t in (np.cos(ang) * live, np.sin(ang) * live):
        hi, lo = split_np(t.reshape(HALF, -1))
        pad = np.zeros((PACK - 3 * HALF, hi.shape[1]), hi.dtype)
        out.append(np.concatenate([hi, hi, lo, pad], axis=0))
    return out


def lane_offsets():
    ax, ay = half_offsets()
    rows = np.full((8, CUBE), 10000, np.int32)
    rows[2:] = 0
    for c in range(2):
        lanes = slice(c * HALF, (c + 1) * HALF)
        rows[0, lanes] = ax
        rows[1, lanes] = ay
        rows[2, c * HALF] = 10000
        rows[3, lanes] = 1 - 2 * c
    return rows


def swap_table():
    t = np.zeros((CUBE, CUBE), np.float32)
    for m in range(KS):
        for n in range(KS):
            t[n * KS + m, m * KS + n] = 1
    return t.astype(ml_dtypes.bfloat16)


def rotation_table():
    perms, signs = cube_rotations()
    table = np.zeros((24, 4), np.int32)
    for q in range(24):
        zaxis = [i for i in range(3) if perms[q, i] == 2][0]
        others = [i for i in range(3) if i != zaxis]
        table[q, 0] = zaxis
        table[q, 1] = 1 if signs[q, zaxis] < 0 else 0
        for i, unit in zip(others, (KS, 1)):
            table[q, 2 + perms[q, i]] = unit * signs[q, i]
    return table


def probe_z_steps():
    kz = np.arange(2 * NZ) % NZ
    lane = np.arange(6 * AZ) % (2 * AZ)
    az = lane % AZ
    quarter = np.where((np.arange(2 * NZ) < NZ)[:, None], np.where(lane < AZ, 0, 16), np.where(lane < AZ, -16, 0))
    turn = (kz[:, None] * (az - RAD)[None, :] + quarter) % NZ
    live = np.broadcast_to((az < KS).astype(np.int64)[None], turn.shape)
    return np.stack([turn, np.broadcast_to(kz[:, None], turn.shape), live]).astype(np.int32)


def grid_z_table():
    k = np.arange(NZ)
    ang = 2 * np.pi * ((k[:, None] * k[None, :]) % NZ) / NZ
    t = np.concatenate([np.cos(ang), np.sin(ang)], axis=0)
    hi, lo = split_np(t)
    return np.concatenate([hi, lo, hi], axis=1)


def grid_y_table(direction):
    k = np.arange(NY)
    ang = 2 * np.pi * ((k[:, None] * k[None, :]) % NY) / NY
    c, s = np.cos(ang), direction * np.sin(ang)
    hi, lo = split_np(np.block([[c, s], [-s, c]]))
    return np.concatenate([hi, hi, lo], axis=0)


def split(x):
    hi = x.astype(BF)
    lo = (x - hi.astype(F32)).astype(BF)
    return hi, lo


def turned_probes(first, last, ids, rots, offs, turns, core, lib_ref, swap_ref, lane_ref, zstep_ref, xa, xb, kd, even, odd, tzs, ph):
    terms = lib_ref.shape[1]
    lane = lax.broadcasted_iota(jnp.int32, (terms, CUBE), 1)
    source = lax.broadcasted_iota(jnp.int32, (CUBE, CUBE), 0)
    zlane = lax.broadcasted_iota(jnp.int32, (2 * NZ, 6 * AZ), 1)
    ky = lax.broadcasted_iota(jnp.int32, (8, 2 * NY), 1) % NY

    def permuted(x, table):
        hi, lo = split(x)
        out = jnp.dot(jnp.concatenate([hi, lo], axis=0), table, preferred_element_type=F32)
        return out[: x.shape[0]] + out[x.shape[0] :]

    @pl.loop(first, last)
    def _(slot):
        rot = rots[slot]
        zaxis, flipped = turns[rot, 0], turns[rot, 1]
        step_x, step_y = turns[rot, 2], turns[rot, 3]
        off_y, off_z = offs[2 * slot], offs[2 * slot + 1]

        turn = (zstep_ref[0] - zstep_ref[1] * off_z + NZ * NZ) & (NZ - 1)
        t = jnp.cos(turn.astype(F32) * (2 * math.pi / NZ)) * zstep_ref[2].astype(F32)
        hi, lo = split(t)
        tzs[slot] = jnp.where((zlane >= 2 * AZ) & (zlane < 4 * AZ), lo.astype(F32), hi.astype(F32)).astype(BF)
        turn = ky * off_y
        ph[slot, 0] = jnp.cos((turn & (NY - 1)).astype(F32) * (2 * math.pi / NY))
        ph[slot, 1] = jnp.cos(((turn - NY // 4) & (NY - 1)).astype(F32) * (2 * math.pi / NY))

        for m in range(KS):
            w = lib_ref[ids[slot], :, m * KS * KS : (m + 1) * KS * KS]
            xa[m, :, : KS * KS] = jnp.where(core == 0, w, pltpu.roll(w, terms // 2, 0))
        x = xa[...]
        swapped = permuted(x.reshape(KS * terms, CUBE), swap_ref[...]).reshape(KS, terms, CUBE)
        xa[...] = jnp.where(zaxis == 2, swapped, x)
        for m in range(KS):
            acc = jnp.concatenate(
                [xa[n, :, m * KS : (m + 1) * KS] for n in range(KS)] + [jnp.zeros((terms, CUBE - KS * KS), F32)],
                axis=1,
            )
            xb[m] = jnp.where(zaxis == 0, xa[m], acc)

        here = lane_ref[0:1] * step_x + lane_ref[1:2] * step_y + (HALF - 1)
        there = 2 * (HALF - 1) - here + lane_ref[2:3]
        plus = (source == here).astype(F32)
        minus = jnp.where(source == there, lane_ref[3:4], 0).astype(F32)
        turned = permuted(xb[...].reshape(KS * terms, CUBE), (plus + minus).astype(BF))
        for m in range(KS):
            f = KS - 1 - m
            row = jnp.where(flipped == 1, turned[f * terms : (f + 1) * terms], turned[m * terms : (m + 1) * terms])
            for j in range(CUBE // 128):
                kd[j, pl.ds(m, terms, stride=AZ), :] = row[:, j * 128 : (j + 1) * 128]
        rows = pl.ds(pl.multiple_of(slot * terms * AZ, terms * AZ), terms * AZ)
        both = jnp.concatenate([kd[j] for j in range(CUBE // 128)], axis=1)
        hi, lo = split(both)
        hi, lo = hi.astype(F32), lo.astype(F32)
        spare = jnp.zeros((terms * AZ, PACK - 3 * HALF), F32)
        for ref, lanes in ((even, slice(0, HALF)), (odd, slice(HALF, 2 * HALF))):
            ref[rows, :] = jnp.concatenate([hi[:, lanes], lo[:, lanes], hi[:, lanes], spare], axis=1).astype(BF)


def probe_pair(p, te, to, even, odd, tzs, ph, q):
    slots, terms = q.shape[0], q.shape[1]
    columns = pl.ds(pl.multiple_of(p * 2 * NY, 2 * NY), 2 * NY)
    re_all = jnp.dot(even[...], te[:, columns], preferred_element_type=F32)
    im_all = jnp.dot(odd[...], to[:, columns], preferred_element_type=F32)
    for s in range(slots):
        c, n = ph[s, 0, 0:1], ph[s, 1, 0:1]
        rows = slice(s * terms * AZ, (s + 1) * terms * AZ)
        re = re_all[rows] * c + im_all[rows] * n
        im = im_all[rows] * c - re_all[rows] * n
        tz = tzs[s]
        for t in range(terms):
            d = jnp.concatenate([re[t * AZ : (t + 1) * AZ], im[t * AZ : (t + 1) * AZ]], axis=0)
            hi, lo = split(d)
            q[s, t, p] = jnp.dot(tz, jnp.concatenate([hi, hi, lo], axis=0), preferred_element_type=F32)


def cos24(m):
    return math.cos(2 * math.pi * (m % 24) / 24)


def sin24(m):
    return math.sin(2 * math.pi * (m % 24) / 24)


def lin(terms):
    total = None
    for coef, value in terms:
        if abs(coef) < 1e-12:
            continue
        if abs(coef - 1) < 1e-12:
            total = value if total is None else total + value
        elif abs(coef + 1) < 1e-12:
            total = -value if total is None else total - value
        else:
            total = coef * value if total is None else total + coef * value
    return total


def real_dft24(r):
    a = [r[0]] + [r[n] + r[24 - n] for n in range(1, 12)] + [r[12]]
    b = [None] + [r[n] - r[24 - n] for n in range(1, 12)]
    re, im = [None] * 13, [None] * 13
    c = [a[n] + a[12 - n] for n in range(6)] + [a[6]]
    d = [a[n] - a[12 - n] for n in range(6)]
    ce = [c[n] + c[6 - n] for n in range(3)] + [c[3]]
    co = [c[n] - c[6 - n] for n in range(3)]
    for m in range(7):
        if m % 2 == 0:
            re[2 * m] = lin([(cos24(2 * m * n), ce[n]) for n in range(4)])
        else:
            re[2 * m] = lin([(cos24(2 * m * n), co[n]) for n in range(3)])
    for k in range(1, 12, 2):
        re[k] = lin([(cos24(k * n), d[n]) for n in range(6)])
    e = [None] + [b[n] + b[12 - n] for n in range(1, 6)] + [b[6]]
    f = [None] + [b[n] - b[12 - n] for n in range(1, 6)]
    for k in range(1, 12, 2):
        im[k] = lin([(-sin24(k * n), e[n]) for n in range(1, 7)])
    fo = [None] + [f[n] + f[6 - n] for n in range(1, 3)] + [f[3]]
    fe = [None] + [f[n] - f[6 - n] for n in range(1, 3)]
    for m in range(1, 6):
        if m % 2 == 1:
            im[2 * m] = lin([(-sin24(2 * m * n), fo[n]) for n in range(1, 4)])
        else:
            im[2 * m] = lin([(-sin24(2 * m * n), fe[n]) for n in range(1, 3)])
    return re, im


def y_stage(x, w):
    hi, lo = split(x)
    return jnp.dot(jnp.concatenate([hi, lo, hi], axis=1), w, preferred_element_type=F32)


def z_stage(tz, x, direction):
    hi, lo = split(x)
    rhs = jnp.concatenate([hi, hi, lo], axis=0)
    p = jnp.dot(tz, rhs, preferred_element_type=F32)
    re = p[:NZ, :NY] - direction * p[NZ:, NY:]
    im = p[:NZ, NY:] + direction * p[NZ:, :NY]
    return re, im


def forward(i, own, before, after, wf_ref, tz, work, spec):
    @pl.loop(0, 8, unroll=True)
    def _(chunk):
        rows = pl.ds(pl.multiple_of(chunk * 8, 8), 8)
        r = (
            [before[i, n, rows] for n in range(8)]
            + [own[i, n, rows] for n in range(8)]
            + [after[i, n, rows] for n in range(8)]
        )
        re, im = real_dft24(r)
        for k in range(KX):
            work[k, rows, :NY] = re[k]
            work[k, rows, NY:] = im[k] if im[k] is not None else jnp.zeros_like(re[k])

    y = y_stage(work[...].reshape(KX * NZ, 2 * NY), wf_ref[...])
    work[...] = y.reshape(KX, NZ, 2 * NY)
    for k in range(KX):
        re, im = z_stage(tz, work[k], -1.0)
        spec[i, k, :, :NY] = re
        spec[i, k, :, NY:] = im


def contract(slot, group, q, spec, source, target):
    @pl.loop(0, 8, unroll=2)
    def _(chunk):
        start = pl.multiple_of(chunk * 8, 8)
        rows = pl.ds(start, 8)
        low = pl.ds(start + NZ, 8)
        for k in range(KX):
            p, lane = k // 2, (k % 2) * NY
            re = None if source is None else source[k, rows, :NY]
            im = None if source is None else source[k, rows, NY:]
            for t in group:
                gr, gi = spec[t, k, rows, :NY], spec[t, k, rows, NY:]
                qr = q[slot, t, p, rows, lane : lane + NY]
                qi = q[slot, t, p, low, lane : lane + NY]
                tr = gr * qr - gi * qi
                ti = gr * qi + gi * qr
                re = tr if re is None else re + tr
                im = ti if im is None else im + ti
            target[k, rows, :NY] = re
            target[k, rows, NY:] = im


def boltzmann(slot, wi_ref, tz, work, total_ref, sum_ref):
    for k in range(KX):
        re, im = z_stage(tz, work[k], 1.0)
        work[k, :, :NY] = re
        work[k, :, NY:] = im
    y = y_stage(work[...].reshape(KX * NZ, 2 * NY), wi_ref[...])
    work[...] = y.reshape(KX, NZ, 2 * NY)
    sum_ref[slot] = jnp.zeros((8, NY), F32)
    scale = 1.0 / (EXT * NZ * NY)

    @pl.loop(0, 8, unroll=4)
    def _(chunk):
        rows = pl.ds(pl.multiple_of(chunk * 8, 8), 8)
        fr = [work[k, rows, :NY] for k in range(KX)]
        fi = [work[k, rows, NY:] for k in range(KX)]
        acc = sum_ref[slot]
        for m in range(5):
            even, odd = [], []
            for k in range(KX):
                w = scale * (1.0 if k in (0, 12) else 2.0) * (-1) ** k
                even.append((w * cos24(k * m), fr[k]))
                odd.append((w * sin24(k * m), fi[k]))
            even, odd = sum_terms(even), sum_terms(odd)
            for x, e in ((4, even),) if m == 0 else ((4 + m, even - odd), (4 - m, even + odd)):
                if x < 8:
                    b = jnp.exp(-ENERGY_CAP * jnp.tanh(e / ENERGY_CAP))
                    total_ref[slot, x, rows] = b
                    acc = acc + b
        sum_ref[slot] = acc


def energy_kernel(
    slabs,
    probes,
    cells,
    ids,
    rots,
    offs,
    weights,
    turns,
    receptor,
    library,
    te_hbm,
    to_hbm,
    swap_ref,
    lane_ref,
    zstep_ref,
    tz_ref,
    wf_ref,
    wi_ref,
    out_ref,
    lib,
    te,
    to,
    own,
    before,
    after,
    xa,
    xb,
    kd,
    even,
    odd,
    tzs,
    ph,
    q,
    spec,
    work,
    joint,
    total,
    sums,
    mine,
    gathered,
    faces,
    mixed,
    blocks,
    send,
    recv,
    hand_send,
    hand_recv,
    near,
    part_send,
    part_recv,
    face_send,
    face_recv,
    block_send,
    block_recv,
):
    terms, planes = receptor.shape[0], receptor.shape[1]
    half = terms // 2
    slots = total.shape[0]
    rows = out_ref.shape[1]
    slab = lax.axis_index("slab")
    probe = lax.axis_index("probe")
    core = lax.rem(probe, 2)
    right = {"slab": lax.rem(slab + 1, slabs)}
    left = {"slab": lax.rem(slab + slabs - 1, slabs)}
    sibling = probe + 1 - 2 * core
    partner = lax.rem(probe + 2, probes)
    other = {"probe": sibling}

    barrier = pltpu.get_barrier_semaphore()

    @pl.loop(1, slabs)
    def _(d):
        pl.semaphore_signal(barrier, inc=1, device_id={"slab": lax.rem(slab + d, slabs)}, device_id_type=MESH)

    for device in (sibling, partner):
        pl.semaphore_signal(barrier, inc=1, device_id={"probe": device}, device_id_type=MESH)
    nearby = [
        pltpu.make_async_copy(library, lib, near.at[0]),
        pltpu.make_async_copy(te_hbm, te, near.at[1]),
        pltpu.make_async_copy(to_hbm, to, near.at[2]),
        pltpu.make_async_copy(receptor.at[pl.ds(core * half, half)], own.at[pl.ds(0, half)], near.at[3]),
        pltpu.make_async_copy(receptor.at[pl.ds((1 - core) * half, half)], own.at[pl.ds(half, half)], near.at[4]),
    ]

    def halo_copy(j, side):
        return pltpu.make_async_remote_copy(
            src_ref=receptor.at[core * half + j],
            dst_ref=(before, after)[side].at[j],
            send_sem=send.at[side, j],
            recv_sem=recv.at[side, j],
            device_id=(right, left)[side],
            device_id_type=MESH,
        )

    def hand_copy(j, side):
        ref = (before, after)[side]
        return pltpu.make_async_remote_copy(
            src_ref=ref.at[j],
            dst_ref=ref.at[half + j],
            send_sem=hand_send.at[side, j],
            recv_sem=hand_recv.at[side, j],
            device_id=other,
            device_id_type=MESH,
        )

    def hand_over(j):
        for side in range(2):
            halo_copy(j, side).wait_recv()
            hand_copy(j, side).start()

    for copy in nearby:
        copy.start()
    xa[...] = jnp.zeros_like(xa)
    kd[...] = jnp.zeros_like(kd)
    pl.semaphore_wait(barrier, slabs - 1 + 2)

    def send_off(j):
        for side in range(2):
            halo_copy(j, side).start()

    send_off(0)
    nearby[0].wait()
    early = slots - 1

    @pl.loop(0, 2)
    def _(part):
        turned_probes(
            part * early, early + part * (slots - early),
            ids, rots, offs, turns, core, lib, swap_ref, lane_ref, zstep_ref, xa, xb, kd, even, odd, tzs, ph,
        )

        @pl.when(part == 0)
        def _():
            send_off(1)

    for copy in nearby[1:]:
        copy.wait()
    hand_over(0)

    def pairs(low, high):
        @pl.loop(low, high)
        def _(p):
            probe_pair(p, te, to, even, odd, tzs, ph, q)

    tz = tz_ref[...]

    def products(group, first):
        @pl.loop(0, slots)
        def _(slot):
            contract(slot, group, q, spec, None if first else joint.at[slot], joint.at[slot])

    pairs(0, 3)
    send_off(2)
    pairs(3, 5)
    hand_over(1)
    pairs(5, PAIRS)
    send_off(3)

    @pl.loop(0, terms)
    def _(i):
        j, h = i // 2, i % 2

        @pl.when(h == 1)
        def _():
            for side in range(2):
                hand_copy(j, side).wait_recv()

        forward(j + half * h, own, before, after, wf_ref, tz, work, spec)

        @pl.when(i == 1)
        def _():
            hand_over(2)

        @pl.when(i == 3)
        def _():
            products((0, 1, half, half + 1), True)
            hand_over(3)

        @pl.when(i == 5)
        def _():
            products((2, half + 2), False)

    def face_copy(slot, side):
        return pltpu.make_async_remote_copy(
            src_ref=total.at[slot, (planes - 1, 0)[side]],
            dst_ref=faces.at[side, slot],
            send_sem=face_send.at[side, slot],
            recv_sem=face_recv.at[side, slot],
            device_id=(right, left)[side],
            device_id_type=MESH,
        )

    @pl.loop(0, slots)
    def _(slot):
        contract(slot, (3, half + 3), q, spec, joint.at[slot], work)
        boltzmann(slot, wi_ref, tz, work, total, sums)
        for side in range(2):
            face_copy(slot, side).start()

    parts = []
    for s in range(slots):
        v = jnp.sum(sums[s], axis=0, keepdims=True)
        parts.append(jnp.broadcast_to(jnp.sum(v, axis=1, keepdims=True), (1, NY)))
    parts += [jnp.zeros((1, NY), F32)] * (8 - slots)
    local_part = jnp.concatenate(parts, axis=0)
    mine[...] = local_part

    def part_copy(d):
        return pltpu.make_async_remote_copy(
            src_ref=mine,
            dst_ref=gathered.at[d],
            send_sem=part_send,
            recv_sem=part_recv,
            device_id={"slab": lax.rem(slab + d, slabs)},
            device_id_type=MESH,
        )

    @pl.loop(1, slabs)
    def _(d):
        part_copy(d).start()

    @pl.loop(0, slots)
    def _(slot):
        for side in range(2):
            face_copy(slot, side).wait_recv()

    others = gathered.at[pl.ds(1, slabs - 1)]
    pltpu.make_async_copy(others, others, part_recv).wait()

    partition = local_part
    for d in range(1, slabs):
        partition = partition + gathered[d]
    share = cells / partition
    coefs = [jnp.broadcast_to(share[s : s + 1] * weights[ids[s]], (8, NY)) for s in range(slots)]

    def weighted(read):
        result = None
        for s in range(slots):
            v = read(s).reshape(NZ // 8, 8, NY) * coefs[s][None]
            result = v if result is None else result + v
        return result.reshape(NZ, NY)

    mixed[0] = weighted(lambda s: faces[0, s])
    mixed[planes + 1] = weighted(lambda s: faces[1, s])
    for x in range(planes):
        mixed[x + 1] = weighted(lambda s: total[s, x])
    for x in range(planes):
        v = (mixed[x] + 2.0 * mixed[x + 1] + mixed[x + 2]) * 0.25
        v = (pltpu.roll(v, 1, 0) + 2.0 * v + pltpu.roll(v, NZ - 1, 0)) * 0.25
        v = (pltpu.roll(v, 1, 1) + 2.0 * v + pltpu.roll(v, NY - 1, 1)) * 0.25
        mixed[x] = v

    def block(p):
        return mixed.at[pl.ds(0, planes), pl.ds(pl.multiple_of(p * rows, 8), rows)]

    away = partner + sibling - probe
    crossing = [
        pltpu.make_async_remote_copy(
            src_ref=block(p),
            dst_ref=blocks.at[i],
            send_sem=block_send.at[i],
            recv_sem=block_recv.at[i],
            device_id={"probe": device},
            device_id_type=MESH,
        )
        for i, (p, device) in enumerate(((away, sibling), (sibling, sibling)))
    ]
    last = pltpu.make_async_remote_copy(
        src_ref=blocks.at[2],
        dst_ref=blocks.at[3],
        send_sem=block_send.at[2],
        recv_sem=block_recv.at[2],
        device_id={"probe": partner},
        device_id_type=MESH,
    )
    for copy in crossing:
        copy.start()
    crossing[0].wait_recv()
    blocks[2] = block(partner)[...] + blocks[0]
    last.start()
    crossing[1].wait_recv()
    result = block(probe)[...] + blocks[1]
    last.wait_recv()
    out_ref[...] = (result + blocks[3]) * (1.0 / weights.shape[0])

    @pl.loop(0, half)
    def _(j):
        for side in range(2):
            halo_copy(j, side).wait_send()
            hand_copy(j, side).wait_send()

    @pl.loop(0, slots)
    def _(slot):
        for side in range(2):
            face_copy(slot, side).wait_send()

    pltpu.make_async_copy(others, others, part_send).wait()

    for copy in (*crossing, last):
        copy.wait_send()


def sum_terms(terms):
    total = None
    for coef, value in terms:
        if abs(coef) < 1e-15:
            continue
        total = coef * value if total is None else total + coef * value
    return total


def local(receptor, library, probe_ids, rotations, offsets, probe_weight):
    terms, planes, nz, ny = receptor.shape
    slabs = lax.axis_size("slab")
    probes = lax.axis_size("probe")
    slots, half = probe_ids.shape[0], terms // 2
    rows = nz // probes
    cells = float(planes * slabs * nz * ny)
    te, to = xy_tables()
    smem = pl.BlockSpec(memory_space=pltpu.SMEM)
    vmem = pl.BlockSpec(memory_space=pltpu.VMEM)
    hbm = pl.BlockSpec(memory_space=pl.ANY)
    dma = pltpu.SemaphoreType.DMA
    return pl.pallas_call(
        functools.partial(energy_kernel, slabs, probes, cells),
        in_specs=[smem] * 5 + [hbm] * 4 + [vmem] * 6,
        out_specs=vmem,
        out_shape=jax.ShapeDtypeStruct((planes, rows, ny), F32),
        scratch_shapes=[
            pltpu.VMEM(library.shape, F32),
            pltpu.VMEM(te.shape, BF),
            pltpu.VMEM(to.shape, BF),
            pltpu.VMEM(receptor.shape, F32),
            pltpu.VMEM(receptor.shape, F32),
            pltpu.VMEM(receptor.shape, F32),
            pltpu.VMEM((KS, terms, CUBE), F32),
            pltpu.VMEM((KS, terms, CUBE), F32),
            pltpu.VMEM((CUBE // 128, terms * AZ, 128), F32),
            pltpu.VMEM((slots * terms * AZ, PACK), BF),
            pltpu.VMEM((slots * terms * AZ, PACK), BF),
            pltpu.VMEM((slots, 2 * NZ, 6 * AZ), BF),
            pltpu.VMEM((slots, 2, 8, 2 * NY), F32),
            pltpu.VMEM((slots, terms, PAIRS, 2 * NZ, 2 * NY), F32),
            pltpu.VMEM((terms, KX, nz, 2 * ny), F32),
            pltpu.VMEM((KX, nz, 2 * ny), F32),
            pltpu.VMEM((slots, KX, nz, 2 * ny), F32),
            pltpu.VMEM((slots, planes, nz, ny), F32),
            pltpu.VMEM((slots, 8, ny), F32),
            pltpu.VMEM((8, ny), F32),
            pltpu.VMEM((slabs, 8, ny), F32),
            pltpu.VMEM((2, slots, nz, ny), F32),
            pltpu.VMEM((planes + 2, nz, ny), F32),
            pltpu.VMEM((4, planes, rows, ny), F32),
            dma((2, half)),
            dma((2, half)),
            dma((2, half)),
            dma((2, half)),
            dma((5,)),
            pltpu.SemaphoreType.DMA,
            pltpu.SemaphoreType.DMA,
            dma((2, slots)),
            dma((2, slots)),
            dma((3,)),
            dma((3,)),
        ],
        compiler_params=pltpu.CompilerParams(
            collective_id=0, has_side_effects=True, vmem_limit_bytes=63 << 20
        ),
        name="consensus_density",
    )(
        probe_ids,
        rotations.reshape(-1),
        offsets.reshape(-1),
        probe_weight,
        jnp.asarray(rotation_table()),
        receptor,
        library,
        jnp.asarray(te),
        jnp.asarray(to),
        jnp.asarray(swap_table()),
        jnp.asarray(lane_offsets()),
        jnp.asarray(probe_z_steps()),
        jnp.asarray(grid_z_table()),
        jnp.asarray(grid_y_table(-1.0)),
        jnp.asarray(grid_y_table(1.0)),
    )


def solution(mesh):
    in_specs = (
        P(None, "slab", None, None),
        P(),
        P("probe"),
        P("probe", None),
        P("probe", None, None),
        P(),
    )
    out_specs = P("slab", "probe", None)
    return jax.shard_map(local, mesh=mesh, in_specs=in_specs, out_specs=out_specs, check_vma=False)
```

```python
import functools
import math

import jax
import jax.numpy as jnp
import ml_dtypes
import numpy as np
from jax import lax
from jax.experimental import pallas as pl
from jax.experimental.pallas import tpu as pltpu
from jax.sharding import PartitionSpec as P

RAD = 8
KS = 17
AZ = 24
EXT = 24
KX = 13
PAIRS = 7
NZ = 64
NY = 128
ENERGY_CAP = 6.0
HIGHEST = lax.Precision.HIGHEST
MESH = pl.DeviceIdType.MESH
BF = jnp.bfloat16
F32 = jnp.float32


def cube_rotations():
    permutes = [(0, 1, 2), (0, 2, 1), (1, 0, 2), (1, 2, 0), (2, 0, 1), (2, 1, 0)]
    parities = [1, -1, -1, 1, 1, -1]
    perms, signs = [], []
    for permute, parity in zip(permutes, parities):
        for sign_x in (1, -1):
            for sign_y in (1, -1):
                for sign_z in (1, -1):
                    if parity * sign_x * sign_y * sign_z == 1:
                        perms.append(permute)
                        signs.append((sign_x, sign_y, sign_z))
    return np.array(perms, np.int32), np.array(signs, np.int32)


def split_np(table):
    table = table.astype(np.float32)
    hi = table.astype(ml_dtypes.bfloat16)
    lo = (table - hi.astype(np.float32)).astype(ml_dtypes.bfloat16)
    return hi, lo


HALF = (KS * KS + 1) // 2
CUBE = 384
PACK = 512


def half_offsets():
    flat = np.arange(HALF) + HALF - 1
    return flat // KS - RAD, flat % KS - RAD


def xy_tables():
    ax, ay = half_offsets()
    kx = np.arange(2 * PAIRS)
    ky = np.arange(NY)
    px = (ax[:, None] * kx[None, :]) % EXT / EXT
    py = (ay[:, None] * ky[None, :]) % NY / NY
    ang = 2 * np.pi * (px[:, :, None] + py[:, None, :])
    live = (kx < KX).astype(np.float64)[None, :, None]
    out = []
    for t in (np.cos(ang) * live, np.sin(ang) * live):
        hi, lo = split_np(t.reshape(HALF, -1))
        pad = np.zeros((PACK - 3 * HALF, hi.shape[1]), hi.dtype)
        out.append(np.concatenate([hi, hi, lo, pad], axis=0))
    return out


def lane_offsets():
    ax, ay = half_offsets()
    rows = np.full((8, CUBE), 10000, np.int32)
    rows[2:] = 0
    for c in range(2):
        lanes = slice(c * HALF, (c + 1) * HALF)
        rows[0, lanes] = ax
        rows[1, lanes] = ay
        rows[2, c * HALF] = 10000
        rows[3, lanes] = 1 - 2 * c
    return rows


def swap_table():
    t = np.zeros((CUBE, CUBE), np.float32)
    for m in range(KS):
        for n in range(KS):
            t[n * KS + m, m * KS + n] = 1
    return t.astype(ml_dtypes.bfloat16)


def rotation_table():
    perms, signs = cube_rotations()
    table = np.zeros((24, 4), np.int32)
    for q in range(24):
        zaxis = [i for i in range(3) if perms[q, i] == 2][0]
        others = [i for i in range(3) if i != zaxis]
        table[q, 0] = zaxis
        table[q, 1] = 1 if signs[q, zaxis] < 0 else 0
        for i, unit in zip(others, (KS, 1)):
            table[q, 2 + perms[q, i]] = unit * signs[q, i]
    return table


def probe_z_steps():
    kz = np.arange(2 * NZ) % NZ
    lane = np.arange(6 * AZ) % (2 * AZ)
    az = lane % AZ
    quarter = np.where((np.arange(2 * NZ) < NZ)[:, None], np.where(lane < AZ, 0, 16), np.where(lane < AZ, -16, 0))
    turn = (kz[:, None] * (az - RAD)[None, :] + quarter) % NZ
    live = np.broadcast_to((az < KS).astype(np.int64)[None], turn.shape)
    return np.stack([turn, np.broadcast_to(kz[:, None], turn.shape), live]).astype(np.int32)


def grid_z_table():
    k = np.arange(NZ)
    ang = 2 * np.pi * ((k[:, None] * k[None, :]) % NZ) / NZ
    t = np.concatenate([np.cos(ang), np.sin(ang)], axis=0)
    hi, lo = split_np(t)
    return np.concatenate([hi, lo, hi], axis=1)


def grid_y_table(direction):
    k = np.arange(NY)
    ang = 2 * np.pi * ((k[:, None] * k[None, :]) % NY) / NY
    c, s = np.cos(ang), direction * np.sin(ang)
    hi, lo = split_np(np.block([[c, s], [-s, c]]))
    return np.concatenate([hi, hi, lo], axis=0)


def split(x):
    hi = x.astype(BF)
    lo = (x - hi.astype(F32)).astype(BF)
    return hi, lo


def turned_probes(first, last, ids, rots, offs, turns, core, lib_ref, swap_ref, lane_ref, zstep_ref, xa, xb, kd, even, odd, tzs, ph):
    terms = lib_ref.shape[1]
    lane = lax.broadcasted_iota(jnp.int32, (terms, CUBE), 1)
    source = lax.broadcasted_iota(jnp.int32, (CUBE, CUBE), 0)
    zlane = lax.broadcasted_iota(jnp.int32, (2 * NZ, 6 * AZ), 1)
    ky = lax.broadcasted_iota(jnp.int32, (8, 2 * NY), 1) % NY

    def permuted(x, table):
        hi, lo = split(x)
        out = jnp.dot(jnp.concatenate([hi, lo], axis=0), table, preferred_element_type=F32)
        return out[: x.shape[0]] + out[x.shape[0] :]

    @pl.loop(first, last)
    def _(slot):
        rot = rots[slot]
        zaxis, flipped = turns[rot, 0], turns[rot, 1]
        step_x, step_y = turns[rot, 2], turns[rot, 3]
        off_y, off_z = offs[2 * slot], offs[2 * slot + 1]

        turn = (zstep_ref[0] - zstep_ref[1] * off_z + NZ * NZ) & (NZ - 1)
        t = jnp.cos(turn.astype(F32) * (2 * math.pi / NZ)) * zstep_ref[2].astype(F32)
        hi, lo = split(t)
        tzs[slot] = jnp.where((zlane >= 2 * AZ) & (zlane < 4 * AZ), lo.astype(F32), hi.astype(F32)).astype(BF)
        turn = ky * off_y
        ph[slot, 0] = jnp.cos((turn & (NY - 1)).astype(F32) * (2 * math.pi / NY))
        ph[slot, 1] = jnp.cos(((turn - NY // 4) & (NY - 1)).astype(F32) * (2 * math.pi / NY))

        for m in range(KS):
            w = lib_ref[ids[slot], :, m * KS * KS : (m + 1) * KS * KS]
            xa[m, :, : KS * KS] = jnp.where(core == 0, w, pltpu.roll(w, terms // 2, 0))
        x = xa[...]
        swapped = permuted(x.reshape(KS * terms, CUBE), swap_ref[...]).reshape(KS, terms, CUBE)
        xa[...] = jnp.where(zaxis == 2, swapped, x)
        for m in range(KS):
            acc = jnp.concatenate(
                [xa[n, :, m * KS : (m + 1) * KS] for n in range(KS)] + [jnp.zeros((terms, CUBE - KS * KS), F32)],
                axis=1,
            )
            xb[m] = jnp.where(zaxis == 0, xa[m], acc)

        here = lane_ref[0:1] * step_x + lane_ref[1:2] * step_y + (HALF - 1)
        there = 2 * (HALF - 1) - here + lane_ref[2:3]
        plus = (source == here).astype(F32)
        minus = jnp.where(source == there, lane_ref[3:4], 0).astype(F32)
        turned = permuted(xb[...].reshape(KS * terms, CUBE), (plus + minus).astype(BF))
        for m in range(KS):
            f = KS - 1 - m
            row = jnp.where(flipped == 1, turned[f * terms : (f + 1) * terms], turned[m * terms : (m + 1) * terms])
            for j in range(CUBE // 128):
                kd[j, pl.ds(m, terms, stride=AZ), :] = row[:, j * 128 : (j + 1) * 128]
        rows = pl.ds(pl.multiple_of(slot * terms * AZ, terms * AZ), terms * AZ)
        both = jnp.concatenate([kd[j] for j in range(CUBE // 128)], axis=1)
        hi, lo = split(both)
        hi, lo = hi.astype(F32), lo.astype(F32)
        spare = jnp.zeros((terms * AZ, PACK - 3 * HALF), F32)
        for ref, lanes in ((even, slice(0, HALF)), (odd, slice(HALF, 2 * HALF))):
            ref[rows, :] = jnp.concatenate([hi[:, lanes], lo[:, lanes], hi[:, lanes], spare], axis=1).astype(BF)


def probe_pair(p, te, to, even, odd, tzs, ph, q):
    slots, terms = q.shape[0], q.shape[1]
    columns = pl.ds(pl.multiple_of(p * 2 * NY, 2 * NY), 2 * NY)
    re_all = jnp.dot(even[...], te[:, columns], preferred_element_type=F32)
    im_all = jnp.dot(odd[...], to[:, columns], preferred_element_type=F32)
    for s in range(slots):
        c, n = ph[s, 0, 0:1], ph[s, 1, 0:1]
        rows = slice(s * terms * AZ, (s + 1) * terms * AZ)
        re = re_all[rows] * c + im_all[rows] * n
        im = im_all[rows] * c - re_all[rows] * n
        tz = tzs[s]
        for t in range(terms):
            d = jnp.concatenate([re[t * AZ : (t + 1) * AZ], im[t * AZ : (t + 1) * AZ]], axis=0)
            hi, lo = split(d)
            q[s, t, p] = jnp.dot(tz, jnp.concatenate([hi, hi, lo], axis=0), preferred_element_type=F32)


def cos24(m):
    return math.cos(2 * math.pi * (m % 24) / 24)


def sin24(m):
    return math.sin(2 * math.pi * (m % 24) / 24)


def lin(terms):
    total = None
    for coef, value in terms:
        if abs(coef) < 1e-12:
            continue
        if abs(coef - 1) < 1e-12:
            total = value if total is None else total + value
        elif abs(coef + 1) < 1e-12:
            total = -value if total is None else total - value
        else:
            total = coef * value if total is None else total + coef * value
    return total


def real_dft24(r):
    a = [r[0]] + [r[n] + r[24 - n] for n in range(1, 12)] + [r[12]]
    b = [None] + [r[n] - r[24 - n] for n in range(1, 12)]
    re, im = [None] * 13, [None] * 13
    c = [a[n] + a[12 - n] for n in range(6)] + [a[6]]
    d = [a[n] - a[12 - n] for n in range(6)]
    ce = [c[n] + c[6 - n] for n in range(3)] + [c[3]]
    co = [c[n] - c[6 - n] for n in range(3)]
    for m in range(7):
        if m % 2 == 0:
            re[2 * m] = lin([(cos24(2 * m * n), ce[n]) for n in range(4)])
        else:
            re[2 * m] = lin([(cos24(2 * m * n), co[n]) for n in range(3)])
    for k in range(1, 12, 2):
        re[k] = lin([(cos24(k * n), d[n]) for n in range(6)])
    e = [None] + [b[n] + b[12 - n] for n in range(1, 6)] + [b[6]]
    f = [None] + [b[n] - b[12 - n] for n in range(1, 6)]
    for k in range(1, 12, 2):
        im[k] = lin([(-sin24(k * n), e[n]) for n in range(1, 7)])
    fo = [None] + [f[n] + f[6 - n] for n in range(1, 3)] + [f[3]]
    fe = [None] + [f[n] - f[6 - n] for n in range(1, 3)]
    for m in range(1, 6):
        if m % 2 == 1:
            im[2 * m] = lin([(-sin24(2 * m * n), fo[n]) for n in range(1, 4)])
        else:
            im[2 * m] = lin([(-sin24(2 * m * n), fe[n]) for n in range(1, 3)])
    return re, im


def y_stage(x, w):
    hi, lo = split(x)
    return jnp.dot(jnp.concatenate([hi, lo, hi], axis=1), w, preferred_element_type=F32)


def z_stage(tz, x, direction):
    hi, lo = split(x)
    rhs = jnp.concatenate([hi, hi, lo], axis=0)
    p = jnp.dot(tz, rhs, preferred_element_type=F32)
    re = p[:NZ, :NY] - direction * p[NZ:, NY:]
    im = p[:NZ, NY:] + direction * p[NZ:, :NY]
    return re, im


def forward(i, own, before, after, wf_ref, tz, work, spec):
    @pl.loop(0, 8, unroll=True)
    def _(chunk):
        rows = pl.ds(pl.multiple_of(chunk * 8, 8), 8)
        r = (
            [before[i, n, rows] for n in range(8)]
            + [own[i, n, rows] for n in range(8)]
            + [after[i, n, rows] for n in range(8)]
        )
        re, im = real_dft24(r)
        for k in range(KX):
            work[k, rows, :NY] = re[k]
            work[k, rows, NY:] = im[k] if im[k] is not None else jnp.zeros_like(re[k])

    y = y_stage(work[...].reshape(KX * NZ, 2 * NY), wf_ref[...])
    work[...] = y.reshape(KX, NZ, 2 * NY)
    for k in range(KX):
        re, im = z_stage(tz, work[k], -1.0)
        spec[i, k, :, :NY] = re
        spec[i, k, :, NY:] = im


def contract(slot, group, q, spec, source, target):
    @pl.loop(0, 8, unroll=4)
    def _(chunk):
        start = pl.multiple_of(chunk * 8, 8)
        rows = pl.ds(start, 8)
        low = pl.ds(start + NZ, 8)
        for k in range(KX):
            p, lane = k // 2, (k % 2) * NY
            re = None if source is None else source[k, rows, :NY]
            im = None if source is None else source[k, rows, NY:]
            for t in group:
                gr, gi = spec[t, k, rows, :NY], spec[t, k, rows, NY:]
                qr = q[slot, t, p, rows, lane : lane + NY]
                qi = q[slot, t, p, low, lane : lane + NY]
                tr = gr * qr - gi * qi
                ti = gr * qi + gi * qr
                re = tr if re is None else re + tr
                im = ti if im is None else im + ti
            target[k, rows, :NY] = re
            target[k, rows, NY:] = im


def boltzmann(slot, wi_ref, tz, work, total_ref, sum_ref):
    for k in range(KX):
        re, im = z_stage(tz, work[k], 1.0)
        work[k, :, :NY] = re
        work[k, :, NY:] = im
    y = y_stage(work[...].reshape(KX * NZ, 2 * NY), wi_ref[...])
    work[...] = y.reshape(KX, NZ, 2 * NY)
    sum_ref[slot] = jnp.zeros((8, NY), F32)
    scale = 1.0 / (EXT * NZ * NY)

    @pl.loop(0, 8, unroll=4)
    def _(chunk):
        rows = pl.ds(pl.multiple_of(chunk * 8, 8), 8)
        fr = [work[k, rows, :NY] for k in range(KX)]
        fi = [work[k, rows, NY:] for k in range(KX)]
        acc = sum_ref[slot]
        for m in range(5):
            even, odd = [], []
            for k in range(KX):
                w = scale * (1.0 if k in (0, 12) else 2.0) * (-1) ** k
                even.append((w * cos24(k * m), fr[k]))
                odd.append((w * sin24(k * m), fi[k]))
            even, odd = sum_terms(even), sum_terms(odd)
            for x, e in ((4, even),) if m == 0 else ((4 + m, even - odd), (4 - m, even + odd)):
                if x < 8:
                    b = jnp.exp(-ENERGY_CAP * jnp.tanh(e / ENERGY_CAP))
                    total_ref[slot, x, rows] = b
                    acc = acc + b
        sum_ref[slot] = acc


def energy_kernel(
    slabs,
    probes,
    cells,
    ids,
    rots,
    offs,
    weights,
    turns,
    receptor,
    library,
    te_hbm,
    to_hbm,
    swap_ref,
    lane_ref,
    zstep_ref,
    tz_ref,
    wf_ref,
    wi_ref,
    out_ref,
    lib,
    te,
    to,
    own,
    before,
    after,
    xa,
    xb,
    kd,
    even,
    odd,
    tzs,
    ph,
    q,
    spec,
    work,
    joint,
    total,
    sums,
    mine,
    gathered,
    faces,
    mixed,
    blocks,
    send,
    recv,
    hand_send,
    hand_recv,
    near,
    part_send,
    part_recv,
    face_send,
    face_recv,
    block_send,
    block_recv,
):
    terms, planes = receptor.shape[0], receptor.shape[1]
    half = terms // 2
    slots = total.shape[0]
    rows = out_ref.shape[1]
    slab = lax.axis_index("slab")
    probe = lax.axis_index("probe")
    core = lax.rem(probe, 2)
    right = {"slab": lax.rem(slab + 1, slabs)}
    left = {"slab": lax.rem(slab + slabs - 1, slabs)}
    sibling = probe + 1 - 2 * core
    partner = lax.rem(probe + 2, probes)
    other = {"probe": sibling}

    barrier = pltpu.get_barrier_semaphore()

    @pl.loop(1, slabs)
    def _(d):
        pl.semaphore_signal(barrier, inc=1, device_id={"slab": lax.rem(slab + d, slabs)}, device_id_type=MESH)

    for device in (sibling, partner):
        pl.semaphore_signal(barrier, inc=1, device_id={"probe": device}, device_id_type=MESH)
    nearby = [
        pltpu.make_async_copy(library, lib, near.at[0]),
        pltpu.make_async_copy(te_hbm, te, near.at[1]),
        pltpu.make_async_copy(to_hbm, to, near.at[2]),
        pltpu.make_async_copy(receptor.at[pl.ds(core * half, half)], own.at[pl.ds(0, half)], near.at[3]),
        pltpu.make_async_copy(receptor.at[pl.ds((1 - core) * half, half)], own.at[pl.ds(half, half)], near.at[4]),
    ]

    def halo_copy(j, side):
        return pltpu.make_async_remote_copy(
            src_ref=receptor.at[core * half + j],
            dst_ref=(before, after)[side].at[j],
            send_sem=send.at[side, j],
            recv_sem=recv.at[side, j],
            device_id=(right, left)[side],
            device_id_type=MESH,
        )

    def hand_copy(j, side):
        ref = (before, after)[side]
        return pltpu.make_async_remote_copy(
            src_ref=ref.at[j],
            dst_ref=ref.at[half + j],
            send_sem=hand_send.at[side, j],
            recv_sem=hand_recv.at[side, j],
            device_id=other,
            device_id_type=MESH,
        )

    def hand_over(j):
        for side in range(2):
            halo_copy(j, side).wait_recv()
            hand_copy(j, side).start()

    for copy in nearby:
        copy.start()
    xa[...] = jnp.zeros_like(xa)
    kd[...] = jnp.zeros_like(kd)
    pl.semaphore_wait(barrier, slabs - 1 + 2)

    def send_off(j):
        for side in range(2):
            halo_copy(j, side).start()

    send_off(0)
    nearby[0].wait()
    early = slots - 1

    @pl.loop(0, 2)
    def _(part):
        turned_probes(
            part * early, early + part * (slots - early),
            ids, rots, offs, turns, core, lib, swap_ref, lane_ref, zstep_ref, xa, xb, kd, even, odd, tzs, ph,
        )

        @pl.when(part == 0)
        def _():
            send_off(1)

    for copy in nearby[1:]:
        copy.wait()
    hand_over(0)

    def pairs(low, high):
        @pl.loop(low, high)
        def _(p):
            probe_pair(p, te, to, even, odd, tzs, ph, q)

    tz = tz_ref[...]

    def products(group, first):
        @pl.loop(0, slots)
        def _(slot):
            contract(slot, group, q, spec, None if first else joint.at[slot], joint.at[slot])

    pairs(0, 3)
    send_off(2)
    pairs(3, 5)
    hand_over(1)
    pairs(5, PAIRS)
    send_off(3)

    @pl.loop(0, terms)
    def _(i):
        j, h = i // 2, i % 2

        @pl.when(h == 1)
        def _():
            for side in range(2):
                hand_copy(j, side).wait_recv()

        forward(j + half * h, own, before, after, wf_ref, tz, work, spec)

        @pl.when(i == 1)
        def _():
            hand_over(2)

        @pl.when(i == 3)
        def _():
            products((0, 1, half, half + 1), True)
            hand_over(3)

        @pl.when(i == 5)
        def _():
            products((2, half + 2), False)

    def face_copy(slot, side):
        return pltpu.make_async_remote_copy(
            src_ref=total.at[slot, (planes - 1, 0)[side]],
            dst_ref=faces.at[side, slot],
            send_sem=face_send.at[side, slot],
            recv_sem=face_recv.at[side, slot],
            device_id=(right, left)[side],
            device_id_type=MESH,
        )

    @pl.loop(0, slots)
    def _(slot):
        contract(slot, (3, half + 3), q, spec, joint.at[slot], work)
        boltzmann(slot, wi_ref, tz, work, total, sums)
        for side in range(2):
            face_copy(slot, side).start()

    parts = []
    for s in range(slots):
        v = jnp.sum(sums[s], axis=0, keepdims=True)
        parts.append(jnp.broadcast_to(jnp.sum(v, axis=1, keepdims=True), (1, NY)))
    parts += [jnp.zeros((1, NY), F32)] * (8 - slots)
    local_part = jnp.concatenate(parts, axis=0)
    mine[...] = local_part

    def part_copy(d):
        return pltpu.make_async_remote_copy(
            src_ref=mine,
            dst_ref=gathered.at[d],
            send_sem=part_send,
            recv_sem=part_recv,
            device_id={"slab": lax.rem(slab + d, slabs)},
            device_id_type=MESH,
        )

    @pl.loop(1, slabs)
    def _(d):
        part_copy(d).start()

    @pl.loop(0, slots)
    def _(slot):
        for side in range(2):
            face_copy(slot, side).wait_recv()

    others = gathered.at[pl.ds(1, slabs - 1)]
    pltpu.make_async_copy(others, others, part_recv).wait()

    partition = local_part
    for d in range(1, slabs):
        partition = partition + gathered[d]
    share = cells / partition
    coefs = [jnp.broadcast_to(share[s : s + 1] * weights[ids[s]], (8, NY)) for s in range(slots)]

    def weighted(read):
        result = None
        for s in range(slots):
            v = read(s).reshape(NZ // 8, 8, NY) * coefs[s][None]
            result = v if result is None else result + v
        return result.reshape(NZ, NY)

    mixed[0] = weighted(lambda s: faces[0, s])
    mixed[planes + 1] = weighted(lambda s: faces[1, s])
    for x in range(planes):
        mixed[x + 1] = weighted(lambda s: total[s, x])
    for x in range(planes):
        v = (mixed[x] + 2.0 * mixed[x + 1] + mixed[x + 2]) * 0.25
        v = (pltpu.roll(v, 1, 0) + 2.0 * v + pltpu.roll(v, NZ - 1, 0)) * 0.25
        v = (pltpu.roll(v, 1, 1) + 2.0 * v + pltpu.roll(v, NY - 1, 1)) * 0.25
        mixed[x] = v

    def block(p):
        return mixed.at[pl.ds(0, planes), pl.ds(pl.multiple_of(p * rows, 8), rows)]

    away = partner + sibling - probe
    crossing = [
        pltpu.make_async_remote_copy(
            src_ref=block(p),
            dst_ref=blocks.at[i],
            send_sem=block_send.at[i],
            recv_sem=block_recv.at[i],
            device_id={"probe": device},
            device_id_type=MESH,
        )
        for i, (p, device) in enumerate(((away, sibling), (sibling, sibling)))
    ]
    last = pltpu.make_async_remote_copy(
        src_ref=blocks.at[2],
        dst_ref=blocks.at[3],
        send_sem=block_send.at[2],
        recv_sem=block_recv.at[2],
        device_id={"probe": partner},
        device_id_type=MESH,
    )
    for copy in crossing:
        copy.start()
    crossing[0].wait_recv()
    blocks[2] = block(partner)[...] + blocks[0]
    last.start()
    crossing[1].wait_recv()
    result = block(probe)[...] + blocks[1]
    last.wait_recv()
    out_ref[...] = (result + blocks[3]) * (1.0 / weights.shape[0])

    @pl.loop(0, half)
    def _(j):
        for side in range(2):
            halo_copy(j, side).wait_send()
            hand_copy(j, side).wait_send()

    @pl.loop(0, slots)
    def _(slot):
        for side in range(2):
            face_copy(slot, side).wait_send()

    pltpu.make_async_copy(others, others, part_send).wait()

    for copy in (*crossing, last):
        copy.wait_send()


def sum_terms(terms):
    total = None
    for coef, value in terms:
        if abs(coef) < 1e-15:
            continue
        total = coef * value if total is None else total + coef * value
    return total


def local(receptor, library, probe_ids, rotations, offsets, probe_weight):
    terms, planes, nz, ny = receptor.shape
    slabs = lax.axis_size("slab")
    probes = lax.axis_size("probe")
    slots, half = probe_ids.shape[0], terms // 2
    rows = nz // probes
    cells = float(planes * slabs * nz * ny)
    te, to = xy_tables()
    smem = pl.BlockSpec(memory_space=pltpu.SMEM)
    vmem = pl.BlockSpec(memory_space=pltpu.VMEM)
    hbm = pl.BlockSpec(memory_space=pl.ANY)
    dma = pltpu.SemaphoreType.DMA
    return pl.pallas_call(
        functools.partial(energy_kernel, slabs, probes, cells),
        in_specs=[smem] * 5 + [hbm] * 4 + [vmem] * 6,
        out_specs=vmem,
        out_shape=jax.ShapeDtypeStruct((planes, rows, ny), F32),
        scratch_shapes=[
            pltpu.VMEM(library.shape, F32),
            pltpu.VMEM(te.shape, BF),
            pltpu.VMEM(to.shape, BF),
            pltpu.VMEM(receptor.shape, F32),
            pltpu.VMEM(receptor.shape, F32),
            pltpu.VMEM(receptor.shape, F32),
            pltpu.VMEM((KS, terms, CUBE), F32),
            pltpu.VMEM((KS, terms, CUBE), F32),
            pltpu.VMEM((CUBE // 128, terms * AZ, 128), F32),
            pltpu.VMEM((slots * terms * AZ, PACK), BF),
            pltpu.VMEM((slots * terms * AZ, PACK), BF),
            pltpu.VMEM((slots, 2 * NZ, 6 * AZ), BF),
            pltpu.VMEM((slots, 2, 8, 2 * NY), F32),
            pltpu.VMEM((slots, terms, PAIRS, 2 * NZ, 2 * NY), F32),
            pltpu.VMEM((terms, KX, nz, 2 * ny), F32),
            pltpu.VMEM((KX, nz, 2 * ny), F32),
            pltpu.VMEM((slots, KX, nz, 2 * ny), F32),
            pltpu.VMEM((slots, planes, nz, ny), F32),
            pltpu.VMEM((slots, 8, ny), F32),
            pltpu.VMEM((8, ny), F32),
            pltpu.VMEM((slabs, 8, ny), F32),
            pltpu.VMEM((2, slots, nz, ny), F32),
            pltpu.VMEM((planes + 2, nz, ny), F32),
            pltpu.VMEM((4, planes, rows, ny), F32),
            dma((2, half)),
            dma((2, half)),
            dma((2, half)),
            dma((2, half)),
            dma((5,)),
            pltpu.SemaphoreType.DMA,
            pltpu.SemaphoreType.DMA,
            dma((2, slots)),
            dma((2, slots)),
            dma((3,)),
            dma((3,)),
        ],
        compiler_params=pltpu.CompilerParams(
            collective_id=0, has_side_effects=True, vmem_limit_bytes=63 << 20
        ),
        name="consensus_density",
    )(
        probe_ids,
        rotations.reshape(-1),
        offsets.reshape(-1),
        probe_weight,
        jnp.asarray(rotation_table()),
        receptor,
        library,
        jnp.asarray(te),
        jnp.asarray(to),
        jnp.asarray(swap_table()),
        jnp.asarray(lane_offsets()),
        jnp.asarray(probe_z_steps()),
        jnp.asarray(grid_z_table()),
        jnp.asarray(grid_y_table(-1.0)),
        jnp.asarray(grid_y_table(1.0)),
    )


def solution(mesh):
    in_specs = (
        P(None, "slab", None, None),
        P(),
        P("probe"),
        P("probe", None),
        P("probe", None, None),
        P(),
    )
    out_specs = P("slab", "probe", None)
    return jax.shard_map(local, mesh=mesh, in_specs=in_specs, out_specs=out_specs, check_vma=False)
```

```python
import functools
import math

import jax
import jax.numpy as jnp
import ml_dtypes
import numpy as np
from jax import lax
from jax.experimental import pallas as pl
from jax.experimental.pallas import tpu as pltpu
from jax.sharding import PartitionSpec as P

RAD = 8
KS = 17
AZ = 24
EXT = 24
KX = 13
PAIRS = 7
NZ = 64
NY = 128
ENERGY_CAP = 6.0
HIGHEST = lax.Precision.HIGHEST
MESH = pl.DeviceIdType.MESH
BF = jnp.bfloat16
F32 = jnp.float32


def cube_rotations():
    permutes = [(0, 1, 2), (0, 2, 1), (1, 0, 2), (1, 2, 0), (2, 0, 1), (2, 1, 0)]
    parities = [1, -1, -1, 1, 1, -1]
    perms, signs = [], []
    for permute, parity in zip(permutes, parities):
        for sign_x in (1, -1):
            for sign_y in (1, -1):
                for sign_z in (1, -1):
                    if parity * sign_x * sign_y * sign_z == 1:
                        perms.append(permute)
                        signs.append((sign_x, sign_y, sign_z))
    return np.array(perms, np.int32), np.array(signs, np.int32)


def split_np(table):
    table = table.astype(np.float32)
    hi = table.astype(ml_dtypes.bfloat16)
    lo = (table - hi.astype(np.float32)).astype(ml_dtypes.bfloat16)
    return hi, lo


HALF = (KS * KS + 1) // 2
CUBE = 384
PACK = 512


def half_offsets():
    flat = np.arange(HALF) + HALF - 1
    return flat // KS - RAD, flat % KS - RAD


def xy_tables():
    ax, ay = half_offsets()
    kx = np.arange(2 * PAIRS)
    ky = np.arange(NY)
    px = (ax[:, None] * kx[None, :]) % EXT / EXT
    py = (ay[:, None] * ky[None, :]) % NY / NY
    ang = 2 * np.pi * (px[:, :, None] + py[:, None, :])
    live = (kx < KX).astype(np.float64)[None, :, None]
    out = []
    for t in (np.cos(ang) * live, np.sin(ang) * live):
        hi, lo = split_np(t.reshape(HALF, -1))
        pad = np.zeros((PACK - 3 * HALF, hi.shape[1]), hi.dtype)
        out.append(np.concatenate([hi, hi, lo, pad], axis=0))
    return out


def lane_offsets():
    ax, ay = half_offsets()
    rows = np.full((8, CUBE), 10000, np.int32)
    rows[2:] = 0
    for c in range(2):
        lanes = slice(c * HALF, (c + 1) * HALF)
        rows[0, lanes] = ax
        rows[1, lanes] = ay
        rows[2, c * HALF] = 10000
        rows[3, lanes] = 1 - 2 * c
    return rows


def swap_table():
    t = np.zeros((CUBE, CUBE), np.float32)
    for m in range(KS):
        for n in range(KS):
            t[n * KS + m, m * KS + n] = 1
    return t.astype(ml_dtypes.bfloat16)


def rotation_table():
    perms, signs = cube_rotations()
    table = np.zeros((24, 4), np.int32)
    for q in range(24):
        zaxis = [i for i in range(3) if perms[q, i] == 2][0]
        others = [i for i in range(3) if i != zaxis]
        table[q, 0] = zaxis
        table[q, 1] = 1 if signs[q, zaxis] < 0 else 0
        for i, unit in zip(others, (KS, 1)):
            table[q, 2 + perms[q, i]] = unit * signs[q, i]
    return table


def probe_z_steps():
    kz = np.arange(2 * NZ) % NZ
    lane = np.arange(6 * AZ) % (2 * AZ)
    az = lane % AZ
    quarter = np.where((np.arange(2 * NZ) < NZ)[:, None], np.where(lane < AZ, 0, 16), np.where(lane < AZ, -16, 0))
    turn = (kz[:, None] * (az - RAD)[None, :] + quarter) % NZ
    live = np.broadcast_to((az < KS).astype(np.int64)[None], turn.shape)
    return np.stack([turn, np.broadcast_to(kz[:, None], turn.shape), live]).astype(np.int32)


def grid_z_table():
    k = np.arange(NZ)
    ang = 2 * np.pi * ((k[:, None] * k[None, :]) % NZ) / NZ
    t = np.concatenate([np.cos(ang), np.sin(ang)], axis=0)
    hi, lo = split_np(t)
    return np.concatenate([hi, lo, hi], axis=1)


def grid_y_table(direction):
    k = np.arange(NY)
    ang = 2 * np.pi * ((k[:, None] * k[None, :]) % NY) / NY
    c, s = np.cos(ang), direction * np.sin(ang)
    hi, lo = split_np(np.block([[c, s], [-s, c]]))
    return np.concatenate([hi, hi, lo], axis=0)


def split(x):
    hi = x.astype(BF)
    lo = (x - hi.astype(F32)).astype(BF)
    return hi, lo


def turned_probes(first, last, ids, rots, offs, turns, core, lib_ref, swap_ref, lane_ref, zstep_ref, xa, xb, kd, even, odd, tzs, ph):
    terms = lib_ref.shape[1]
    lane = lax.broadcasted_iota(jnp.int32, (terms, CUBE), 1)
    source = lax.broadcasted_iota(jnp.int32, (CUBE, CUBE), 0)
    zlane = lax.broadcasted_iota(jnp.int32, (2 * NZ, 6 * AZ), 1)
    ky = lax.broadcasted_iota(jnp.int32, (8, 2 * NY), 1) % NY

    def permuted(x, table):
        hi, lo = split(x)
        out = jnp.dot(jnp.concatenate([hi, lo], axis=0), table, preferred_element_type=F32)
        return out[: x.shape[0]] + out[x.shape[0] :]

    @pl.loop(first, last)
    def _(slot):
        rot = rots[slot]
        zaxis, flipped = turns[rot, 0], turns[rot, 1]
        step_x, step_y = turns[rot, 2], turns[rot, 3]
        off_y, off_z = offs[2 * slot], offs[2 * slot + 1]

        turn = (zstep_ref[0] - zstep_ref[1] * off_z + NZ * NZ) & (NZ - 1)
        t = jnp.cos(turn.astype(F32) * (2 * math.pi / NZ)) * zstep_ref[2].astype(F32)
        hi, lo = split(t)
        tzs[slot] = jnp.where((zlane >= 2 * AZ) & (zlane < 4 * AZ), lo.astype(F32), hi.astype(F32)).astype(BF)
        turn = ky * off_y
        ph[slot, 0] = jnp.cos((turn & (NY - 1)).astype(F32) * (2 * math.pi / NY))
        ph[slot, 1] = jnp.cos(((turn - NY // 4) & (NY - 1)).astype(F32) * (2 * math.pi / NY))

        for m in range(KS):
            w = lib_ref[ids[slot], :, m * KS * KS : (m + 1) * KS * KS]
            xa[m, :, : KS * KS] = jnp.where(core == 0, w, pltpu.roll(w, terms // 2, 0))
        x = xa[...]
        swapped = permuted(x.reshape(KS * terms, CUBE), swap_ref[...]).reshape(KS, terms, CUBE)
        xa[...] = jnp.where(zaxis == 2, swapped, x)
        for m in range(KS):
            acc = jnp.concatenate(
                [xa[n, :, m * KS : (m + 1) * KS] for n in range(KS)] + [jnp.zeros((terms, CUBE - KS * KS), F32)],
                axis=1,
            )
            xb[m] = jnp.where(zaxis == 0, xa[m], acc)

        here = lane_ref[0:1] * step_x + lane_ref[1:2] * step_y + (HALF - 1)
        there = 2 * (HALF - 1) - here + lane_ref[2:3]
        plus = (source == here).astype(F32)
        minus = jnp.where(source == there, lane_ref[3:4], 0).astype(F32)
        turned = permuted(xb[...].reshape(KS * terms, CUBE), (plus + minus).astype(BF))
        for m in range(KS):
            f = KS - 1 - m
            row = jnp.where(flipped == 1, turned[f * terms : (f + 1) * terms], turned[m * terms : (m + 1) * terms])
            for j in range(CUBE // 128):
                kd[j, pl.ds(m, terms, stride=AZ), :] = row[:, j * 128 : (j + 1) * 128]
        rows = pl.ds(pl.multiple_of(slot * terms * AZ, terms * AZ), terms * AZ)
        both = jnp.concatenate([kd[j] for j in range(CUBE // 128)], axis=1)
        hi, lo = split(both)
        hi, lo = hi.astype(F32), lo.astype(F32)
        spare = jnp.zeros((terms * AZ, PACK - 3 * HALF), F32)
        for ref, lanes in ((even, slice(0, HALF)), (odd, slice(HALF, 2 * HALF))):
            ref[rows, :] = jnp.concatenate([hi[:, lanes], lo[:, lanes], hi[:, lanes], spare], axis=1).astype(BF)


def probe_pair(p, te, to, even, odd, tzs, ph, q):
    slots, terms = q.shape[0], q.shape[1]
    columns = pl.ds(pl.multiple_of(p * 2 * NY, 2 * NY), 2 * NY)
    re_all = jnp.dot(even[...], te[:, columns], preferred_element_type=F32)
    im_all = jnp.dot(odd[...], to[:, columns], preferred_element_type=F32)
    for s in range(slots):
        c, n = ph[s, 0, 0:1], ph[s, 1, 0:1]
        rows = slice(s * terms * AZ, (s + 1) * terms * AZ)
        re = re_all[rows] * c + im_all[rows] * n
        im = im_all[rows] * c - re_all[rows] * n
        tz = tzs[s]
        for t in range(terms):
            d = jnp.concatenate([re[t * AZ : (t + 1) * AZ], im[t * AZ : (t + 1) * AZ]], axis=0)
            hi, lo = split(d)
            q[s, t, p] = jnp.dot(tz, jnp.concatenate([hi, hi, lo], axis=0), preferred_element_type=F32)


def cos24(m):
    return math.cos(2 * math.pi * (m % 24) / 24)


def sin24(m):
    return math.sin(2 * math.pi * (m % 24) / 24)


def lin(terms):
    total = None
    for coef, value in terms:
        if abs(coef) < 1e-12:
            continue
        if abs(coef - 1) < 1e-12:
            total = value if total is None else total + value
        elif abs(coef + 1) < 1e-12:
            total = -value if total is None else total - value
        else:
            total = coef * value if total is None else total + coef * value
    return total


def real_dft24(r):
    a = [r[0]] + [r[n] + r[24 - n] for n in range(1, 12)] + [r[12]]
    b = [None] + [r[n] - r[24 - n] for n in range(1, 12)]
    re, im = [None] * 13, [None] * 13
    c = [a[n] + a[12 - n] for n in range(6)] + [a[6]]
    d = [a[n] - a[12 - n] for n in range(6)]
    ce = [c[n] + c[6 - n] for n in range(3)] + [c[3]]
    co = [c[n] - c[6 - n] for n in range(3)]
    for m in range(7):
        if m % 2 == 0:
            re[2 * m] = lin([(cos24(2 * m * n), ce[n]) for n in range(4)])
        else:
            re[2 * m] = lin([(cos24(2 * m * n), co[n]) for n in range(3)])
    for k in range(1, 12, 2):
        re[k] = lin([(cos24(k * n), d[n]) for n in range(6)])
    e = [None] + [b[n] + b[12 - n] for n in range(1, 6)] + [b[6]]
    f = [None] + [b[n] - b[12 - n] for n in range(1, 6)]
    for k in range(1, 12, 2):
        im[k] = lin([(-sin24(k * n), e[n]) for n in range(1, 7)])
    fo = [None] + [f[n] + f[6 - n] for n in range(1, 3)] + [f[3]]
    fe = [None] + [f[n] - f[6 - n] for n in range(1, 3)]
    for m in range(1, 6):
        if m % 2 == 1:
            im[2 * m] = lin([(-sin24(2 * m * n), fo[n]) for n in range(1, 4)])
        else:
            im[2 * m] = lin([(-sin24(2 * m * n), fe[n]) for n in range(1, 3)])
    return re, im


def y_stage(x, w):
    hi, lo = split(x)
    return jnp.dot(jnp.concatenate([hi, lo, hi], axis=1), w, preferred_element_type=F32)


def z_stage(tz, x, direction):
    hi, lo = split(x)
    rhs = jnp.concatenate([hi, hi, lo], axis=0)
    p = jnp.dot(tz, rhs, preferred_element_type=F32)
    re = p[:NZ, :NY] - direction * p[NZ:, NY:]
    im = p[:NZ, NY:] + direction * p[NZ:, :NY]
    return re, im


def forward(i, own, before, after, wf_ref, tz, work, spec):
    @pl.loop(0, 8, unroll=True)
    def _(chunk):
        rows = pl.ds(pl.multiple_of(chunk * 8, 8), 8)
        r = (
            [before[i, n, rows] for n in range(8)]
            + [own[i, n, rows] for n in range(8)]
            + [after[i, n, rows] for n in range(8)]
        )
        re, im = real_dft24(r)
        for k in range(KX):
            work[k, rows, :NY] = re[k]
            work[k, rows, NY:] = im[k] if im[k] is not None else jnp.zeros_like(re[k])

    y = y_stage(work[...].reshape(KX * NZ, 2 * NY), wf_ref[...])
    work[...] = y.reshape(KX, NZ, 2 * NY)
    for k in range(KX):
        re, im = z_stage(tz, work[k], -1.0)
        spec[i, k, :, :NY] = re
        spec[i, k, :, NY:] = im


def contract(slot, group, q, spec, source, target):
    @pl.loop(0, 8, unroll=4)
    def _(chunk):
        start = pl.multiple_of(chunk * 8, 8)
        rows = pl.ds(start, 8)
        low = pl.ds(start + NZ, 8)
        for k in range(KX):
            p, lane = k // 2, (k % 2) * NY
            re = None if source is None else source[k, rows, :NY]
            im = None if source is None else source[k, rows, NY:]
            for t in group:
                gr, gi = spec[t, k, rows, :NY], spec[t, k, rows, NY:]
                qr = q[slot, t, p, rows, lane : lane + NY]
                qi = q[slot, t, p, low, lane : lane + NY]
                tr = gr * qr - gi * qi
                ti = gr * qi + gi * qr
                re = tr if re is None else re + tr
                im = ti if im is None else im + ti
            target[k, rows, :NY] = re
            target[k, rows, NY:] = im


def boltzmann(slot, wi_ref, tz, work, total_ref, sum_ref):
    for k in range(KX):
        re, im = z_stage(tz, work[k], 1.0)
        work[k, :, :NY] = re
        work[k, :, NY:] = im
    y = y_stage(work[...].reshape(KX * NZ, 2 * NY), wi_ref[...])
    work[...] = y.reshape(KX, NZ, 2 * NY)
    sum_ref[slot] = jnp.zeros((8, NY), F32)
    scale = 1.0 / (EXT * NZ * NY)

    @pl.loop(0, 8, unroll=True)
    def _(chunk):
        rows = pl.ds(pl.multiple_of(chunk * 8, 8), 8)
        fr = [work[k, rows, :NY] for k in range(KX)]
        fi = [work[k, rows, NY:] for k in range(KX)]
        acc = sum_ref[slot]
        for m in range(5):
            even, odd = [], []
            for k in range(KX):
                w = scale * (1.0 if k in (0, 12) else 2.0) * (-1) ** k
                even.append((w * cos24(k * m), fr[k]))
                odd.append((w * sin24(k * m), fi[k]))
            even, odd = sum_terms(even), sum_terms(odd)
            for x, e in ((4, even),) if m == 0 else ((4 + m, even - odd), (4 - m, even + odd)):
                if x < 8:
                    b = jnp.exp(-ENERGY_CAP * jnp.tanh(e / ENERGY_CAP))
                    total_ref[slot, x, rows] = b
                    acc = acc + b
        sum_ref[slot] = acc


def energy_kernel(
    slabs,
    probes,
    cells,
    ids,
    rots,
    offs,
    weights,
    turns,
    receptor,
    library,
    te_hbm,
    to_hbm,
    swap_ref,
    lane_ref,
    zstep_ref,
    tz_ref,
    wf_ref,
    wi_ref,
    out_ref,
    lib,
    te,
    to,
    own,
    before,
    after,
    xa,
    xb,
    kd,
    even,
    odd,
    tzs,
    ph,
    q,
    spec,
    work,
    joint,
    total,
    sums,
    mine,
    gathered,
    faces,
    mixed,
    blocks,
    send,
    recv,
    hand_send,
    hand_recv,
    near,
    part_send,
    part_recv,
    face_send,
    face_recv,
    block_send,
    block_recv,
):
    terms, planes = receptor.shape[0], receptor.shape[1]
    half = terms // 2
    slots = total.shape[0]
    rows = out_ref.shape[1]
    slab = lax.axis_index("slab")
    probe = lax.axis_index("probe")
    core = lax.rem(probe, 2)
    right = {"slab": lax.rem(slab + 1, slabs)}
    left = {"slab": lax.rem(slab + slabs - 1, slabs)}
    sibling = probe + 1 - 2 * core
    partner = lax.rem(probe + 2, probes)
    other = {"probe": sibling}

    barrier = pltpu.get_barrier_semaphore()

    @pl.loop(1, slabs)
    def _(d):
        pl.semaphore_signal(barrier, inc=1, device_id={"slab": lax.rem(slab + d, slabs)}, device_id_type=MESH)

    for device in (sibling, partner):
        pl.semaphore_signal(barrier, inc=1, device_id={"probe": device}, device_id_type=MESH)
    nearby = [
        pltpu.make_async_copy(library, lib, near.at[0]),
        pltpu.make_async_copy(te_hbm, te, near.at[1]),
        pltpu.make_async_copy(to_hbm, to, near.at[2]),
        pltpu.make_async_copy(receptor.at[pl.ds(core * half, half)], own.at[pl.ds(0, half)], near.at[3]),
        pltpu.make_async_copy(receptor.at[pl.ds((1 - core) * half, half)], own.at[pl.ds(half, half)], near.at[4]),
    ]

    def halo_copy(j, side):
        return pltpu.make_async_remote_copy(
            src_ref=receptor.at[core * half + j],
            dst_ref=(before, after)[side].at[j],
            send_sem=send.at[side, j],
            recv_sem=recv.at[side, j],
            device_id=(right, left)[side],
            device_id_type=MESH,
        )

    def hand_copy(j, side):
        ref = (before, after)[side]
        return pltpu.make_async_remote_copy(
            src_ref=ref.at[j],
            dst_ref=ref.at[half + j],
            send_sem=hand_send.at[side, j],
            recv_sem=hand_recv.at[side, j],
            device_id=other,
            device_id_type=MESH,
        )

    def hand_over(j):
        for side in range(2):
            halo_copy(j, side).wait_recv()
            hand_copy(j, side).start()

    for copy in nearby:
        copy.start()
    xa[...] = jnp.zeros_like(xa)
    kd[...] = jnp.zeros_like(kd)
    pl.semaphore_wait(barrier, slabs - 1 + 2)

    def send_off(j):
        for side in range(2):
            halo_copy(j, side).start()

    send_off(0)
    nearby[0].wait()
    early = slots - 1

    @pl.loop(0, 2)
    def _(part):
        turned_probes(
            part * early, early + part * (slots - early),
            ids, rots, offs, turns, core, lib, swap_ref, lane_ref, zstep_ref, xa, xb, kd, even, odd, tzs, ph,
        )

        @pl.when(part == 0)
        def _():
            send_off(1)

    for copy in nearby[1:]:
        copy.wait()
    hand_over(0)

    def pairs(low, high):
        @pl.loop(low, high)
        def _(p):
            probe_pair(p, te, to, even, odd, tzs, ph, q)

    tz = tz_ref[...]

    def products(group, first):
        @pl.loop(0, slots)
        def _(slot):
            contract(slot, group, q, spec, None if first else joint.at[slot], joint.at[slot])

    pairs(0, 3)
    send_off(2)
    pairs(3, 5)
    hand_over(1)
    pairs(5, PAIRS)
    send_off(3)

    @pl.loop(0, terms)
    def _(i):
        j, h = i // 2, i % 2

        @pl.when(h == 1)
        def _():
            for side in range(2):
                hand_copy(j, side).wait_recv()

        forward(j + half * h, own, before, after, wf_ref, tz, work, spec)

        @pl.when(i == 1)
        def _():
            hand_over(2)

        @pl.when(i == 3)
        def _():
            products((0, 1, half, half + 1), True)
            hand_over(3)

        @pl.when(i == 5)
        def _():
            products((2, half + 2), False)

    def face_copy(slot, side):
        return pltpu.make_async_remote_copy(
            src_ref=total.at[slot, (planes - 1, 0)[side]],
            dst_ref=faces.at[side, slot],
            send_sem=face_send.at[side, slot],
            recv_sem=face_recv.at[side, slot],
            device_id=(right, left)[side],
            device_id_type=MESH,
        )

    @pl.loop(0, slots)
    def _(slot):
        contract(slot, (3, half + 3), q, spec, joint.at[slot], work)
        boltzmann(slot, wi_ref, tz, work, total, sums)
        for side in range(2):
            face_copy(slot, side).start()

    parts = []
    for s in range(slots):
        v = jnp.sum(sums[s], axis=0, keepdims=True)
        parts.append(jnp.broadcast_to(jnp.sum(v, axis=1, keepdims=True), (1, NY)))
    parts += [jnp.zeros((1, NY), F32)] * (8 - slots)
    local_part = jnp.concatenate(parts, axis=0)
    mine[...] = local_part

    def part_copy(d):
        return pltpu.make_async_remote_copy(
            src_ref=mine,
            dst_ref=gathered.at[d],
            send_sem=part_send,
            recv_sem=part_recv,
            device_id={"slab": lax.rem(slab + d, slabs)},
            device_id_type=MESH,
        )

    @pl.loop(1, slabs)
    def _(d):
        part_copy(d).start()

    @pl.loop(0, slots)
    def _(slot):
        for side in range(2):
            face_copy(slot, side).wait_recv()

    others = gathered.at[pl.ds(1, slabs - 1)]
    pltpu.make_async_copy(others, others, part_recv).wait()

    partition = local_part
    for d in range(1, slabs):
        partition = partition + gathered[d]
    share = cells / partition
    coefs = [jnp.broadcast_to(share[s : s + 1] * weights[ids[s]], (8, NY)) for s in range(slots)]

    def weighted(read):
        result = None
        for s in range(slots):
            v = read(s).reshape(NZ // 8, 8, NY) * coefs[s][None]
            result = v if result is None else result + v
        return result.reshape(NZ, NY)

    mixed[0] = weighted(lambda s: faces[0, s])
    mixed[planes + 1] = weighted(lambda s: faces[1, s])
    for x in range(planes):
        mixed[x + 1] = weighted(lambda s: total[s, x])
    for x in range(planes):
        v = (mixed[x] + 2.0 * mixed[x + 1] + mixed[x + 2]) * 0.25
        v = (pltpu.roll(v, 1, 0) + 2.0 * v + pltpu.roll(v, NZ - 1, 0)) * 0.25
        v = (pltpu.roll(v, 1, 1) + 2.0 * v + pltpu.roll(v, NY - 1, 1)) * 0.25
        mixed[x] = v

    def block(p):
        return mixed.at[pl.ds(0, planes), pl.ds(pl.multiple_of(p * rows, 8), rows)]

    away = partner + sibling - probe
    crossing = [
        pltpu.make_async_remote_copy(
            src_ref=block(p),
            dst_ref=blocks.at[i],
            send_sem=block_send.at[i],
            recv_sem=block_recv.at[i],
            device_id={"probe": device},
            device_id_type=MESH,
        )
        for i, (p, device) in enumerate(((away, sibling), (sibling, sibling)))
    ]
    last = pltpu.make_async_remote_copy(
        src_ref=blocks.at[2],
        dst_ref=blocks.at[3],
        send_sem=block_send.at[2],
        recv_sem=block_recv.at[2],
        device_id={"probe": partner},
        device_id_type=MESH,
    )
    for copy in crossing:
        copy.start()
    crossing[0].wait_recv()
    blocks[2] = block(partner)[...] + blocks[0]
    last.start()
    crossing[1].wait_recv()
    result = block(probe)[...] + blocks[1]
    last.wait_recv()
    out_ref[...] = (result + blocks[3]) * (1.0 / weights.shape[0])

    @pl.loop(0, half)
    def _(j):
        for side in range(2):
            halo_copy(j, side).wait_send()
            hand_copy(j, side).wait_send()

    @pl.loop(0, slots)
    def _(slot):
        for side in range(2):
            face_copy(slot, side).wait_send()

    pltpu.make_async_copy(others, others, part_send).wait()

    for copy in (*crossing, last):
        copy.wait_send()


def sum_terms(terms):
    total = None
    for coef, value in terms:
        if abs(coef) < 1e-15:
            continue
        total = coef * value if total is None else total + coef * value
    return total


def local(receptor, library, probe_ids, rotations, offsets, probe_weight):
    terms, planes, nz, ny = receptor.shape
    slabs = lax.axis_size("slab")
    probes = lax.axis_size("probe")
    slots, half = probe_ids.shape[0], terms // 2
    rows = nz // probes
    cells = float(planes * slabs * nz * ny)
    te, to = xy_tables()
    smem = pl.BlockSpec(memory_space=pltpu.SMEM)
    vmem = pl.BlockSpec(memory_space=pltpu.VMEM)
    hbm = pl.BlockSpec(memory_space=pl.ANY)
    dma = pltpu.SemaphoreType.DMA
    return pl.pallas_call(
        functools.partial(energy_kernel, slabs, probes, cells),
        in_specs=[smem] * 5 + [hbm] * 4 + [vmem] * 6,
        out_specs=vmem,
        out_shape=jax.ShapeDtypeStruct((planes, rows, ny), F32),
        scratch_shapes=[
            pltpu.VMEM(library.shape, F32),
            pltpu.VMEM(te.shape, BF),
            pltpu.VMEM(to.shape, BF),
            pltpu.VMEM(receptor.shape, F32),
            pltpu.VMEM(receptor.shape, F32),
            pltpu.VMEM(receptor.shape, F32),
            pltpu.VMEM((KS, terms, CUBE), F32),
            pltpu.VMEM((KS, terms, CUBE), F32),
            pltpu.VMEM((CUBE // 128, terms * AZ, 128), F32),
            pltpu.VMEM((slots * terms * AZ, PACK), BF),
            pltpu.VMEM((slots * terms * AZ, PACK), BF),
            pltpu.VMEM((slots, 2 * NZ, 6 * AZ), BF),
            pltpu.VMEM((slots, 2, 8, 2 * NY), F32),
            pltpu.VMEM((slots, terms, PAIRS, 2 * NZ, 2 * NY), F32),
            pltpu.VMEM((terms, KX, nz, 2 * ny), F32),
            pltpu.VMEM((KX, nz, 2 * ny), F32),
            pltpu.VMEM((slots, KX, nz, 2 * ny), F32),
            pltpu.VMEM((slots, planes, nz, ny), F32),
            pltpu.VMEM((slots, 8, ny), F32),
            pltpu.VMEM((8, ny), F32),
            pltpu.VMEM((slabs, 8, ny), F32),
            pltpu.VMEM((2, slots, nz, ny), F32),
            pltpu.VMEM((planes + 2, nz, ny), F32),
            pltpu.VMEM((4, planes, rows, ny), F32),
            dma((2, half)),
            dma((2, half)),
            dma((2, half)),
            dma((2, half)),
            dma((5,)),
            pltpu.SemaphoreType.DMA,
            pltpu.SemaphoreType.DMA,
            dma((2, slots)),
            dma((2, slots)),
            dma((3,)),
            dma((3,)),
        ],
        compiler_params=pltpu.CompilerParams(
            collective_id=0, has_side_effects=True, vmem_limit_bytes=63 << 20
        ),
        name="consensus_density",
    )(
        probe_ids,
        rotations.reshape(-1),
        offsets.reshape(-1),
        probe_weight,
        jnp.asarray(rotation_table()),
        receptor,
        library,
        jnp.asarray(te),
        jnp.asarray(to),
        jnp.asarray(swap_table()),
        jnp.asarray(lane_offsets()),
        jnp.asarray(probe_z_steps()),
        jnp.asarray(grid_z_table()),
        jnp.asarray(grid_y_table(-1.0)),
        jnp.asarray(grid_y_table(1.0)),
    )


def solution(mesh):
    in_specs = (
        P(None, "slab", None, None),
        P(),
        P("probe"),
        P("probe", None),
        P("probe", None, None),
        P(),
    )
    out_specs = P("slab", "probe", None)
    return jax.shard_map(local, mesh=mesh, in_specs=in_specs, out_specs=out_specs, check_vma=False)
```

```python
import functools
import math

import jax
import jax.numpy as jnp
import ml_dtypes
import numpy as np
from jax import lax
from jax.experimental import pallas as pl
from jax.experimental.pallas import tpu as pltpu
from jax.sharding import PartitionSpec as P

RAD = 8
KS = 17
AZ = 24
EXT = 24
KX = 13
PAIRS = 7
NZ = 64
NY = 128
ENERGY_CAP = 6.0
HIGHEST = lax.Precision.HIGHEST
MESH = pl.DeviceIdType.MESH
BF = jnp.bfloat16
F32 = jnp.float32


def cube_rotations():
    permutes = [(0, 1, 2), (0, 2, 1), (1, 0, 2), (1, 2, 0), (2, 0, 1), (2, 1, 0)]
    parities = [1, -1, -1, 1, 1, -1]
    perms, signs = [], []
    for permute, parity in zip(permutes, parities):
        for sign_x in (1, -1):
            for sign_y in (1, -1):
                for sign_z in (1, -1):
                    if parity * sign_x * sign_y * sign_z == 1:
                        perms.append(permute)
                        signs.append((sign_x, sign_y, sign_z))
    return np.array(perms, np.int32), np.array(signs, np.int32)


def split_np(table):
    table = table.astype(np.float32)
    hi = table.astype(ml_dtypes.bfloat16)
    lo = (table - hi.astype(np.float32)).astype(ml_dtypes.bfloat16)
    return hi, lo


HALF = (KS * KS + 1) // 2
CUBE = 384
PACK = 512


def half_offsets():
    flat = np.arange(HALF) + HALF - 1
    return flat // KS - RAD, flat % KS - RAD


def xy_tables():
    ax, ay = half_offsets()
    kx = np.arange(2 * PAIRS)
    ky = np.arange(NY)
    px = (ax[:, None] * kx[None, :]) % EXT / EXT
    py = (ay[:, None] * ky[None, :]) % NY / NY
    ang = 2 * np.pi * (px[:, :, None] + py[:, None, :])
    live = (kx < KX).astype(np.float64)[None, :, None]
    out = []
    for t in (np.cos(ang) * live, np.sin(ang) * live):
        hi, lo = split_np(t.reshape(HALF, -1))
        pad = np.zeros((PACK - 3 * HALF, hi.shape[1]), hi.dtype)
        out.append(np.concatenate([hi, hi, lo, pad], axis=0))
    return out


def lane_offsets():
    ax, ay = half_offsets()
    rows = np.full((8, CUBE), 10000, np.int32)
    rows[2:] = 0
    for c in range(2):
        lanes = slice(c * HALF, (c + 1) * HALF)
        rows[0, lanes] = ax
        rows[1, lanes] = ay
        rows[2, c * HALF] = 10000
        rows[3, lanes] = 1 - 2 * c
    return rows


def swap_table():
    t = np.zeros((CUBE, CUBE), np.float32)
    for m in range(KS):
        for n in range(KS):
            t[n * KS + m, m * KS + n] = 1
    return t.astype(ml_dtypes.bfloat16)


def rotation_table():
    perms, signs = cube_rotations()
    table = np.zeros((24, 4), np.int32)
    for q in range(24):
        zaxis = [i for i in range(3) if perms[q, i] == 2][0]
        others = [i for i in range(3) if i != zaxis]
        table[q, 0] = zaxis
        table[q, 1] = 1 if signs[q, zaxis] < 0 else 0
        for i, unit in zip(others, (KS, 1)):
            table[q, 2 + perms[q, i]] = unit * signs[q, i]
    return table


def probe_z_steps():
    kz = np.arange(2 * NZ) % NZ
    lane = np.arange(6 * AZ) % (2 * AZ)
    az = lane % AZ
    quarter = np.where((np.arange(2 * NZ) < NZ)[:, None], np.where(lane < AZ, 0, 16), np.where(lane < AZ, -16, 0))
    turn = (kz[:, None] * (az - RAD)[None, :] + quarter) % NZ
    live = np.broadcast_to((az < KS).astype(np.int64)[None], turn.shape)
    return np.stack([turn, np.broadcast_to(kz[:, None], turn.shape), live]).astype(np.int32)


def grid_z_table():
    k = np.arange(NZ)
    ang = 2 * np.pi * ((k[:, None] * k[None, :]) % NZ) / NZ
    t = np.concatenate([np.cos(ang), np.sin(ang)], axis=0)
    hi, lo = split_np(t)
    return np.concatenate([hi, lo, hi], axis=1)


def grid_y_table(direction):
    k = np.arange(NY)
    ang = 2 * np.pi * ((k[:, None] * k[None, :]) % NY) / NY
    c, s = np.cos(ang), direction * np.sin(ang)
    hi, lo = split_np(np.block([[c, s], [-s, c]]))
    return np.concatenate([hi, hi, lo], axis=0)


def split(x):
    hi = x.astype(BF)
    lo = (x - hi.astype(F32)).astype(BF)
    return hi, lo


def turned_probes(first, last, ids, rots, offs, turns, core, lib_ref, swap_ref, lane_ref, zstep_ref, xa, xb, kd, even, odd, tzs, ph):
    terms = lib_ref.shape[1]
    lane = lax.broadcasted_iota(jnp.int32, (terms, CUBE), 1)
    source = lax.broadcasted_iota(jnp.int32, (CUBE, CUBE), 0)
    zlane = lax.broadcasted_iota(jnp.int32, (2 * NZ, 6 * AZ), 1)
    ky = lax.broadcasted_iota(jnp.int32, (8, 2 * NY), 1) % NY

    def permuted(x, table):
        hi, lo = split(x)
        out = jnp.dot(jnp.concatenate([hi, lo], axis=0), table, preferred_element_type=F32)
        return out[: x.shape[0]] + out[x.shape[0] :]

    @pl.loop(first, last)
    def _(slot):
        rot = rots[slot]
        zaxis, flipped = turns[rot, 0], turns[rot, 1]
        step_x, step_y = turns[rot, 2], turns[rot, 3]
        off_y, off_z = offs[2 * slot], offs[2 * slot + 1]

        turn = (zstep_ref[0] - zstep_ref[1] * off_z + NZ * NZ) & (NZ - 1)
        t = jnp.cos(turn.astype(F32) * (2 * math.pi / NZ)) * zstep_ref[2].astype(F32)
        hi, lo = split(t)
        tzs[slot] = jnp.where((zlane >= 2 * AZ) & (zlane < 4 * AZ), lo.astype(F32), hi.astype(F32)).astype(BF)
        turn = ky * off_y
        ph[slot, 0] = jnp.cos((turn & (NY - 1)).astype(F32) * (2 * math.pi / NY))
        ph[slot, 1] = jnp.cos(((turn - NY // 4) & (NY - 1)).astype(F32) * (2 * math.pi / NY))

        for m in range(KS):
            w = lib_ref[ids[slot], :, m * KS * KS : (m + 1) * KS * KS]
            xa[m, :, : KS * KS] = jnp.where(core == 0, w, pltpu.roll(w, terms // 2, 0))
        x = xa[...]
        swapped = permuted(x.reshape(KS * terms, CUBE), swap_ref[...]).reshape(KS, terms, CUBE)
        xa[...] = jnp.where(zaxis == 2, swapped, x)
        for m in range(KS):
            acc = jnp.concatenate(
                [xa[n, :, m * KS : (m + 1) * KS] for n in range(KS)] + [jnp.zeros((terms, CUBE - KS * KS), F32)],
                axis=1,
            )
            xb[m] = jnp.where(zaxis == 0, xa[m], acc)

        here = lane_ref[0:1] * step_x + lane_ref[1:2] * step_y + (HALF - 1)
        there = 2 * (HALF - 1) - here + lane_ref[2:3]
        plus = (source == here).astype(F32)
        minus = jnp.where(source == there, lane_ref[3:4], 0).astype(F32)
        turned = permuted(xb[...].reshape(KS * terms, CUBE), (plus + minus).astype(BF))
        for m in range(KS):
            f = KS - 1 - m
            row = jnp.where(flipped == 1, turned[f * terms : (f + 1) * terms], turned[m * terms : (m + 1) * terms])
            for j in range(CUBE // 128):
                kd[j, pl.ds(m, terms, stride=AZ), :] = row[:, j * 128 : (j + 1) * 128]
        rows = pl.ds(pl.multiple_of(slot * terms * AZ, terms * AZ), terms * AZ)
        both = jnp.concatenate([kd[j] for j in range(CUBE // 128)], axis=1)
        hi, lo = split(both)
        hi, lo = hi.astype(F32), lo.astype(F32)
        spare = jnp.zeros((terms * AZ, PACK - 3 * HALF), F32)
        for ref, lanes in ((even, slice(0, HALF)), (odd, slice(HALF, 2 * HALF))):
            ref[rows, :] = jnp.concatenate([hi[:, lanes], lo[:, lanes], hi[:, lanes], spare], axis=1).astype(BF)


def probe_pair(p, te, to, even, odd, tzs, ph, q):
    slots, terms = q.shape[0], q.shape[1]
    columns = pl.ds(pl.multiple_of(p * 2 * NY, 2 * NY), 2 * NY)
    re_all = jnp.dot(even[...], te[:, columns], preferred_element_type=F32)
    im_all = jnp.dot(odd[...], to[:, columns], preferred_element_type=F32)
    for s in range(slots):
        c, n = ph[s, 0, 0:1], ph[s, 1, 0:1]
        rows = slice(s * terms * AZ, (s + 1) * terms * AZ)
        re = re_all[rows] * c + im_all[rows] * n
        im = im_all[rows] * c - re_all[rows] * n
        tz = tzs[s]
        for t in range(terms):
            d = jnp.concatenate([re[t * AZ : (t + 1) * AZ], im[t * AZ : (t + 1) * AZ]], axis=0)
            hi, lo = split(d)
            q[s, t, p] = jnp.dot(tz, jnp.concatenate([hi, hi, lo], axis=0), preferred_element_type=F32)


def cos24(m):
    return math.cos(2 * math.pi * (m % 24) / 24)


def sin24(m):
    return math.sin(2 * math.pi * (m % 24) / 24)


def lin(terms):
    total = None
    for coef, value in terms:
        if abs(coef) < 1e-12:
            continue
        if abs(coef - 1) < 1e-12:
            total = value if total is None else total + value
        elif abs(coef + 1) < 1e-12:
            total = -value if total is None else total - value
        else:
            total = coef * value if total is None else total + coef * value
    return total


def real_dft24(r):
    a = [r[0]] + [r[n] + r[24 - n] for n in range(1, 12)] + [r[12]]
    b = [None] + [r[n] - r[24 - n] for n in range(1, 12)]
    re, im = [None] * 13, [None] * 13
    c = [a[n] + a[12 - n] for n in range(6)] + [a[6]]
    d = [a[n] - a[12 - n] for n in range(6)]
    ce = [c[n] + c[6 - n] for n in range(3)] + [c[3]]
    co = [c[n] - c[6 - n] for n in range(3)]
    for m in range(7):
        if m % 2 == 0:
            re[2 * m] = lin([(cos24(2 * m * n), ce[n]) for n in range(4)])
        else:
            re[2 * m] = lin([(cos24(2 * m * n), co[n]) for n in range(3)])
    for k in range(1, 12, 2):
        re[k] = lin([(cos24(k * n), d[n]) for n in range(6)])
    e = [None] + [b[n] + b[12 - n] for n in range(1, 6)] + [b[6]]
    f = [None] + [b[n] - b[12 - n] for n in range(1, 6)]
    for k in range(1, 12, 2):
        im[k] = lin([(-sin24(k * n), e[n]) for n in range(1, 7)])
    fo = [None] + [f[n] + f[6 - n] for n in range(1, 3)] + [f[3]]
    fe = [None] + [f[n] - f[6 - n] for n in range(1, 3)]
    for m in range(1, 6):
        if m % 2 == 1:
            im[2 * m] = lin([(-sin24(2 * m * n), fo[n]) for n in range(1, 4)])
        else:
            im[2 * m] = lin([(-sin24(2 * m * n), fe[n]) for n in range(1, 3)])
    return re, im


def y_stage(x, w):
    hi, lo = split(x)
    return jnp.dot(jnp.concatenate([hi, lo, hi], axis=1), w, preferred_element_type=F32)


def z_stage(tz, x, direction):
    hi, lo = split(x)
    rhs = jnp.concatenate([hi, hi, lo], axis=0)
    p = jnp.dot(tz, rhs, preferred_element_type=F32)
    re = p[:NZ, :NY] - direction * p[NZ:, NY:]
    im = p[:NZ, NY:] + direction * p[NZ:, :NY]
    return re, im


def forward(i, own, before, after, wf_ref, tz, work, spec):
    @pl.loop(0, 8, unroll=True)
    def _(chunk):
        rows = pl.ds(pl.multiple_of(chunk * 8, 8), 8)
        r = (
            [before[i, n, rows] for n in range(8)]
            + [own[i, n, rows] for n in range(8)]
            + [after[i, n, rows] for n in range(8)]
        )
        re, im = real_dft24(r)
        for k in range(KX):
            work[k, rows, :NY] = re[k]
            work[k, rows, NY:] = im[k] if im[k] is not None else jnp.zeros_like(re[k])

    y = y_stage(work[...].reshape(KX * NZ, 2 * NY), wf_ref[...])
    work[...] = y.reshape(KX, NZ, 2 * NY)
    for k in range(KX):
        re, im = z_stage(tz, work[k], -1.0)
        spec[i, k, :, :NY] = re
        spec[i, k, :, NY:] = im


def contract(slot, group, q, spec, source, target):
    @pl.loop(0, 8, unroll=4)
    def _(chunk):
        start = pl.multiple_of(chunk * 8, 8)
        rows = pl.ds(start, 8)
        low = pl.ds(start + NZ, 8)
        for k in range(KX):
            p, lane = k // 2, (k % 2) * NY
            re = None if source is None else source[k, rows, :NY]
            im = None if source is None else source[k, rows, NY:]
            for t in group:
                gr, gi = spec[t, k, rows, :NY], spec[t, k, rows, NY:]
                qr = q[slot, t, p, rows, lane : lane + NY]
                qi = q[slot, t, p, low, lane : lane + NY]
                tr = gr * qr - gi * qi
                ti = gr * qi + gi * qr
                re = tr if re is None else re + tr
                im = ti if im is None else im + ti
            target[k, rows, :NY] = re
            target[k, rows, NY:] = im


def boltzmann(slot, wi_ref, tz, work, total_ref, sum_ref):
    for k in range(KX):
        re, im = z_stage(tz, work[k], 1.0)
        work[k, :, :NY] = re
        work[k, :, NY:] = im
    y = y_stage(work[...].reshape(KX * NZ, 2 * NY), wi_ref[...])
    work[...] = y.reshape(KX, NZ, 2 * NY)
    sum_ref[slot] = jnp.zeros((8, NY), F32)
    scale = 1.0 / (EXT * NZ * NY)

    @pl.loop(0, 8, unroll=2)
    def _(chunk):
        rows = pl.ds(pl.multiple_of(chunk * 8, 8), 8)
        fr = [work[k, rows, :NY] for k in range(KX)]
        fi = [work[k, rows, NY:] for k in range(KX)]
        acc = sum_ref[slot]
        for m in range(5):
            even, odd = [], []
            for k in range(KX):
                w = scale * (1.0 if k in (0, 12) else 2.0) * (-1) ** k
                even.append((w * cos24(k * m), fr[k]))
                odd.append((w * sin24(k * m), fi[k]))
            even, odd = sum_terms(even), sum_terms(odd)
            for x, e in ((4, even),) if m == 0 else ((4 + m, even - odd), (4 - m, even + odd)):
                if x < 8:
                    b = jnp.exp(-ENERGY_CAP * jnp.tanh(e / ENERGY_CAP))
                    total_ref[slot, x, rows] = b
                    acc = acc + b
        sum_ref[slot] = acc


def energy_kernel(
    slabs,
    probes,
    cells,
    ids,
    rots,
    offs,
    weights,
    turns,
    receptor,
    library,
    te_hbm,
    to_hbm,
    swap_ref,
    lane_ref,
    zstep_ref,
    tz_ref,
    wf_ref,
    wi_ref,
    out_ref,
    lib,
    te,
    to,
    own,
    before,
    after,
    xa,
    xb,
    kd,
    even,
    odd,
    tzs,
    ph,
    q,
    spec,
    work,
    joint,
    total,
    sums,
    mine,
    gathered,
    faces,
    mixed,
    blocks,
    send,
    recv,
    hand_send,
    hand_recv,
    near,
    part_send,
    part_recv,
    face_send,
    face_recv,
    block_send,
    block_recv,
):
    terms, planes = receptor.shape[0], receptor.shape[1]
    half = terms // 2
    slots = total.shape[0]
    rows = out_ref.shape[1]
    slab = lax.axis_index("slab")
    probe = lax.axis_index("probe")
    core = lax.rem(probe, 2)
    right = {"slab": lax.rem(slab + 1, slabs)}
    left = {"slab": lax.rem(slab + slabs - 1, slabs)}
    sibling = probe + 1 - 2 * core
    partner = lax.rem(probe + 2, probes)
    other = {"probe": sibling}

    barrier = pltpu.get_barrier_semaphore()

    @pl.loop(1, slabs)
    def _(d):
        pl.semaphore_signal(barrier, inc=1, device_id={"slab": lax.rem(slab + d, slabs)}, device_id_type=MESH)

    for device in (sibling, partner):
        pl.semaphore_signal(barrier, inc=1, device_id={"probe": device}, device_id_type=MESH)
    nearby = [
        pltpu.make_async_copy(library, lib, near.at[0]),
        pltpu.make_async_copy(te_hbm, te, near.at[1]),
        pltpu.make_async_copy(to_hbm, to, near.at[2]),
        pltpu.make_async_copy(receptor.at[pl.ds(core * half, half)], own.at[pl.ds(0, half)], near.at[3]),
        pltpu.make_async_copy(receptor.at[pl.ds((1 - core) * half, half)], own.at[pl.ds(half, half)], near.at[4]),
    ]

    def halo_copy(j, side):
        return pltpu.make_async_remote_copy(
            src_ref=receptor.at[core * half + j],
            dst_ref=(before, after)[side].at[j],
            send_sem=send.at[side, j],
            recv_sem=recv.at[side, j],
            device_id=(right, left)[side],
            device_id_type=MESH,
        )

    def hand_copy(j, side):
        ref = (before, after)[side]
        return pltpu.make_async_remote_copy(
            src_ref=ref.at[j],
            dst_ref=ref.at[half + j],
            send_sem=hand_send.at[side, j],
            recv_sem=hand_recv.at[side, j],
            device_id=other,
            device_id_type=MESH,
        )

    def hand_over(j):
        for side in range(2):
            halo_copy(j, side).wait_recv()
            hand_copy(j, side).start()

    for copy in nearby:
        copy.start()
    xa[...] = jnp.zeros_like(xa)
    kd[...] = jnp.zeros_like(kd)
    pl.semaphore_wait(barrier, slabs - 1 + 2)

    def send_off(j):
        for side in range(2):
            halo_copy(j, side).start()

    send_off(0)
    nearby[0].wait()
    early = slots - 1

    @pl.loop(0, 2)
    def _(part):
        turned_probes(
            part * early, early + part * (slots - early),
            ids, rots, offs, turns, core, lib, swap_ref, lane_ref, zstep_ref, xa, xb, kd, even, odd, tzs, ph,
        )

        @pl.when(part == 0)
        def _():
            send_off(1)

    for copy in nearby[1:]:
        copy.wait()
    hand_over(0)

    def pairs(low, high):
        @pl.loop(low, high)
        def _(p):
            probe_pair(p, te, to, even, odd, tzs, ph, q)

    tz = tz_ref[...]

    def products(group, first):
        @pl.loop(0, slots)
        def _(slot):
            contract(slot, group, q, spec, None if first else joint.at[slot], joint.at[slot])

    pairs(0, 3)
    send_off(2)
    pairs(3, 5)
    hand_over(1)
    pairs(5, PAIRS)
    send_off(3)

    @pl.loop(0, terms)
    def _(i):
        j, h = i // 2, i % 2

        @pl.when(h == 1)
        def _():
            for side in range(2):
                hand_copy(j, side).wait_recv()

        forward(j + half * h, own, before, after, wf_ref, tz, work, spec)

        @pl.when(i == 1)
        def _():
            hand_over(2)

        @pl.when(i == 3)
        def _():
            products((0, 1, half, half + 1), True)
            hand_over(3)

        @pl.when(i == 5)
        def _():
            products((2, half + 2), False)

    def face_copy(slot, side):
        return pltpu.make_async_remote_copy(
            src_ref=total.at[slot, (planes - 1, 0)[side]],
            dst_ref=faces.at[side, slot],
            send_sem=face_send.at[side, slot],
            recv_sem=face_recv.at[side, slot],
            device_id=(right, left)[side],
            device_id_type=MESH,
        )

    @pl.loop(0, slots)
    def _(slot):
        contract(slot, (3, half + 3), q, spec, joint.at[slot], work)
        boltzmann(slot, wi_ref, tz, work, total, sums)
        for side in range(2):
            face_copy(slot, side).start()

    parts = []
    for s in range(slots):
        v = jnp.sum(sums[s], axis=0, keepdims=True)
        parts.append(jnp.broadcast_to(jnp.sum(v, axis=1, keepdims=True), (1, NY)))
    parts += [jnp.zeros((1, NY), F32)] * (8 - slots)
    local_part = jnp.concatenate(parts, axis=0)
    mine[...] = local_part

    def part_copy(d):
        return pltpu.make_async_remote_copy(
            src_ref=mine,
            dst_ref=gathered.at[d],
            send_sem=part_send,
            recv_sem=part_recv,
            device_id={"slab": lax.rem(slab + d, slabs)},
            device_id_type=MESH,
        )

    @pl.loop(1, slabs)
    def _(d):
        part_copy(d).start()

    @pl.loop(0, slots)
    def _(slot):
        for side in range(2):
            face_copy(slot, side).wait_recv()

    others = gathered.at[pl.ds(1, slabs - 1)]
    pltpu.make_async_copy(others, others, part_recv).wait()

    partition = local_part
    for d in range(1, slabs):
        partition = partition + gathered[d]
    share = cells / partition
    coefs = [jnp.broadcast_to(share[s : s + 1] * weights[ids[s]], (8, NY)) for s in range(slots)]

    def weighted(read):
        result = None
        for s in range(slots):
            v = read(s).reshape(NZ // 8, 8, NY) * coefs[s][None]
            result = v if result is None else result + v
        return result.reshape(NZ, NY)

    mixed[0] = weighted(lambda s: faces[0, s])
    mixed[planes + 1] = weighted(lambda s: faces[1, s])
    for x in range(planes):
        mixed[x + 1] = weighted(lambda s: total[s, x])
    for x in range(planes):
        v = (mixed[x] + 2.0 * mixed[x + 1] + mixed[x + 2]) * 0.25
        v = (pltpu.roll(v, 1, 0) + 2.0 * v + pltpu.roll(v, NZ - 1, 0)) * 0.25
        v = (pltpu.roll(v, 1, 1) + 2.0 * v + pltpu.roll(v, NY - 1, 1)) * 0.25
        mixed[x] = v

    def block(p):
        return mixed.at[pl.ds(0, planes), pl.ds(pl.multiple_of(p * rows, 8), rows)]

    away = partner + sibling - probe
    crossing = [
        pltpu.make_async_remote_copy(
            src_ref=block(p),
            dst_ref=blocks.at[i],
            send_sem=block_send.at[i],
            recv_sem=block_recv.at[i],
            device_id={"probe": device},
            device_id_type=MESH,
        )
        for i, (p, device) in enumerate(((away, sibling), (sibling, sibling)))
    ]
    last = pltpu.make_async_remote_copy(
        src_ref=blocks.at[2],
        dst_ref=blocks.at[3],
        send_sem=block_send.at[2],
        recv_sem=block_recv.at[2],
        device_id={"probe": partner},
        device_id_type=MESH,
    )
    for copy in crossing:
        copy.start()
    crossing[0].wait_recv()
    blocks[2] = block(partner)[...] + blocks[0]
    last.start()
    crossing[1].wait_recv()
    result = block(probe)[...] + blocks[1]
    last.wait_recv()
    out_ref[...] = (result + blocks[3]) * (1.0 / weights.shape[0])

    @pl.loop(0, half)
    def _(j):
        for side in range(2):
            halo_copy(j, side).wait_send()
            hand_copy(j, side).wait_send()

    @pl.loop(0, slots)
    def _(slot):
        for side in range(2):
            face_copy(slot, side).wait_send()

    pltpu.make_async_copy(others, others, part_send).wait()

    for copy in (*crossing, last):
        copy.wait_send()


def sum_terms(terms):
    total = None
    for coef, value in terms:
        if abs(coef) < 1e-15:
            continue
        total = coef * value if total is None else total + coef * value
    return total


def local(receptor, library, probe_ids, rotations, offsets, probe_weight):
    terms, planes, nz, ny = receptor.shape
    slabs = lax.axis_size("slab")
    probes = lax.axis_size("probe")
    slots, half = probe_ids.shape[0], terms // 2
    rows = nz // probes
    cells = float(planes * slabs * nz * ny)
    te, to = xy_tables()
    smem = pl.BlockSpec(memory_space=pltpu.SMEM)
    vmem = pl.BlockSpec(memory_space=pltpu.VMEM)
    hbm = pl.BlockSpec(memory_space=pl.ANY)
    dma = pltpu.SemaphoreType.DMA
    return pl.pallas_call(
        functools.partial(energy_kernel, slabs, probes, cells),
        in_specs=[smem] * 5 + [hbm] * 4 + [vmem] * 6,
        out_specs=vmem,
        out_shape=jax.ShapeDtypeStruct((planes, rows, ny), F32),
        scratch_shapes=[
            pltpu.VMEM(library.shape, F32),
            pltpu.VMEM(te.shape, BF),
            pltpu.VMEM(to.shape, BF),
            pltpu.VMEM(receptor.shape, F32),
            pltpu.VMEM(receptor.shape, F32),
            pltpu.VMEM(receptor.shape, F32),
            pltpu.VMEM((KS, terms, CUBE), F32),
            pltpu.VMEM((KS, terms, CUBE), F32),
            pltpu.VMEM((CUBE // 128, terms * AZ, 128), F32),
            pltpu.VMEM((slots * terms * AZ, PACK), BF),
            pltpu.VMEM((slots * terms * AZ, PACK), BF),
            pltpu.VMEM((slots, 2 * NZ, 6 * AZ), BF),
            pltpu.VMEM((slots, 2, 8, 2 * NY), F32),
            pltpu.VMEM((slots, terms, PAIRS, 2 * NZ, 2 * NY), F32),
            pltpu.VMEM((terms, KX, nz, 2 * ny), F32),
            pltpu.VMEM((KX, nz, 2 * ny), F32),
            pltpu.VMEM((slots, KX, nz, 2 * ny), F32),
            pltpu.VMEM((slots, planes, nz, ny), F32),
            pltpu.VMEM((slots, 8, ny), F32),
            pltpu.VMEM((8, ny), F32),
            pltpu.VMEM((slabs, 8, ny), F32),
            pltpu.VMEM((2, slots, nz, ny), F32),
            pltpu.VMEM((planes + 2, nz, ny), F32),
            pltpu.VMEM((4, planes, rows, ny), F32),
            dma((2, half)),
            dma((2, half)),
            dma((2, half)),
            dma((2, half)),
            dma((5,)),
            pltpu.SemaphoreType.DMA,
            pltpu.SemaphoreType.DMA,
            dma((2, slots)),
            dma((2, slots)),
            dma((3,)),
            dma((3,)),
        ],
        compiler_params=pltpu.CompilerParams(
            collective_id=0, has_side_effects=True, vmem_limit_bytes=63 << 20
        ),
        name="consensus_density",
    )(
        probe_ids,
        rotations.reshape(-1),
        offsets.reshape(-1),
        probe_weight,
        jnp.asarray(rotation_table()),
        receptor,
        library,
        jnp.asarray(te),
        jnp.asarray(to),
        jnp.asarray(swap_table()),
        jnp.asarray(lane_offsets()),
        jnp.asarray(probe_z_steps()),
        jnp.asarray(grid_z_table()),
        jnp.asarray(grid_y_table(-1.0)),
        jnp.asarray(grid_y_table(1.0)),
    )


def solution(mesh):
    in_specs = (
        P(None, "slab", None, None),
        P(),
        P("probe"),
        P("probe", None),
        P("probe", None, None),
        P(),
    )
    out_specs = P("slab", "probe", None)
    return jax.shard_map(local, mesh=mesh, in_specs=in_specs, out_specs=out_specs, check_vma=False)
```
